128 devices in a mesh: gx: 4 (over z), gy: 32 (over x, y, core).
Axes of the slice: x: 4, y: 4, z: 4, core: 2. Of those that a mesh axis runs over, the one named last changes fastest.
Arguments:
- fine_rhs: float32 [16384, 512], P(('gx', 'gy')), may hold values from -6 to 6
- fine_guess: float32 [16384, 512], P(('gx', 'gy')), may hold values from -3 to 3
- fine_coef: float32 [16384, 512], P(('gx', 'gy')), may hold values from 0.2 to 5
- fine_links: int32 [16384, 6], P(('gx', 'gy')), may hold values from -1 to 16383, as said below
- parent_owner: int32 [16384, 1], P(('gx', 'gy')), may hold values from 0 to 127, as said below
- coarse_coef: float32 [4096, 512], P(('gx', 'gy')), may hold values from 0.2 to 5
- coarse_links: int32 [4096, 6], P(('gx', 'gy')), may hold values from -1 to 4095, as said below
Outputs:
- fine_solution: float32 [16384, 512], P(('gx', 'gy'))
- coarse_correction: float32 [4096, 512], P(('gx', 'gy'))
The draws below stay inside these ranges and needn't reach their ends.
Inputs may be any that keep to these rules, and one draw needn't show every extreme that they name: fine_links[b, 2k + 1] names the fine brick across brick b's upper face along dimension k and fine_links[b, 2k] the one across its lower face, -1 at the domain's boundary. The relation is symmetric: if fine_links[b, f] = c then fine_links[c, f xor 1] = b. The brick across an upper face lies on the same device or the next one in gx+gy order, the brick across a lower face on the same device or the previous one. `coarse_links`: as for fine_links, over the 4096 coarse brick slots with 32 slots a device. `parent_owner`: the parent of a fine brick on device d lies on device d - 1, d or d + 1 in gx+gy order; along a device's bricks the owners never fall. At most 64 fine bricks of one device have their parent on the previous device and at most 64 on the next; some device has exactly 64 on the next.
All inputs are finite; a program needn't handle non-finite values.
Results may differ from the reference program's by a relative error of at most 0.0003.
Values sent between devices are 32-bit elements; how exact they have to be, the bound alone decides.
A program may use at most 64 MiB of HBM per device.

```python
import math
import jax
import jax.numpy as jnp
import numpy as np
from jax import lax

B = 8
BF = 128
SWEEPS = 3
CAP = 64
BC = 32
NF = 16384
NC = 4096
N_GX = 4
N_GY = 32


def build_links(key, slots, total):
    devices_all = total // slots
    key_shift, key_perm, key_keep = jax.random.split(key, 3)
    offsets = jax.random.randint(key_shift, (3,), 1, slots).astype(jnp.int32)
    keep_pair = jax.random.randint(key_keep, (3, total), 0, 8) != 0
    perm_keys = jax.random.split(key_perm, 3 * devices_all)
    tables = jax.vmap(lambda one_key: jax.random.permutation(one_key, slots))(perm_keys)
    tables = tables.astype(jnp.int32).reshape(3, devices_all, slots)
    inverse = jnp.argsort(tables, axis=-1).astype(jnp.int32)
    bricks = jnp.arange(total, dtype=jnp.int32)
    columns = []
    for dimension in range(3):
        target = bricks + offsets[dimension]
        target_dev = jnp.minimum(target // slots, devices_all - 1)
        target_pos = target % slots
        upper_ok = (target < total) & keep_pair[dimension]
        upper = jnp.where(upper_ok, target_dev * slots + tables[dimension, target_dev, target_pos], -1)
        home_dev = bricks // slots
        home_pos = bricks % slots
        source = home_dev * slots + inverse[dimension, home_dev, home_pos] - offsets[dimension]
        lower_ok = (source >= 0) & keep_pair[dimension, jnp.maximum(source, 0)]
        lower = jnp.where(lower_ok, source, -1)
        columns.append(lower)
        columns.append(upper)
    return jnp.stack(columns, axis=1).astype(jnp.int32)


def draw_fine_links(key, part):
    key = jax.random.fold_in(key, 11)
    return build_links(key, BF, NF)


def draw_coarse_links(key, part):
    key = jax.random.fold_in(key, 23)
    return build_links(key, BC, NC)


def draw_parent_owner(key, part):
    key = jax.random.fold_in(key, 37)
    devices_all = NF // BF
    key_low, key_high, key_pick = jax.random.split(key, 3)
    lower_cut = jax.random.randint(key_low, (devices_all,), 0, CAP + 1).astype(jnp.int32)
    upper_cut = jax.random.randint(key_high, (devices_all,), 0, CAP + 1).astype(jnp.int32)
    picked_dev = jax.random.randint(key_pick, (), 0, devices_all - 1).astype(jnp.int32)
    device_ids = jnp.arange(devices_all, dtype=jnp.int32)
    upper_cut = jnp.where(device_ids == picked_dev, CAP, upper_cut)
    lower_cut = jnp.where(device_ids == 0, 0, lower_cut)
    upper_cut = jnp.where(device_ids == devices_all - 1, 0, upper_cut)
    positions = jnp.arange(BF, dtype=jnp.int32)
    to_prev = (positions[None, :] < lower_cut[:, None]).astype(jnp.int32)
    to_next = (positions[None, :] >= BF - upper_cut[:, None]).astype(jnp.int32)
    owners = device_ids[:, None] - to_prev + to_next
    return owners.reshape(NF, 1).astype(jnp.int32)


def shard_levels(stream_key, shape, pieces, low, high):
    def one(dim, blocks):
        steps = jax.random.uniform(jax.random.fold_in(jax.random.fold_in(stream_key, 6), dim), (blocks,), jnp.float32, low / len(pieces), high / len(pieces))
        return jnp.repeat(jnp.exp(steps), shape[dim] // blocks).reshape((-1,) + (1,) * (len(shape) - dim - 1))

    level = one(*pieces[0])
    for cut in pieces[1:]:
        level = level * one(*cut)
    return level


def centred(rng, extent, deviation, limit, cuts=(), kind=jnp.bfloat16):
    values = deviation * jax.random.normal(rng, extent, jnp.float32)
    if cuts:
        values = values * shard_levels(rng, extent, cuts, -0.22, 0.18)
    return jnp.clip(values, -limit, limit).astype(kind)


def setup_inputs(seed: int = 0) -> dict:
    keys = jax.random.split(jax.random.key(seed), 8)
    fine_rhs = centred(keys[0], (NF, B**3), 1.0, 6.0, ((0, 128),), jnp.float32)
    fine_guess = centred(keys[1], (NF, B**3), 0.5, 3.0, ((0, 128),), jnp.float32)
    fine_coef = jnp.clip(jnp.exp(math.log(5.0) - 3.218876 * jax.random.uniform(keys[2], (NF, B**3), jnp.float32) ** shard_levels(keys[2], (NF, B**3), ((0, 128),), -0.2, 0.2)), 0.2, 5.0)
    fine_links = draw_fine_links(jax.random.fold_in(keys[7], 71), 0)
    parent_owner = draw_parent_owner(jax.random.fold_in(keys[7], 71), 0)
    coarse_coef = jnp.clip(jnp.exp(math.log(5.0) - 3.218876 * jax.random.uniform(keys[5], (NC, B**3), jnp.float32) ** shard_levels(keys[5], (NC, B**3), ((0, 128),), -0.2, 0.2)), 0.2, 5.0)
    coarse_links = draw_coarse_links(jax.random.fold_in(keys[7], 71), 0)
    return {"fine_rhs": fine_rhs, "fine_guess": fine_guess, "fine_coef": fine_coef, "fine_links": fine_links, "parent_owner": parent_owner, "coarse_coef": coarse_coef, "coarse_links": coarse_links}


THETA = 1.25
DELTA = 0.75
SIGMA = THETA / DELTA
OPPOSITE = np.array([1, 0, 3, 2, 5, 4], dtype=np.int32)


def face_stack(volume):
    edge_len = volume.shape[1]
    face_list = []
    for dimension in range(3):
        face_list.append(lax.index_in_dim(volume, 0, 1 + dimension, keepdims=False))
        face_list.append(lax.index_in_dim(volume, edge_len - 1, 1 + dimension, keepdims=False))
    return jnp.stack(face_list, axis=1)


def neighbor_values(volume, ghosts):
    edge_len = volume.shape[1]
    result = []
    for dimension in range(3):
        axis_at = 1 + dimension
        lower = jnp.expand_dims(ghosts[:, 2 * dimension], axis_at)
        upper = jnp.expand_dims(ghosts[:, 2 * dimension + 1], axis_at)
        result.append(jnp.concatenate([lower, lax.slice_in_dim(volume, 0, edge_len - 1, axis=axis_at)], axis=axis_at))
        result.append(jnp.concatenate([lax.slice_in_dim(volume, 1, edge_len, axis=axis_at), upper], axis=axis_at))
    return result


def face_weights(coef_volume, coef_ghosts):
    weights = [0.5 * (coef_volume + other) for other in neighbor_values(coef_volume, coef_ghosts)]
    diagonal = weights[0]
    for weight in weights[1:]:
        diagonal = diagonal + weight
    return weights, diagonal


def operate(volume, weights, ghost_fn):
    result = jnp.zeros_like(volume)
    for weight, other in zip(weights, neighbor_values(volume, ghost_fn(volume, False))):
        result = result + weight * (volume - other)
    return result


def smooth(start, source, weights, diagonal, ghost_fn, from_zero):
    solution = start
    rho_now = 1.0 / SIGMA
    update = None
    for sweep_at in range(SWEEPS):
        if sweep_at == 0 and from_zero:
            residual = source
        else:
            residual = source - operate(solution, weights, ghost_fn)
        scaled = residual / diagonal
        if sweep_at == 0:
            update = scaled / THETA
        else:
            rho_next = 1.0 / (2.0 * SIGMA - rho_now)
            update = rho_next * rho_now * update + (2.0 * rho_next / DELTA) * scaled
            rho_now = rho_next
        solution = solution + update
    return solution


def to_octants(volume):
    count = volume.shape[0]
    half = volume.shape[1] // 2
    shaped = volume.reshape(count, 2, half, 2, half, 2, half).transpose(0, 1, 3, 5, 2, 4, 6)
    return shaped.reshape(count, 8, half * half * half)


def from_octants(octants, edge_len):
    count = octants.shape[0]
    half = edge_len // 2
    shaped = octants.reshape(count, 2, 2, 2, half, half, half).transpose(0, 1, 4, 2, 5, 3, 6)
    return shaped.reshape(count, edge_len, edge_len, edge_len)


def restrict(residual):
    count = residual.shape[0]
    half = residual.shape[1] // 2
    summed = residual.reshape(count, half, 2, half, 2, half, 2).sum(axis=(2, 4, 6)) * 0.5
    return summed.reshape(count, half * half * half)


def prolong(values, edge_len):
    count = values.shape[0]
    half = edge_len // 2
    shaped = values.reshape(count, half, 1, half, 1, half, 1)
    shaped = jnp.broadcast_to(shaped, (count, half, 2, half, 2, half, 2))
    return shaped.reshape(count, edge_len, edge_len, edge_len)


def ghosts_global(volume, link_ids, keep_own):
    face_set = face_stack(volume)
    safe_ids = jnp.maximum(link_ids, 0)
    picked = face_set[safe_ids, OPPOSITE[None, :]]
    is_live = (link_ids >= 0)[:, :, None, None]
    if keep_own:
        return jnp.where(is_live, picked, face_set)
    return jnp.where(is_live, picked, jnp.zeros_like(picked))


def reference(fine_rhs, fine_guess, fine_coef, fine_links, parent_owner, coarse_coef, coarse_links):
    def fine_ghosts(volume, keep_own):
        return ghosts_global(volume, fine_links, keep_own)

    def coarse_ghosts(volume, keep_own):
        return ghosts_global(volume, coarse_links, keep_own)

    devices_all = N_GX * N_GY
    half = B // 2
    fine_shape = (NF, B, B, B)
    coarse_shape = (NC, B, B, B)
    source = fine_rhs.reshape(fine_shape)
    coef_volume = fine_coef.reshape(fine_shape)
    weights, diagonal = face_weights(coef_volume, fine_ghosts(coef_volume, True))
    smoothed = smooth(fine_guess.reshape(fine_shape), source, weights, diagonal, fine_ghosts, False)
    residual = source - operate(smoothed, weights, fine_ghosts)
    restricted = restrict(residual)
    owner_dev = parent_owner[:, 0]
    one_hot = (owner_dev[:, None] == jnp.arange(devices_all, dtype=jnp.int32)[None, :]).astype(jnp.int32)
    earlier = jnp.cumsum(one_hot, axis=0, dtype=jnp.int32) - one_hot
    local_rank = jnp.sum(earlier * one_hot, axis=1, dtype=jnp.int32)
    coarse_slot = owner_dev * BC + local_rank // 8
    octant = local_rank % 8
    octant_data = jnp.zeros((NC, 8, half * half * half), jnp.float32).at[coarse_slot, octant].set(restricted)
    coarse_source = from_octants(octant_data, B)
    coarse_volume = coarse_coef.reshape(coarse_shape)
    coarse_weights, coarse_diagonal = face_weights(coarse_volume, coarse_ghosts(coarse_volume, True))
    correction = smooth(jnp.zeros(coarse_shape, jnp.float32), coarse_source, coarse_weights, coarse_diagonal, coarse_ghosts, True)
    back_values = to_octants(correction)[coarse_slot, octant]
    corrected = smoothed + prolong(back_values, B)
    fine_solution = smooth(corrected, source, weights, diagonal, fine_ghosts, False)
    return fine_solution.reshape(NF, B * B * B), correction.reshape(NC, B * B * B)
```

```python
import functools

import jax
import jax.numpy as jnp
from jax import lax
from jax.experimental import pallas as pl
from jax.experimental.pallas import tpu as pltpu
from jax.sharding import PartitionSpec as P

THETA = 1.25
DELTA = 0.75
SIGMA = THETA / DELTA
RHO0 = 1.0 / SIGMA
RHO1 = 1.0 / (2.0 * SIGMA - RHO0)
RHO2 = 1.0 / (2.0 * SIGMA - RHO1)
SWEEPS = ((0.0, 1.0 / THETA), (RHO1 * RHO0, 2.0 * RHO1 / DELTA), (RHO2 * RHO1, 2.0 * RHO2 / DELTA))

LANES = 128
FINE = 128
COARSE = 32
MESH = pl.DeviceIdType.MESH
N_COPIES = 64


def pick(values, index):
    rows = values.shape[0]
    whole = jnp.broadcast_to(index[None], (rows // 8, 8, LANES)).reshape(rows, LANES)
    return jnp.take_along_axis(values, whole, axis=1, mode="promise_in_bounds")


def pick_face(face, index):
    return pick(face.reshape(64, LANES), index).reshape(8, 8, LANES)


def kernel(
    gx, gy,
    rhs_ref, guess_ref, coef_ref, links_ref, owner_ref, ccoef_ref, clinks_ref,
    out_ref, cout_ref,
    xb, wt, bd, dg, upd, ghost, packed, recv, fidx, fmask,
    ccrow, cxb, cwt, cidg, cbd, cupd, cghost, idrow, tidx, tsrc, cidx, crec, cpack, cnidx,
    counts, src, pair2, pair2r, tall, back, backr, expand,
    ssem, rsem,
):
    devices = gx * gy
    me = lax.axis_index("gx") * gy + lax.axis_index("gy")
    valid = {1: me < devices - 1, -1: me > 0, 2: me < devices - 2, -2: me > 1}

    def device(offset):
        target = lax.rem(me + offset + devices, devices)
        return (target // gy, lax.rem(target, gy))

    barrier = pltpu.get_barrier_semaphore()
    for offset in (1, -1, 2, -2):
        @pl.when(valid[offset])
        def _():
            pl.semaphore_signal(barrier, inc=1, device_id=device(offset), device_id_type=MESH)

    used = [0]
    sent = []

    def send(offset, pairs):
        made = []
        for source, target in pairs:
            at = used[0]
            used[0] += 1
            made.append(pltpu.make_async_remote_copy(
                src_ref=source, dst_ref=target, send_sem=ssem.at[at], recv_sem=rsem.at[at],
                device_id=device(offset), device_id_type=MESH))

        @pl.when(valid[offset])
        def _():
            for copy in made:
                copy.start()

        sent.append((offset, made))
        return (offset, made)

    def arrived(handle, which=None):
        offset, made = handle

        @pl.when(valid[-offset])
        def _():
            for copy in (made if which is None else [made[which]]):
                copy.wait_recv()

    lane = lax.broadcasted_iota(jnp.int32, (8, LANES), 1)
    row = lax.broadcasted_iota(jnp.int32, (8, LANES), 0)
    row3 = lax.broadcasted_iota(jnp.int32, (8, 8, LANES), 1)
    first, last = row3 == 0, row3 == 7

    def load_cells(buffer, rows_ref):
        for c in range(4):
            block = rows_ref[:, c * LANES:(c + 1) * LANES].T
            buffer[2 * c + 1:2 * c + 3, 1:9] = block.reshape(2, 8, 8, LANES)

    def face(x, f):
        at = 1 if f % 2 == 0 else 8
        if f // 2 == 0:
            return x[at, 1:9]
        if f // 2 == 1:
            return x[1:9, at]
        return x[1:9, 1:9, 0 if f % 2 == 0 else 7]

    def put_ghost(x, g, f, value):
        at = 0 if f % 2 == 0 else 9
        if f // 2 == 0:
            x[at, 1:9] = value
        elif f // 2 == 1:
            x[1:9, at] = value
        else:
            g[f % 2] = value

    def get_ghost(x, g, f):
        at = 0 if f % 2 == 0 else 9
        if f // 2 == 0:
            return x[at, 1:9]
        if f // 2 == 1:
            return x[1:9, at]
        return g[f % 2]

    def neighbours(x, g, i):
        centre = x[i + 1, 1:9]
        low = jnp.where(first, g[0, i][:, None, :], pltpu.roll(centre, 1, 1))
        high = jnp.where(last, g[1, i][:, None, :], pltpu.roll(centre, 7, 1))
        return centre, (x[i, 1:9], x[i + 2, 1:9], x[i + 1, 0:8], x[i + 1, 2:10], low, high)

    def scaled_residual(x, g, w, b, i):
        centre, others = neighbours(x, g, i)
        total = b[i] - centre
        for f in range(6):
            total = total + w[f, i] * others[f]
        return centre, total

    def sweep(x, g, w, b, d, new, at):
        keep, gain = SWEEPS[at]

        def step(i, carry):
            centre, total = scaled_residual(x, g, w, b, i)
            update = gain * total
            if at > 0:
                update = update + keep * d[i]
            d[i] = update
            new[i + 1, 1:9] = centre + update
            return carry

        lax.fori_loop(0, 8, step, 0)

    def start_faces(e, x):
        packed[e, 0] = face(x, 4)
        packed[e, 1] = face(x, 5)
        up = send(1, [(x.at[8, 1:9], recv.at[e, 0, 0]), (x.at[1:9, 8], recv.at[e, 0, 1]), (packed.at[e, 1], recv.at[e, 0, 2])])
        down = send(-1, [(x.at[1, 1:9], recv.at[e, 1, 0]), (x.at[1:9, 1], recv.at[e, 1, 1]), (packed.at[e, 0], recv.at[e, 1, 2])])
        return up, down

    def own_ghosts(x, keep_own):
        for f in range(6):
            value = pick_face(face(x, f ^ 1), fidx[f])
            if keep_own:
                value = jnp.where(fmask[6 + f][None] != 0, value, face(x, f))
            put_ghost(x, ghost, f, value)

    def far_ghosts(e, x, handles):
        for k in range(3):
            for side in range(2):
                f = 2 * k + side
                arrived(handles[side], k)
                value = pick_face(recv[e, side, k], fidx[f])
                put_ghost(x, ghost, f, jnp.where(fmask[f][None] != 0, value, get_ghost(x, ghost, f)))

    def exchange(e, x, between=None):
        handles = start_faces(e, x)
        own_ghosts(x, False)
        if between is not None:
            between()
        far_ghosts(e, x, handles)

    coef, x0 = xb.at[0], xb.at[1]
    load_cells(coef, coef_ref)
    load_cells(x0, guess_ref)

    owner = owner_ref[...]
    to_prev = jnp.sum((owner == me - 1).astype(jnp.float32), axis=0, keepdims=True).astype(jnp.int32)
    to_next = jnp.sum((owner == me + 1).astype(jnp.float32), axis=0, keepdims=True).astype(jnp.int32)
    counts[2, 0] = jnp.broadcast_to(to_prev, (8, LANES))
    counts[2, 1] = jnp.broadcast_to(to_next, (8, LANES))
    ccrow[COARSE:2 * COARSE] = ccoef_ref[...]
    ccrow[3 * COARSE:] = jnp.ones((COARSE, 512), jnp.float32)

    pl.semaphore_wait(barrier, jnp.minimum(me, 2) + jnp.minimum(devices - 1 - me, 2))

    coef_handles = start_faces(0, coef)
    x0_handles = start_faces(1, x0)
    count_handles = [send(o, [(counts.at[2], counts.at[2 - o])]) for o in (1, -1, 2, -2)]
    ccoef_handles = [send(1, [(ccrow.at[COARSE:2 * COARSE], ccrow.at[0:COARSE])]),
                     send(-1, [(ccrow.at[COARSE:2 * COARSE], ccrow.at[2 * COARSE:3 * COARSE])])]

    links = links_ref[...].T
    for f in range(6):
        ids = jnp.broadcast_to(links[f:f + 1], (8, LANES))
        live = ids >= 0
        fidx[f] = jnp.bitwise_and(ids, FINE - 1)
        fmask[f] = jnp.where(live & (jnp.right_shift(ids, 7) != me), 1, 0)
        fmask[6 + f] = jnp.where(live, 1, 0)

    for c in range(4):
        dg[2 * c:2 * c + 2] = rhs_ref[:, c * LANES:(c + 1) * LANES].T.reshape(2, 8, 8, LANES)
    own_ghosts(coef, True)
    far_ghosts(0, coef, coef_handles)

    def weigh(x, g, w, lives, finish):
        mask4 = jnp.where((row == 0) & (lives[4] == 0), 0.0, 1.0)[None]
        mask5 = jnp.where((row == 7) & (lives[5] == 0), 0.0, 1.0)[None]

        def step(i, carry):
            centre, others = neighbours(x, g, i)
            weights = [0.5 * (centre + other) for other in others]
            diag = weights[0]
            for weight in weights[1:]:
                diag = diag + weight
            inverse = 1.0 / diag
            for f in range(6):
                value = weights[f] * inverse
                if f == 4:
                    value = value * mask4
                if f == 5:
                    value = value * mask5
                w[f, i] = value
            finish(i, diag, inverse)
            return carry

        lax.fori_loop(0, 8, step, 0)
        w[0, 0] = jnp.where(lives[0][None] != 0, w[0, 0], 0.0)
        w[1, 7] = jnp.where(lives[1][None] != 0, w[1, 7], 0.0)
        w[2, :, 0] = jnp.where(lives[2][None] != 0, w[2, :, 0], 0.0)
        w[3, :, 7] = jnp.where(lives[3][None] != 0, w[3, :, 7], 0.0)

    def fine_finish(i, diag, inverse):
        bd[i] = dg[i] * inverse
        dg[i] = diag

    weigh(coef, ghost, wt, [fmask[6 + f] for f in range(6)], fine_finish)

    own_ghosts(x0, False)
    far_ghosts(1, x0, x0_handles)
    sweep(x0, ghost, wt, bd, upd, xb.at[2], 0)

    own_lane = (jnp.right_shift(lane, 5) == 1)
    group = jnp.right_shift(lane, 5)
    slot = jnp.bitwise_and(lane, COARSE - 1)
    coarse_handles = []

    def coarse_setup_a():
        for handle in ccoef_handles + count_handles:
            arrived(handle)
        load_cells(cxb.at[0], ccrow)
        zeros = jnp.zeros((COARSE, 6), jnp.int32)
        links_c = jnp.concatenate([zeros, clinks_ref[...], zeros, zeros], axis=0).T
        lives = []
        x = cxb.at[0]
        for f in range(6):
            ids = jnp.broadcast_to(links_c[f:f + 1], (8, LANES))
            live = ids >= 0
            step_by = jnp.right_shift(ids, 5) - me
            place = jnp.bitwise_and((step_by + 1) * COARSE + jnp.bitwise_and(ids, COARSE - 1), LANES - 1)
            place = jnp.where(own_lane & live, place, lane)
            cidx[f] = place
            cnidx[f] = jnp.bitwise_and(ids, COARSE - 1) + (f // 2) * COARSE
            cnidx[6 + f] = jnp.where(own_lane & live & (step_by != 0), 1, 0)
            lives.append(jnp.where(live, 1, 0))
            value = jnp.where(live[None], pick_face(face(x, f ^ 1), place), face(x, f))
            put_ghost(x, cghost, f, value)

        def finish(i, diag, inverse):
            cidg[i] = inverse

        weigh(x, cghost, cwt, lives, finish)
        for c in range(4):
            block = cidg[2 * c:2 * c + 2].reshape(LANES, LANES).T
            idrow[COARSE:2 * COARSE, c * LANES:(c + 1) * LANES] = block[COARSE:2 * COARSE]
        coarse_handles.append(send(1, [(idrow.at[COARSE:2 * COARSE], idrow.at[0:COARSE])]))
        coarse_handles.append(send(-1, [(idrow.at[COARSE:2 * COARSE], idrow.at[2 * COARSE:3 * COARSE])]))

    def known(k, which):
        return counts[k, which] if k == 2 else jnp.where(valid[k - 2], counts[k, which], 0)

    def by_group(values):
        return jnp.where(group == 0, values[0], jnp.where(group == 1, values[1], values[2]))

    def coarse_setup_b():
        a = [known(k, 0) for k in range(5)]
        n = [known(k, 1) for k in range(5)]
        stay = [FINE - a[k] - n[k] if k == 2 else jnp.where(valid[k - 2], FINE - a[k] - n[k], 0) for k in range(5)]
        before, here = by_group(n[0:3]), by_group(stay[1:4])
        start, after = by_group(a[1:4]), by_group(a[2:5])
        for o in range(4):
            rank = 8 * slot + 2 * o + jnp.where(row >= 4, 1, 0)
            in_before = rank < before
            in_here = rank < before + here
            in_after = rank < before + here + after
            at = jnp.where(in_before, FINE - before + rank, jnp.where(in_here, start + rank - before, rank - before - here))
            step_by = jnp.where(in_before, group - 2, jnp.where(in_here, group - 1, group))
            source = jnp.where((step_by == 2) | (step_by == -2), 0, step_by + 2)
            tidx[o] = jnp.bitwise_and(at, LANES - 1)
            tsrc[o] = jnp.where(in_after & (group < 3), source, 4)
        rank_own = n[1] + lane - a[2]
        rank_far = jnp.where(lane < 64, n[1] + stay[2] + lane, lane - FINE + n[1])
        for k, rank in enumerate((rank_own, rank_far)):
            rank = jnp.bitwise_and(rank, 255)
            tidx[4 + 2 * k] = COARSE + jnp.right_shift(rank, 3)
            tidx[5 + 2 * k] = jnp.bitwise_and(rank, 7)

    def coarse_setup_c():
        for handle in coarse_handles:
            arrived(handle)
        for c in range(4):
            block = idrow[:, c * LANES:(c + 1) * LANES].T
            cidg[2 * c:2 * c + 2] = block.reshape(2, 8, 8, LANES)

    exchange(2, xb.at[2], coarse_setup_a)
    sweep(xb.at[2], ghost, wt, bd, upd, xb.at[3], 1)
    exchange(3, xb.at[3], coarse_setup_b)
    sweep(xb.at[3], ghost, wt, bd, upd, xb.at[4], 2)
    exchange(4, xb.at[4], coarse_setup_c)

    x3 = xb.at[4]

    def restrict_step(i, carry):
        total = jnp.zeros((4, 8, LANES), jnp.float32)
        for half in range(2):
            _, scaled = scaled_residual(x3, ghost, wt, bd, 2 * i + half)
            quads = (scaled * dg[2 * i + half]).reshape(4, 2, 8, LANES)
            total = total + quads[:, 0] + quads[:, 1]
        total = total + pltpu.roll(total, 7, 1)
        tall[pl.ds(pl.multiple_of(i * 32, 32), 32)] = 0.5 * total.reshape(32, LANES)
        return carry

    lax.fori_loop(0, 4, restrict_step, 0)
    restricted = tall[pl.ds(0, 64, stride=2)]
    src[2] = restricted
    low_lane = jnp.broadcast_to((lane < 64)[None], (4, 8, LANES)).reshape(32, LANES)
    turned = pltpu.roll(restricted[32:], 64, 1)
    pair2[0] = jnp.where(low_lane, turned, restricted[:32])
    pair2[1] = jnp.where(low_lane, restricted[:32], turned)
    r_handles = [send(1, [(src.at[2], src.at[1])]), send(-1, [(src.at[2], src.at[3])]),
                 send(2, [(pair2.at[0], pair2r.at[0])]), send(-2, [(pair2.at[1], pair2r.at[1])])]
    for handle in r_handles:
        arrived(handle)
    src[0, 0:32] = jnp.where(low_lane, pair2r[1], pair2r[0])
    src[0, 32:64] = pltpu.roll(jnp.where(low_lane, pair2r[0], pair2r[1]), 64, 1)

    for o in range(4):
        ox, oy = o // 2, o % 2
        index, which = tidx[o], tsrc[o]
        for i in range(4):
            for j in range(4):
                q = 4 * (4 * i + j)
                value = jnp.zeros((8, LANES), jnp.float32)
                for k in range(4):
                    four = src[k, q:q + 4]
                    taken = pick(jnp.concatenate([four, four], axis=0), index)
                    value = jnp.where(which == k, taken, value)
                at = (4 * ox + i, 4 * oy + j)
                scaled = value * cidg[at[0], at[1]]
                cbd[at[0], at[1]] = scaled
                update = scaled * (1.0 / THETA)
                cupd[at[0], at[1]] = update
                cxb[1, at[0] + 1, at[1] + 1] = update

    c1, c2, c3 = cxb.at[1], cxb.at[2], cxb.at[3]
    for f in range(6):
        put_ghost(c1, cghost, f, pick_face(face(c1, f ^ 1), cidx[f]))
    sweep(c1, cghost, cwt, cbd, cupd, c2, 1)

    lane64 = jnp.broadcast_to(lane[None], (8, 8, LANES)).reshape(64, LANES)
    for side in range(2):
        faces = [face(c2, 2 * k + side).reshape(64, LANES) for k in range(3)]
        cpack[side] = jnp.where(lane64 < 32, pltpu.roll(faces[0], 96, 1), jnp.where(lane64 < 64, faces[1], pltpu.roll(faces[2], 32, 1)))
    c_handles = [send(1, [(cpack.at[1], crec.at[0])]), send(-1, [(cpack.at[0], crec.at[1])])]
    for f in range(6):
        put_ghost(c2, cghost, f, pick_face(face(c2, f ^ 1), cidx[f]))
    for side in range(2):
        arrived(c_handles[side])
        for k in range(3):
            f = 2 * k + side
            value = pick(crec[side], cnidx[f]).reshape(8, 8, LANES)
            put_ghost(c2, cghost, f, jnp.where(cnidx[6 + f][None] != 0, value, get_ghost(c2, cghost, f)))
    sweep(c2, cghost, cwt, cbd, cupd, c3, 2)

    for k in (1, 0):
        place, octant = tidx[4 + 2 * k], tidx[5 + 2 * k]
        straight = (jnp.bitwise_and(octant, 1) == 0) == (row < 4)
        outer = jnp.right_shift(octant, 1)
        for i in range(4):
            quads = []
            for j in range(4):
                value = pick(c3[i + 1, j + 1], place)
                for o in range(1, 4):
                    value = jnp.where(outer == o, pick(c3[4 * (o // 2) + i + 1, 4 * (o % 2) + j + 1], place), value)
                quads.append(jnp.where(straight, value, pltpu.roll(value, 4, 0)))
            for half in range(2):
                at = 16 * i + 8 * half
                back[k, at:at + 8] = jnp.where(row < 4, quads[2 * half], quads[2 * half + 1])
        if k == 1:
            b_handles = [send(1, [(back.at[1], backr.at[0])]), send(-1, [(back.at[1], backr.at[1])])]
    for c in range(4):
        block = c3[2 * c + 1:2 * c + 3, 1:9].reshape(LANES, LANES).T
        cout_ref[:, c * LANES:(c + 1) * LANES] = block[COARSE:2 * COARSE]
    for handle in b_handles:
        arrived(handle)
    from_prev = jnp.where(lane < counts[2, 0], 1, 0)
    from_next = jnp.where(lane >= FINE - counts[2, 1], 1, 0)
    from_prev = jnp.broadcast_to(from_prev[None], (8, 8, LANES)).reshape(64, LANES)
    from_next = jnp.broadcast_to(from_next[None], (8, 8, LANES)).reshape(64, LANES)
    values = jnp.where(from_prev != 0, backr[0], jnp.where(from_next != 0, backr[1], back[0]))
    expand[pl.ds(0, 64, stride=2)] = values
    expand[pl.ds(1, 64, stride=2)] = values

    def correct_step(i, carry):
        four = expand[pl.ds(pl.multiple_of((i // 2) * 32, 32), 32)].reshape(4, 1, 8, LANES)
        xb[5, i + 1, 1:9] = x3[i + 1, 1:9] + jnp.broadcast_to(four, (4, 2, 8, LANES)).reshape(8, 8, LANES)
        return carry

    lax.fori_loop(0, 8, correct_step, 0)

    for at in range(3):
        exchange(5 + at, xb.at[5 + at])
        sweep(xb.at[5 + at], ghost, wt, bd, upd, xb.at[6 + at], at)
    for c in range(4):
        block = xb[8, 2 * c + 1:2 * c + 3, 1:9].reshape(LANES, LANES).T
        out_ref[:, c * LANES:(c + 1) * LANES] = block

    for offset in (1, -1, 2, -2):
        @pl.when(valid[offset])
        def _():
            for o, made in sent:
                if o == offset:
                    for copy in made:
                        copy.wait_send()


def solution(mesh):
    gx, gy = mesh.shape["gx"], mesh.shape["gy"]
    f32, i32 = jnp.float32, jnp.int32

    def on_device(*args):
        whole = pl.BlockSpec(memory_space=pltpu.VMEM)
        volume, padded = (8, 8, 8, LANES), (10, 10, 8, LANES)
        return pl.pallas_call(
            functools.partial(kernel, gx, gy),
            out_shape=(jax.ShapeDtypeStruct((FINE, 512), f32), jax.ShapeDtypeStruct((COARSE, 512), f32)),
            in_specs=[whole] * 7,
            out_specs=(whole, whole),
            scratch_shapes=[
                pltpu.VMEM((9,) + padded, f32),
                pltpu.VMEM((6,) + volume, f32),
                pltpu.VMEM(volume, f32),
                pltpu.VMEM(volume, f32),
                pltpu.VMEM(volume, f32),
                pltpu.VMEM((2, 8, 8, LANES), f32),
                pltpu.VMEM((8, 2, 8, 8, LANES), f32),
                pltpu.VMEM((8, 2, 3, 8, 8, LANES), f32),
                pltpu.VMEM((6, 8, LANES), i32),
                pltpu.VMEM((12, 8, LANES), i32),
                pltpu.VMEM((LANES, 512), f32),
                pltpu.VMEM((4,) + padded, f32),
                pltpu.VMEM((6,) + volume, f32),
                pltpu.VMEM(volume, f32),
                pltpu.VMEM(volume, f32),
                pltpu.VMEM(volume, f32),
                pltpu.VMEM((2, 8, 8, LANES), f32),
                pltpu.VMEM((LANES, 512), f32),
                pltpu.VMEM((8, 8, LANES), i32),
                pltpu.VMEM((4, 8, LANES), i32),
                pltpu.VMEM((6, 8, LANES), i32),
                pltpu.VMEM((2, 64, LANES), f32),
                pltpu.VMEM((2, 64, LANES), f32),
                pltpu.VMEM((12, 8, LANES), i32),
                pltpu.VMEM((5, 2, 8, LANES), i32),
                pltpu.VMEM((4, 64, LANES), f32),
                pltpu.VMEM((2, 32, LANES), f32),
                pltpu.VMEM((2, 32, LANES), f32),
                pltpu.VMEM((LANES, LANES), f32),
                pltpu.VMEM((2, 64, LANES), f32),
                pltpu.VMEM((2, 64, LANES), f32),
                pltpu.VMEM((LANES, LANES), f32),
                pltpu.SemaphoreType.DMA((N_COPIES,)),
                pltpu.SemaphoreType.DMA((N_COPIES,)),
            ],
            compiler_params=pltpu.CompilerParams(collective_id=0, has_side_effects=True, vmem_limit_bytes=40 * 1024 * 1024),
        )(*args)

    rows = P(("gx", "gy"), None)
    return jax.shard_map(on_device, mesh=mesh, in_specs=(rows,) * 7, out_specs=(rows, rows), check_vma=False)
```

```python
import functools

import jax
import jax.numpy as jnp
from jax import lax
from jax.experimental import pallas as pl
from jax.experimental.pallas import tpu as pltpu
from jax.sharding import PartitionSpec as P

THETA = 1.25
DELTA = 0.75
SIGMA = THETA / DELTA
RHO0 = 1.0 / SIGMA
RHO1 = 1.0 / (2.0 * SIGMA - RHO0)
RHO2 = 1.0 / (2.0 * SIGMA - RHO1)
SWEEPS = ((0.0, 1.0 / THETA), (RHO1 * RHO0, 2.0 * RHO1 / DELTA), (RHO2 * RHO1, 2.0 * RHO2 / DELTA))

LANES = 128
FINE = 128
COARSE = 32
MESH = pl.DeviceIdType.MESH
N_COPIES = 64


def pick(values, index):
    rows = values.shape[0]
    whole = jnp.broadcast_to(index[None], (rows // 8, 8, LANES)).reshape(rows, LANES)
    return jnp.take_along_axis(values, whole, axis=1, mode="promise_in_bounds")


def pick_face(face, index):
    return pick(face.reshape(64, LANES), index).reshape(8, 8, LANES)


def kernel(
    gx, gy,
    rhs_hbm, guess_hbm, coef_hbm, links_hbm, owner_hbm, ccoef_hbm, clinks_hbm,
    out_ref, cout_ref,
    rhs_ref, guess_ref, coef_ref, links_ref, owner_ref, clinks_ref,
    xb, wt, bd, dg, upd, ghost, packed, recv, fidx, fmask,
    ccrow, cxb, cwt, cidg, cbd, cupd, cghost, idrow, tidx, tsrc, cidx, crec, cpack, cnidx,
    counts, src, pair2, pair2r, tall, back, backr, expand,
    ssem, rsem, isem,
):
    devices = gx * gy
    me = lax.axis_index("gx") * gy + lax.axis_index("gy")
    valid = {1: me < devices - 1, -1: me > 0, 2: me < devices - 2, -2: me > 1}

    def device(offset):
        target = lax.rem(me + offset + devices, devices)
        return (target // gy, lax.rem(target, gy))

    barrier = pltpu.get_barrier_semaphore()
    for offset in (1, -1, 2, -2):
        @pl.when(valid[offset])
        def _():
            pl.semaphore_signal(barrier, inc=1, device_id=device(offset), device_id_type=MESH)

    fetches = []
    for at, (source, target) in enumerate((
            (coef_hbm, coef_ref), (guess_hbm, guess_ref), (owner_hbm, owner_ref), (links_hbm, links_ref),
            (ccoef_hbm, ccrow.at[COARSE:2 * COARSE]), (rhs_hbm, rhs_ref), (clinks_hbm, clinks_ref))):
        fetches.append(pltpu.make_async_copy(source, target, isem.at[at]))
        fetches[-1].start()

    used = [0]
    sent = []

    def send(offset, pairs):
        made = []
        for source, target in pairs:
            at = used[0]
            used[0] += 1
            made.append(pltpu.make_async_remote_copy(
                src_ref=source, dst_ref=target, send_sem=ssem.at[at], recv_sem=rsem.at[at],
                device_id=device(offset), device_id_type=MESH))

        @pl.when(valid[offset])
        def _():
            for copy in made:
                copy.start()

        sent.append((offset, made))
        return (offset, made)

    def arrived(handle, which=None):
        offset, made = handle

        @pl.when(valid[-offset])
        def _():
            for copy in (made if which is None else [made[which]]):
                copy.wait_recv()

    lane = lax.broadcasted_iota(jnp.int32, (8, LANES), 1)
    row = lax.broadcasted_iota(jnp.int32, (8, LANES), 0)
    row3 = lax.broadcasted_iota(jnp.int32, (8, 8, LANES), 1)
    first, last = row3 == 0, row3 == 7

    def load_cells(buffer, rows_ref):
        for c in range(4):
            block = rows_ref[:, c * LANES:(c + 1) * LANES].T
            buffer[2 * c + 1:2 * c + 3, 1:9] = block.reshape(2, 8, 8, LANES)

    def face(x, f):
        at = 1 if f % 2 == 0 else 8
        if f // 2 == 0:
            return x[at, 1:9]
        if f // 2 == 1:
            return x[1:9, at]
        return x[1:9, 1:9, 0 if f % 2 == 0 else 7]

    def put_ghost(x, g, f, value):
        at = 0 if f % 2 == 0 else 9
        if f // 2 == 0:
            x[at, 1:9] = value
        elif f // 2 == 1:
            x[1:9, at] = value
        else:
            g[f % 2] = value

    def get_ghost(x, g, f):
        at = 0 if f % 2 == 0 else 9
        if f // 2 == 0:
            return x[at, 1:9]
        if f // 2 == 1:
            return x[1:9, at]
        return g[f % 2]

    def neighbours(x, g, i):
        centre = x[i + 1, 1:9]
        low = jnp.where(first, g[0, i][:, None, :], pltpu.roll(centre, 1, 1))
        high = jnp.where(last, g[1, i][:, None, :], pltpu.roll(centre, 7, 1))
        return centre, (x[i, 1:9], x[i + 2, 1:9], x[i + 1, 0:8], x[i + 1, 2:10], low, high)

    def scaled_residual(x, g, w, b, i):
        centre, others = neighbours(x, g, i)
        total = b[i] - centre
        for f in range(6):
            total = total + w[f, i] * others[f]
        return centre, total

    def sweep(x, g, w, b, d, new, at):
        keep, gain = SWEEPS[at]

        def step(i, carry):
            centre, total = scaled_residual(x, g, w, b, i)
            update = gain * total
            if at > 0:
                update = update + keep * d[i]
            d[i] = update
            new[i + 1, 1:9] = centre + update
            return carry

        lax.fori_loop(0, 8, step, 0, unroll=True)

    def start_faces(e, x):
        packed[e, 0] = face(x, 4)
        packed[e, 1] = face(x, 5)
        up = send(1, [(x.at[8, 1:9], recv.at[e, 0, 0]), (x.at[1:9, 8], recv.at[e, 0, 1]), (packed.at[e, 1], recv.at[e, 0, 2])])
        down = send(-1, [(x.at[1, 1:9], recv.at[e, 1, 0]), (x.at[1:9, 1], recv.at[e, 1, 1]), (packed.at[e, 0], recv.at[e, 1, 2])])
        return up, down

    def own_ghosts(x, keep_own):
        for f in range(6):
            value = pick_face(face(x, f ^ 1), fidx[f])
            if keep_own:
                value = jnp.where(fmask[6 + f][None] != 0, value, face(x, f))
            put_ghost(x, ghost, f, value)

    def far_ghosts(e, x, handles):
        for side in range(2):
            arrived(handles[side])
        for k in range(3):
            for side in range(2):
                f = 2 * k + side
                value = pick_face(recv[e, side, k], fidx[f])
                put_ghost(x, ghost, f, jnp.where(fmask[f][None] != 0, value, get_ghost(x, ghost, f)))

    def exchange(e, x, between=None):
        handles = start_faces(e, x)
        own_ghosts(x, False)
        if between is not None:
            between()
        far_ghosts(e, x, handles)

    coef, x0 = xb.at[0], xb.at[1]
    fetches[0].wait()
    load_cells(coef, coef_ref)
    fetches[1].wait()
    load_cells(x0, guess_ref)
    for fetch in fetches[2:]:
        fetch.wait()

    owner = owner_ref[...]
    to_prev = jnp.sum((owner == me - 1).astype(jnp.float32), axis=1, keepdims=True).astype(jnp.int32)
    to_next = jnp.sum((owner == me + 1).astype(jnp.float32), axis=1, keepdims=True).astype(jnp.int32)
    counts[2, 0] = jnp.broadcast_to(to_prev, (8, LANES))
    counts[2, 1] = jnp.broadcast_to(to_next, (8, LANES))
    ccrow[3 * COARSE:] = jnp.ones((COARSE, 512), jnp.float32)

    pl.semaphore_wait(barrier, jnp.minimum(me, 2) + jnp.minimum(devices - 1 - me, 2))

    coef_handles = start_faces(0, coef)
    x0_handles = start_faces(1, x0)
    count_handles = [send(o, [(counts.at[2], counts.at[2 - o])]) for o in (1, -1, 2, -2)]
    ccoef_handles = [send(1, [(ccrow.at[COARSE:2 * COARSE], ccrow.at[0:COARSE])]),
                     send(-1, [(ccrow.at[COARSE:2 * COARSE], ccrow.at[2 * COARSE:3 * COARSE])])]

    links = links_ref[...]
    for f in range(6):
        ids = jnp.broadcast_to(links[f:f + 1], (8, LANES))
        live = ids >= 0
        fidx[f] = jnp.bitwise_and(ids, FINE - 1)
        fmask[f] = jnp.where(live & (jnp.right_shift(ids, 7) != me), 1, 0)
        fmask[6 + f] = jnp.where(live, 1, 0)

    for c in range(4):
        dg[2 * c:2 * c + 2] = rhs_ref[:, c * LANES:(c + 1) * LANES].T.reshape(2, 8, 8, LANES)
    own_ghosts(coef, True)
    far_ghosts(0, coef, coef_handles)

    def weigh(x, g, w, lives, finish):
        mask4 = jnp.where((row == 0) & (lives[4] == 0), 0.0, 1.0)[None]
        mask5 = jnp.where((row == 7) & (lives[5] == 0), 0.0, 1.0)[None]

        def step(i, carry):
            centre, others = neighbours(x, g, i)
            weights = [0.5 * (centre + other) for other in others]
            diag = weights[0]
            for weight in weights[1:]:
                diag = diag + weight
            inverse = 1.0 / diag
            for f in range(6):
                value = weights[f] * inverse
                if f == 4:
                    value = value * mask4
                if f == 5:
                    value = value * mask5
                w[f, i] = value
            finish(i, diag, inverse)
            return carry

        lax.fori_loop(0, 8, step, 0, unroll=True)
        w[0, 0] = jnp.where(lives[0][None] != 0, w[0, 0], 0.0)
        w[1, 7] = jnp.where(lives[1][None] != 0, w[1, 7], 0.0)
        w[2, :, 0] = jnp.where(lives[2][None] != 0, w[2, :, 0], 0.0)
        w[3, :, 7] = jnp.where(lives[3][None] != 0, w[3, :, 7], 0.0)

    def fine_finish(i, diag, inverse):
        bd[i] = dg[i] * inverse
        dg[i] = diag

    weigh(coef, ghost, wt, [fmask[6 + f] for f in range(6)], fine_finish)

    own_ghosts(x0, False)
    far_ghosts(1, x0, x0_handles)
    sweep(x0, ghost, wt, bd, upd, xb.at[2], 0)

    own_lane = (jnp.right_shift(lane, 5) == 1)
    group = jnp.right_shift(lane, 5)
    slot = jnp.bitwise_and(lane, COARSE - 1)
    coarse_handles = []

    def coarse_setup_a():
        for handle in ccoef_handles + count_handles:
            arrived(handle)
        load_cells(cxb.at[0], ccrow)
        zeros = jnp.zeros((6, COARSE), jnp.int32)
        links_c = jnp.concatenate([zeros, clinks_ref[...], zeros, zeros], axis=1)
        lives = []
        x = cxb.at[0]
        for f in range(6):
            ids = jnp.broadcast_to(links_c[f:f + 1], (8, LANES))
            live = ids >= 0
            step_by = jnp.right_shift(ids, 5) - me
            place = jnp.bitwise_and((step_by + 1) * COARSE + jnp.bitwise_and(ids, COARSE - 1), LANES - 1)
            place = jnp.where(own_lane & live, place, lane)
            cidx[f] = place
            cnidx[f] = jnp.bitwise_and(ids, COARSE - 1) + (f // 2) * COARSE
            cnidx[6 + f] = jnp.where(own_lane & live & (step_by != 0), 1, 0)
            lives.append(jnp.where(live, 1, 0))
            value = jnp.where(live[None], pick_face(face(x, f ^ 1), place), face(x, f))
            put_ghost(x, cghost, f, value)

        def finish(i, diag, inverse):
            cidg[i] = inverse

        weigh(x, cghost, cwt, lives, finish)
        for c in range(4):
            block = cidg[2 * c:2 * c + 2].reshape(LANES, LANES).T
            idrow[COARSE:2 * COARSE, c * LANES:(c + 1) * LANES] = block[COARSE:2 * COARSE]
        coarse_handles.append(send(1, [(idrow.at[COARSE:2 * COARSE], idrow.at[0:COARSE])]))
        coarse_handles.append(send(-1, [(idrow.at[COARSE:2 * COARSE], idrow.at[2 * COARSE:3 * COARSE])]))

    def known(k, which):
        return counts[k, which] if k == 2 else jnp.where(valid[k - 2], counts[k, which], 0)

    def by_group(values):
        return jnp.where(group == 0, values[0], jnp.where(group == 1, values[1], values[2]))

    def coarse_setup_b():
        a = [known(k, 0) for k in range(5)]
        n = [known(k, 1) for k in range(5)]
        stay = [FINE - a[k] - n[k] if k == 2 else jnp.where(valid[k - 2], FINE - a[k] - n[k], 0) for k in range(5)]
        before, here = by_group(n[0:3]), by_group(stay[1:4])
        start, after = by_group(a[1:4]), by_group(a[2:5])
        for o in range(4):
            rank = 8 * slot + 2 * o + jnp.where(row >= 4, 1, 0)
            in_before = rank < before
            in_here = rank < before + here
            in_after = rank < before + here + after
            at = jnp.where(in_before, FINE - before + rank, jnp.where(in_here, start + rank - before, rank - before - here))
            step_by = jnp.where(in_before, group - 2, jnp.where(in_here, group - 1, group))
            source = jnp.where((step_by == 2) | (step_by == -2), 0, step_by + 2)
            tidx[o] = jnp.bitwise_and(at, LANES - 1)
            tsrc[o] = jnp.where(in_after & (group < 3), source, 4)
        rank_own = n[1] + lane - a[2]
        rank_far = jnp.where(lane < 64, n[1] + stay[2] + lane, lane - FINE + n[1])
        for k, rank in enumerate((rank_own, rank_far)):
            rank = jnp.bitwise_and(rank, 255)
            tidx[4 + 2 * k] = COARSE + jnp.right_shift(rank, 3)
            tidx[5 + 2 * k] = jnp.bitwise_and(rank, 7)

    def coarse_setup_c():
        for handle in coarse_handles:
            arrived(handle)
        for c in range(4):
            block = idrow[:, c * LANES:(c + 1) * LANES].T
            cidg[2 * c:2 * c + 2] = block.reshape(2, 8, 8, LANES)

    exchange(2, xb.at[2], coarse_setup_a)
    sweep(xb.at[2], ghost, wt, bd, upd, xb.at[3], 1)
    exchange(3, xb.at[3], coarse_setup_b)
    sweep(xb.at[3], ghost, wt, bd, upd, xb.at[4], 2)
    exchange(4, xb.at[4], coarse_setup_c)

    x3 = xb.at[4]

    def restrict_step(i, carry):
        total = jnp.zeros((4, 8, LANES), jnp.float32)
        for half in range(2):
            _, scaled = scaled_residual(x3, ghost, wt, bd, 2 * i + half)
            quads = (scaled * dg[2 * i + half]).reshape(4, 2, 8, LANES)
            total = total + quads[:, 0] + quads[:, 1]
        total = total + pltpu.roll(total, 7, 1)
        tall[pl.ds(pl.multiple_of(i * 32, 32), 32)] = 0.5 * total.reshape(32, LANES)
        return carry

    lax.fori_loop(0, 4, restrict_step, 0, unroll=True)
    restricted = tall[pl.ds(0, 64, stride=2)]
    src[2] = restricted
    low_lane = jnp.broadcast_to((lane < 64)[None], (4, 8, LANES)).reshape(32, LANES)
    turned = pltpu.roll(restricted[32:], 64, 1)
    pair2[0] = jnp.where(low_lane, turned, restricted[:32])
    pair2[1] = jnp.where(low_lane, restricted[:32], turned)
    r_handles = [send(1, [(src.at[2], src.at[1])]), send(-1, [(src.at[2], src.at[3])]),
                 send(2, [(pair2.at[0], pair2r.at[0])]), send(-2, [(pair2.at[1], pair2r.at[1])])]
    for handle in r_handles:
        arrived(handle)
    src[0, 0:32] = jnp.where(low_lane, pair2r[1], pair2r[0])
    src[0, 32:64] = pltpu.roll(jnp.where(low_lane, pair2r[0], pair2r[1]), 64, 1)

    for o in range(4):
        ox, oy = o // 2, o % 2
        index, which = tidx[o], tsrc[o]
        for i in range(4):
            for j in range(4):
                q = 4 * (4 * i + j)
                value = jnp.zeros((8, LANES), jnp.float32)
                for k in range(4):
                    four = src[k, q:q + 4]
                    taken = pick(jnp.concatenate([four, four], axis=0), index)
                    value = jnp.where(which == k, taken, value)
                at = (4 * ox + i, 4 * oy + j)
                scaled = value * cidg[at[0], at[1]]
                cbd[at[0], at[1]] = scaled
                update = scaled * (1.0 / THETA)
                cupd[at[0], at[1]] = update
                cxb[1, at[0] + 1, at[1] + 1] = update

    c1, c2, c3 = cxb.at[1], cxb.at[2], cxb.at[3]
    for f in range(6):
        put_ghost(c1, cghost, f, pick_face(face(c1, f ^ 1), cidx[f]))
    sweep(c1, cghost, cwt, cbd, cupd, c2, 1)

    lane64 = jnp.broadcast_to(lane[None], (8, 8, LANES)).reshape(64, LANES)
    for side in range(2):
        faces = [face(c2, 2 * k + side).reshape(64, LANES) for k in range(3)]
        cpack[side] = jnp.where(lane64 < 32, pltpu.roll(faces[0], 96, 1), jnp.where(lane64 < 64, faces[1], pltpu.roll(faces[2], 32, 1)))
    c_handles = [send(1, [(cpack.at[1], crec.at[0])]), send(-1, [(cpack.at[0], crec.at[1])])]
    for f in range(6):
        put_ghost(c2, cghost, f, pick_face(face(c2, f ^ 1), cidx[f]))
    for side in range(2):
        arrived(c_handles[side])
        for k in range(3):
            f = 2 * k + side
            value = pick(crec[side], cnidx[f]).reshape(8, 8, LANES)
            put_ghost(c2, cghost, f, jnp.where(cnidx[6 + f][None] != 0, value, get_ghost(c2, cghost, f)))
    sweep(c2, cghost, cwt, cbd, cupd, c3, 2)

    for k in (1, 0):
        place, octant = tidx[4 + 2 * k], tidx[5 + 2 * k]
        straight = (jnp.bitwise_and(octant, 1) == 0) == (row < 4)
        outer = jnp.right_shift(octant, 1)
        for i in range(4):
            quads = []
            for j in range(4):
                value = pick(c3[i + 1, j + 1], place)
                for o in range(1, 4):
                    value = jnp.where(outer == o, pick(c3[4 * (o // 2) + i + 1, 4 * (o % 2) + j + 1], place), value)
                quads.append(jnp.where(straight, value, pltpu.roll(value, 4, 0)))
            for half in range(2):
                at = 16 * i + 8 * half
                back[k, at:at + 8] = jnp.where(row < 4, quads[2 * half], quads[2 * half + 1])
        if k == 1:
            b_handles = [send(1, [(back.at[1], backr.at[0])]), send(-1, [(back.at[1], backr.at[1])])]
    for c in range(4):
        block = c3[2 * c + 1:2 * c + 3, 1:9].reshape(LANES, LANES).T
        cout_ref[:, c * LANES:(c + 1) * LANES] = block[COARSE:2 * COARSE]
    for handle in b_handles:
        arrived(handle)
    from_prev = jnp.where(lane < counts[2, 0], 1, 0)
    from_next = jnp.where(lane >= FINE - counts[2, 1], 1, 0)
    from_prev = jnp.broadcast_to(from_prev[None], (8, 8, LANES)).reshape(64, LANES)
    from_next = jnp.broadcast_to(from_next[None], (8, 8, LANES)).reshape(64, LANES)
    values = jnp.where(from_prev != 0, backr[0], jnp.where(from_next != 0, backr[1], back[0]))
    expand[pl.ds(0, 64, stride=2)] = values
    expand[pl.ds(1, 64, stride=2)] = values

    def correct_step(i, carry):
        four = expand[pl.ds(pl.multiple_of((i // 2) * 32, 32), 32)].reshape(4, 1, 8, LANES)
        xb[5, i + 1, 1:9] = x3[i + 1, 1:9] + jnp.broadcast_to(four, (4, 2, 8, LANES)).reshape(8, 8, LANES)
        return carry

    lax.fori_loop(0, 8, correct_step, 0, unroll=True)

    for at in range(3):
        exchange(5 + at, xb.at[5 + at])
        sweep(xb.at[5 + at], ghost, wt, bd, upd, xb.at[6 + at], at)
    for c in range(4):
        block = xb[8, 2 * c + 1:2 * c + 3, 1:9].reshape(LANES, LANES).T
        out_ref[:, c * LANES:(c + 1) * LANES] = block

    for offset in (1, -1, 2, -2):
        @pl.when(valid[offset])
        def _():
            for o, made in sent:
                if o == offset:
                    for copy in made:
                        copy.wait_send()


def solution(mesh):
    gx, gy = mesh.shape["gx"], mesh.shape["gy"]
    f32, i32 = jnp.float32, jnp.int32

    def on_device(rhs, guess, coef, links, owner, ccoef, clinks):
        whole = pl.BlockSpec(memory_space=pltpu.VMEM)
        volume, padded = (8, 8, 8, LANES), (10, 10, 8, LANES)
        return pl.pallas_call(
            functools.partial(kernel, gx, gy),
            out_shape=(jax.ShapeDtypeStruct((FINE, 512), f32), jax.ShapeDtypeStruct((COARSE, 512), f32)),
            in_specs=[pl.BlockSpec(memory_space=pltpu.HBM)] * 7,
            out_specs=(whole, whole),
            scratch_shapes=[
                pltpu.VMEM((FINE, 512), f32),
                pltpu.VMEM((FINE, 512), f32),
                pltpu.VMEM((FINE, 512), f32),
                pltpu.VMEM((6, FINE), i32),
                pltpu.VMEM((1, FINE), i32),
                pltpu.VMEM((6, COARSE), i32),
                pltpu.VMEM((9,) + padded, f32),
                pltpu.VMEM((6,) + volume, f32),
                pltpu.VMEM(volume, f32),
                pltpu.VMEM(volume, f32),
                pltpu.VMEM(volume, f32),
                pltpu.VMEM((2, 8, 8, LANES), f32),
                pltpu.VMEM((8, 2, 8, 8, LANES), f32),
                pltpu.VMEM((8, 2, 3, 8, 8, LANES), f32),
                pltpu.VMEM((6, 8, LANES), i32),
                pltpu.VMEM((12, 8, LANES), i32),
                pltpu.VMEM((LANES, 512), f32),
                pltpu.VMEM((4,) + padded, f32),
                pltpu.VMEM((6,) + volume, f32),
                pltpu.VMEM(volume, f32),
                pltpu.VMEM(volume, f32),
                pltpu.VMEM(volume, f32),
                pltpu.VMEM((2, 8, 8, LANES), f32),
                pltpu.VMEM((LANES, 512), f32),
                pltpu.VMEM((8, 8, LANES), i32),
                pltpu.VMEM((4, 8, LANES), i32),
                pltpu.VMEM((6, 8, LANES), i32),
                pltpu.VMEM((2, 64, LANES), f32),
                pltpu.VMEM((2, 64, LANES), f32),
                pltpu.VMEM((12, 8, LANES), i32),
                pltpu.VMEM((5, 2, 8, LANES), i32),
                pltpu.VMEM((4, 64, LANES), f32),
                pltpu.VMEM((2, 32, LANES), f32),
                pltpu.VMEM((2, 32, LANES), f32),
                pltpu.VMEM((LANES, LANES), f32),
                pltpu.VMEM((2, 64, LANES), f32),
                pltpu.VMEM((2, 64, LANES), f32),
                pltpu.VMEM((LANES, LANES), f32),
                pltpu.SemaphoreType.DMA((N_COPIES,)),
                pltpu.SemaphoreType.DMA((N_COPIES,)),
                pltpu.SemaphoreType.DMA((7,)),
            ],
            compiler_params=pltpu.CompilerParams(collective_id=0, has_side_effects=True, vmem_limit_bytes=56 * 1024 * 1024),
        )(rhs, guess, coef, links.T, owner.T, ccoef, clinks.T)

    rows = P(("gx", "gy"), None)
    return jax.shard_map(on_device, mesh=mesh, in_specs=(rows,) * 7, out_specs=(rows, rows), check_vma=False)
```

```python
import functools

import jax
import jax.numpy as jnp
from jax import lax
from jax.experimental import pallas as pl
from jax.experimental.pallas import tpu as pltpu
from jax.sharding import PartitionSpec as P

THETA = 1.25
DELTA = 0.75
SIGMA = THETA / DELTA
RHO0 = 1.0 / SIGMA
RHO1 = 1.0 / (2.0 * SIGMA - RHO0)
RHO2 = 1.0 / (2.0 * SIGMA - RHO1)
SWEEPS = ((0.0, 1.0 / THETA), (RHO1 * RHO0, 2.0 * RHO1 / DELTA), (RHO2 * RHO1, 2.0 * RHO2 / DELTA))

LANES = 128
FINE = 128
COARSE = 32
MESH = pl.DeviceIdType.MESH
N_COPIES = 96


def pick(values, index):
    rows = values.shape[0]
    whole = jnp.broadcast_to(index[None], (rows // 8, 8, LANES)).reshape(rows, LANES)
    return jnp.take_along_axis(values, whole, axis=1, mode="promise_in_bounds")


def pick_face(face, index):
    return pick(face.reshape(64, LANES), index).reshape(8, 8, LANES)


def kernel(
    gx, gy,
    rhs_hbm, guess_hbm, coef_hbm, links_hbm, owner_hbm, ccoef_hbm, clinks_hbm,
    out_ref, cout_ref,
    rhs_ref, guess_ref, coef_ref, links_ref, owner_ref, clinks_ref,
    xb, wt, bd, dg, upd, ghost, packed, recv, fidx, fmask,
    ccrow, cxb, cwt, cidg, cbd, cupd, cghost, idrow, tidx, tsrc, cidx, crec, cpack, cnidx,
    counts, src, pair2, pair2r, tall, back, backr, expand, near, expand2, ghost2,
    nlinks, nidx, nmask, wface, flux, edges, erecv, beside, ghost3,
    ssem, rsem, isem,
):
    devices = gx * gy
    me = lax.axis_index("gx") * gy + lax.axis_index("gy")
    valid = {1: me < devices - 1, -1: me > 0, 2: me < devices - 2, -2: me > 1}

    def device(offset):
        target = lax.rem(me + offset + devices, devices)
        return (target // gy, lax.rem(target, gy))

    barrier = pltpu.get_barrier_semaphore()
    for offset in (1, -1, 2, -2):
        @pl.when(valid[offset])
        def _():
            pl.semaphore_signal(barrier, inc=1, device_id=device(offset), device_id_type=MESH)

    fetches = []
    for at, (source, target) in enumerate((
            (coef_hbm, coef_ref), (guess_hbm, guess_ref), (owner_hbm, owner_ref), (links_hbm, links_ref),
            (ccoef_hbm, ccrow.at[COARSE:2 * COARSE]), (rhs_hbm, rhs_ref), (clinks_hbm, clinks_ref))):
        fetches.append(pltpu.make_async_copy(source, target, isem.at[at]))
        fetches[-1].start()

    used = [0]
    sent = []

    def send(offset, pairs):
        made = []
        for source, target in pairs:
            at = used[0]
            used[0] += 1
            made.append(pltpu.make_async_remote_copy(
                src_ref=source, dst_ref=target, send_sem=ssem.at[at], recv_sem=rsem.at[at],
                device_id=device(offset), device_id_type=MESH))

        @pl.when(valid[offset])
        def _():
            for copy in made:
                copy.start()

        sent.append((offset, made))
        return (offset, made)

    def arrived(handle, which=None):
        offset, made = handle

        @pl.when(valid[-offset])
        def _():
            for copy in (made if which is None else [made[which]]):
                copy.wait_recv()

    lane = lax.broadcasted_iota(jnp.int32, (8, LANES), 1)
    row = lax.broadcasted_iota(jnp.int32, (8, LANES), 0)
    row3 = lax.broadcasted_iota(jnp.int32, (8, 8, LANES), 1)
    first, last = row3 == 0, row3 == 7

    def load_cells(buffer, rows_ref):
        for c in range(4):
            block = rows_ref[:, c * LANES:(c + 1) * LANES].T
            buffer[2 * c + 1:2 * c + 3, 1:9] = block.reshape(2, 8, 8, LANES)

    def face(x, f):
        at = 1 if f % 2 == 0 else 8
        if f // 2 == 0:
            return x[at, 1:9]
        if f // 2 == 1:
            return x[1:9, at]
        return x[1:9, 1:9, 0 if f % 2 == 0 else 7]

    def put_ghost(x, g, f, value):
        at = 0 if f % 2 == 0 else 9
        if f // 2 == 0:
            x[at, 1:9] = value
        elif f // 2 == 1:
            x[1:9, at] = value
        else:
            g[f % 2] = value

    def get_ghost(x, g, f):
        at = 0 if f % 2 == 0 else 9
        if f // 2 == 0:
            return x[at, 1:9]
        if f // 2 == 1:
            return x[1:9, at]
        return g[f % 2]

    def neighbours(x, g, i):
        centre = x[i + 1, 1:9]
        low = jnp.where(first, g[0, i][:, None, :], pltpu.roll(centre, 1, 1))
        high = jnp.where(last, g[1, i][:, None, :], pltpu.roll(centre, 7, 1))
        return centre, (x[i, 1:9], x[i + 2, 1:9], x[i + 1, 0:8], x[i + 1, 2:10], low, high)

    def scaled_residual(x, g, w, b, i):
        centre, others = neighbours(x, g, i)
        total = b[i] - centre
        for f in range(6):
            total = total + w[f, i] * others[f]
        return centre, total

    def sweep(x, g, w, b, d, new, at, final=True):
        keep, gain = SWEEPS[at]

        def step(i, carry):
            centre, total = scaled_residual(x, g, w, b, i)
            update = gain * total
            if at > 0:
                update = update + keep * d[i]
            if final:
                d[i] = update
            new[i + 1, 1:9] = centre + update
            return carry

        lax.fori_loop(0, 8, step, 0, unroll=True)

    def start_faces(e, x):
        packed[e, 0] = face(x, 4)
        packed[e, 1] = face(x, 5)
        up = send(1, [(x.at[8, 1:9], recv.at[e, 0, 0]), (x.at[1:9, 8], recv.at[e, 0, 1]), (packed.at[e, 1], recv.at[e, 0, 2])])
        down = send(-1, [(x.at[1, 1:9], recv.at[e, 1, 0]), (x.at[1:9, 1], recv.at[e, 1, 1]), (packed.at[e, 0], recv.at[e, 1, 2])])
        return up, down

    def own_ghosts(x, g, keep_own=False, zero_far=False):
        for f in range(6):
            value = pick_face(face(x, f ^ 1), fidx[f])
            if keep_own:
                value = jnp.where(fmask[6 + f][None] != 0, value, face(x, f))
            if zero_far:
                value = jnp.where(fmask[f][None] != 0, 0.0, value)
            put_ghost(x, g, f, value)

    def far_ghosts(faces, x, g, handles=()):
        for handle in handles:
            arrived(handle)
        for k in range(3):
            for side in range(2):
                f = 2 * k + side
                value = pick_face(faces[side, k], fidx[f])
                put_ghost(x, g, f, jnp.where(fmask[f][None] != 0, value, get_ghost(x, g, f)))

    def across(k, m):
        return (m if m < k else m - 1)

    def line(k, m, at):
        return (at,) if across(k, m) == 0 else (slice(None), at)

    def two_sweeps(x, g, middle, g_middle, new, partial, e, between=None):
        keep, gain = SWEEPS[1]
        handles = start_faces(e, x)
        for side in range(2):
            for k in range(3):
                f = 2 * k + side
                value = pick_face(face(x, f) * wface[f], nidx[side, k])
                flux[side, k] = jnp.where(nmask[side, k][None] != 0, value, 0.0)
        at = 0
        for m in range(3):
            for k in range(3):
                if k != m:
                    for side in range(2):
                        edges[e // 7, side, at] = flux[(side, m) + line(m, k, 7 if side else 0)]
                    at += 1
        edge_handles = [send(2, [(edges.at[e // 7, 1], erecv.at[e // 7, 0])]), send(-2, [(edges.at[e // 7, 0], erecv.at[e // 7, 1])])]
        own_ghosts(x, g, zero_far=True)
        sweep(x, g, wt, bd, upd, partial, 1, final=False)
        partial_handles = start_faces(e + 1, partial)
        for side in range(2):
            end = 0 if side else 7
            for k in range(3):
                beside[side, k] = flux[side, k]
                for m in range(3):
                    if m != k:
                        where = (side, k) + line(k, m, end)
                        beside[where] = beside[where] + flux[(side, m) + line(m, k, end)]
        if between is not None:
            between()
        far_ghosts(recv.at[e], x, g, handles)
        sweep(x, g, wt, bd, upd, middle, 1)
        own_ghosts(middle, g_middle)
        for handle in edge_handles + list(partial_handles):
            arrived(handle)
        for side in range(2):
            end = 0 if side else 7
            at = 0
            for m in range(3):
                for k in range(3):
                    if k != m:
                        where = (side, k) + line(k, m, 7 - end)
                        behind = jnp.where(valid[2 if side else -2], erecv[e // 7, side, at], 0.0)
                        beside[where] = beside[where] + behind
                        at += 1
        for side in range(2):
            for k in range(3):
                beside[side, k] = recv[e + 1, side, k] + gain * recv[3, side, k] * beside[side, k]
        far_ghosts(beside, middle, g_middle)
        sweep(middle, g_middle, wt, bd, upd, new, 2)

    coef, x0 = xb.at[0], xb.at[1]
    fetches[0].wait()
    load_cells(coef, coef_ref)
    fetches[1].wait()
    load_cells(x0, guess_ref)
    for fetch in fetches[2:]:
        fetch.wait()

    owner = owner_ref[...]
    to_prev = jnp.sum((owner == me - 1).astype(jnp.float32), axis=1, keepdims=True).astype(jnp.int32)
    to_next = jnp.sum((owner == me + 1).astype(jnp.float32), axis=1, keepdims=True).astype(jnp.int32)
    counts[2, 0] = jnp.broadcast_to(to_prev, (8, LANES))
    counts[2, 1] = jnp.broadcast_to(to_next, (8, LANES))
    ccrow[3 * COARSE:] = jnp.ones((COARSE, 512), jnp.float32)

    pl.semaphore_wait(barrier, jnp.minimum(me, 2) + jnp.minimum(devices - 1 - me, 2))

    coef_handles = start_faces(0, coef)
    x0_handles = start_faces(1, x0)
    count_handles = [send(o, [(counts.at[2], counts.at[2 - o])]) for o in (1, -1, 2, -2)]
    link_handles = [send(1, [(links_ref, nlinks.at[0])]), send(-1, [(links_ref, nlinks.at[1])])]
    ccoef_handles = [send(1, [(ccrow.at[COARSE:2 * COARSE], ccrow.at[0:COARSE])]),
                     send(-1, [(ccrow.at[COARSE:2 * COARSE], ccrow.at[2 * COARSE:3 * COARSE])])]

    links = links_ref[...]
    for f in range(6):
        ids = jnp.broadcast_to(links[f:f + 1], (8, LANES))
        live = ids >= 0
        fidx[f] = jnp.bitwise_and(ids, FINE - 1)
        fmask[f] = jnp.where(live & (jnp.right_shift(ids, 7) != me), 1, 0)
        fmask[6 + f] = jnp.where(live, 1, 0)

    for c in range(4):
        dg[2 * c:2 * c + 2] = rhs_ref[:, c * LANES:(c + 1) * LANES].T.reshape(2, 8, 8, LANES)
    own_ghosts(coef, ghost, keep_own=True)
    far_ghosts(recv.at[0], coef, ghost, coef_handles)

    def weigh(x, g, w, lives, finish):
        mask4 = jnp.where((row == 0) & (lives[4] == 0), 0.0, 1.0)[None]
        mask5 = jnp.where((row == 7) & (lives[5] == 0), 0.0, 1.0)[None]

        def step(i, carry):
            centre, others = neighbours(x, g, i)
            weights = [0.5 * (centre + other) for other in others]
            diag = weights[0]
            for weight in weights[1:]:
                diag = diag + weight
            inverse = 1.0 / diag
            for f in range(6):
                value = weights[f] * inverse
                if f == 4:
                    value = value * mask4
                if f == 5:
                    value = value * mask5
                w[f, i] = value
            finish(i, diag, inverse)
            return carry

        lax.fori_loop(0, 8, step, 0, unroll=True)
        w[0, 0] = jnp.where(lives[0][None] != 0, w[0, 0], 0.0)
        w[1, 7] = jnp.where(lives[1][None] != 0, w[1, 7], 0.0)
        w[2, :, 0] = jnp.where(lives[2][None] != 0, w[2, :, 0], 0.0)
        w[3, :, 7] = jnp.where(lives[3][None] != 0, w[3, :, 7], 0.0)

    def fine_finish(i, diag, inverse):
        bd[i] = dg[i] * inverse
        dg[i] = diag
        xb[9, i + 1, 1:9] = inverse

    weigh(coef, ghost, wt, [fmask[6 + f] for f in range(6)], fine_finish)

    inverse_handles = start_faces(3, xb.at[9])
    own_ghosts(x0, ghost)
    far_ghosts(recv.at[1], x0, ghost, x0_handles)
    sweep(x0, ghost, wt, bd, upd, xb.at[2], 0)
    for handle in link_handles:
        arrived(handle)
    for side in range(2):
        for k in range(3):
            f = 2 * k + side
            cut = (0 if side == 0 else 7,)
            cut = (slice(None),) * k + cut
            wface[f] = wt[(f,) + cut] * dg[cut]
            ids = jnp.broadcast_to(nlinks[side, 2 * k + 1 - side:2 * k + 2 - side], (8, LANES))
            nidx[side, k] = jnp.bitwise_and(ids, FINE - 1)
            linked = (ids >= 0) & (jnp.right_shift(ids, 7) == me) & valid[1 if side else -1]
            nmask[side, k] = jnp.where(linked, 1, 0)

    own_lane = (jnp.right_shift(lane, 5) == 1)
    group = jnp.right_shift(lane, 5)
    slot = jnp.bitwise_and(lane, COARSE - 1)
    coarse_handles = []

    def coarse_setup_a():
        for handle in ccoef_handles + count_handles:
            arrived(handle)
        load_cells(cxb.at[0], ccrow)
        zeros = jnp.zeros((6, COARSE), jnp.int32)
        links_c = jnp.concatenate([zeros, clinks_ref[...], zeros, zeros], axis=1)
        lives = []
        x = cxb.at[0]
        for f in range(6):
            ids = jnp.broadcast_to(links_c[f:f + 1], (8, LANES))
            live = ids >= 0
            step_by = jnp.right_shift(ids, 5) - me
            place = jnp.bitwise_and((step_by + 1) * COARSE + jnp.bitwise_and(ids, COARSE - 1), LANES - 1)
            place = jnp.where(own_lane & live, place, lane)
            cidx[f] = place
            cnidx[f] = jnp.bitwise_and(ids, COARSE - 1) + (f // 2) * COARSE
            cnidx[6 + f] = jnp.where(own_lane & live & (step_by != 0), 1, 0)
            lives.append(jnp.where(live, 1, 0))
            value = jnp.where(live[None], pick_face(face(x, f ^ 1), place), face(x, f))
            put_ghost(x, cghost, f, value)

        def finish(i, diag, inverse):
            cidg[i] = inverse

        weigh(x, cghost, cwt, lives, finish)
        for c in range(4):
            block = cidg[2 * c:2 * c + 2].reshape(LANES, LANES).T
            idrow[COARSE:2 * COARSE, c * LANES:(c + 1) * LANES] = block[COARSE:2 * COARSE]
        coarse_handles.append(send(1, [(idrow.at[COARSE:2 * COARSE], idrow.at[0:COARSE])]))
        coarse_handles.append(send(-1, [(idrow.at[COARSE:2 * COARSE], idrow.at[2 * COARSE:3 * COARSE])]))

    def known(k, which):
        return counts[k, which] if k == 2 else jnp.where(valid[k - 2], counts[k, which], 0)

    def by_group(values):
        return jnp.where(group == 0, values[0], jnp.where(group == 1, values[1], values[2]))

    def coarse_setup_b():
        a = [known(k, 0) for k in range(5)]
        n = [known(k, 1) for k in range(5)]
        stay = [FINE - a[k] - n[k] if k == 2 else jnp.where(valid[k - 2], FINE - a[k] - n[k], 0) for k in range(5)]
        before, here = by_group(n[0:3]), by_group(stay[1:4])
        start, after = by_group(a[1:4]), by_group(a[2:5])
        for o in range(4):
            rank = 8 * slot + 2 * o + jnp.where(row >= 4, 1, 0)
            in_before = rank < before
            in_here = rank < before + here
            in_after = rank < before + here + after
            at = jnp.where(in_before, FINE - before + rank, jnp.where(in_here, start + rank - before, rank - before - here))
            step_by = jnp.where(in_before, group - 2, jnp.where(in_here, group - 1, group))
            source = jnp.where((step_by == 2) | (step_by == -2), 0, step_by + 2)
            tidx[o] = jnp.bitwise_and(at, LANES - 1)
            tsrc[o] = jnp.where(in_after & (group < 3), source, 4)
        rank_own = n[1] + lane - a[2]
        rank_far = jnp.where(lane < 64, n[1] + stay[2] + lane, lane - FINE + n[1])
        for k, rank in enumerate((rank_own, rank_far)):
            rank = jnp.bitwise_and(rank, 255)
            tidx[4 + 2 * k] = COARSE + jnp.right_shift(rank, 3)
            tidx[5 + 2 * k] = jnp.bitwise_and(rank, 7)

    def coarse_setup_c():
        for handle in coarse_handles:
            arrived(handle)
        for c in range(4):
            block = idrow[:, c * LANES:(c + 1) * LANES].T
            cidg[2 * c:2 * c + 2] = block.reshape(2, 8, 8, LANES)

    def setup_first():
        for handle in inverse_handles:
            arrived(handle)
        coarse_setup_a()
        coarse_setup_b()

    two_sweeps(xb.at[2], ghost, xb.at[3], ghost3, xb.at[4], xb.at[10], 6, setup_first)
    x3_handles = start_faces(4, xb.at[4])
    own_ghosts(xb.at[4], ghost)
    coarse_setup_c()
    far_ghosts(recv.at[4], xb.at[4], ghost, x3_handles)

    x3 = xb.at[4]

    def restrict_step(i, carry):
        total = jnp.zeros((4, 8, LANES), jnp.float32)
        for half in range(2):
            _, scaled = scaled_residual(x3, ghost, wt, bd, 2 * i + half)
            quads = (scaled * dg[2 * i + half]).reshape(4, 2, 8, LANES)
            total = total + quads[:, 0] + quads[:, 1]
        total = total + pltpu.roll(total, 7, 1)
        tall[pl.ds(pl.multiple_of(i * 32, 32), 32)] = 0.5 * total.reshape(32, LANES)
        return carry

    lax.fori_loop(0, 4, restrict_step, 0, unroll=True)
    restricted = tall[pl.ds(0, 64, stride=2)]
    src[2] = restricted
    low_lane = jnp.broadcast_to((lane < 64)[None], (4, 8, LANES)).reshape(32, LANES)
    turned = pltpu.roll(restricted[32:], 64, 1)
    pair2[0] = jnp.where(low_lane, turned, restricted[:32])
    pair2[1] = jnp.where(low_lane, restricted[:32], turned)
    r_handles = [send(1, [(src.at[2], src.at[1])]), send(-1, [(src.at[2], src.at[3])]),
                 send(2, [(pair2.at[0], pair2r.at[0])]), send(-2, [(pair2.at[1], pair2r.at[1])])]
    for handle in r_handles:
        arrived(handle)
    src[0, 0:32] = jnp.where(low_lane, pair2r[1], pair2r[0])
    src[0, 32:64] = pltpu.roll(jnp.where(low_lane, pair2r[0], pair2r[1]), 64, 1)

    for o in range(4):
        ox, oy = o // 2, o % 2
        index, which = tidx[o], tsrc[o]
        for i in range(4):
            for j in range(4):
                q = 4 * (4 * i + j)
                value = jnp.zeros((8, LANES), jnp.float32)
                for k in range(4):
                    four = src[k, q:q + 4]
                    taken = pick(jnp.concatenate([four, four], axis=0), index)
                    value = jnp.where(which == k, taken, value)
                at = (4 * ox + i, 4 * oy + j)
                scaled = value * cidg[at[0], at[1]]
                cbd[at[0], at[1]] = scaled
                update = scaled * (1.0 / THETA)
                cupd[at[0], at[1]] = update
                cxb[1, at[0] + 1, at[1] + 1] = update

    c1, c2, c3 = cxb.at[1], cxb.at[2], cxb.at[3]
    for f in range(6):
        put_ghost(c1, cghost, f, pick_face(face(c1, f ^ 1), cidx[f]))
    sweep(c1, cghost, cwt, cbd, cupd, c2, 1)

    lane64 = jnp.broadcast_to(lane[None], (8, 8, LANES)).reshape(64, LANES)
    for side in range(2):
        faces = [face(c2, 2 * k + side).reshape(64, LANES) for k in range(3)]
        cpack[side] = jnp.where(lane64 < 32, pltpu.roll(faces[0], 96, 1), jnp.where(lane64 < 64, faces[1], pltpu.roll(faces[2], 32, 1)))
    c_handles = [send(1, [(cpack.at[1], crec.at[0])]), send(-1, [(cpack.at[0], crec.at[1])])]
    for f in range(6):
        put_ghost(c2, cghost, f, pick_face(face(c2, f ^ 1), cidx[f]))
    for side in range(2):
        arrived(c_handles[side])
        for k in range(3):
            f = 2 * k + side
            value = pick(crec[side], cnidx[f]).reshape(8, 8, LANES)
            put_ghost(c2, cghost, f, jnp.where(cnidx[6 + f][None] != 0, value, get_ghost(c2, cghost, f)))
    sweep(c2, cghost, cwt, cbd, cupd, c3, 2)

    for k in (1, 0):
        place, octant = tidx[4 + 2 * k], tidx[5 + 2 * k]
        straight = (jnp.bitwise_and(octant, 1) == 0) == (row < 4)
        outer = jnp.right_shift(octant, 1)
        for i in range(4):
            quads = []
            for j in range(4):
                value = pick(c3[i + 1, j + 1], place)
                for o in range(1, 4):
                    value = jnp.where(outer == o, pick(c3[4 * (o // 2) + i + 1, 4 * (o % 2) + j + 1], place), value)
                quads.append(jnp.where(straight, value, pltpu.roll(value, 4, 0)))
            for half in range(2):
                at = 16 * i + 8 * half
                back[k, at:at + 8] = jnp.where(row < 4, quads[2 * half], quads[2 * half + 1])
        if k == 1:
            b_handles = [send(1, [(back.at[1], backr.at[0])]), send(-1, [(back.at[1], backr.at[1])]),
                         send(2, [(back.at[1], backr.at[2])]), send(-2, [(back.at[1], backr.at[3])])]
        else:
            b_handles += [send(1, [(back.at[0], backr.at[4])]), send(-1, [(back.at[0], backr.at[5])])]
    for c in range(4):
        block = c3[2 * c + 1:2 * c + 3, 1:9].reshape(LANES, LANES).T
        cout_ref[:, c * LANES:(c + 1) * LANES] = block[COARSE:2 * COARSE]
    for handle in b_handles:
        arrived(handle)

    def by_owner(at, before, here, after):
        low = jnp.where(lane < known(at, 0), 1, 0)
        high = jnp.where(lane >= FINE - known(at, 1), 1, 0)
        low = jnp.broadcast_to(low[None], (8, 8, LANES)).reshape(64, LANES)
        high = jnp.broadcast_to(high[None], (8, 8, LANES)).reshape(64, LANES)
        return jnp.where(low != 0, before, jnp.where(high != 0, after, here))

    values = by_owner(2, backr[0], back[0], backr[1])
    near[0] = by_owner(1, backr[2], backr[4], back[1])
    near[1] = by_owner(3, back[1], backr[5], backr[3])
    expand[pl.ds(0, 64, stride=2)] = values
    expand[pl.ds(1, 64, stride=2)] = values

    def correct_step(i, carry):
        four = expand[pl.ds(pl.multiple_of((i // 2) * 32, 32), 32)].reshape(4, 1, 8, LANES)
        xb[5, i + 1, 1:9] = x3[i + 1, 1:9] + jnp.broadcast_to(four, (4, 2, 8, LANES)).reshape(8, 8, LANES)
        return carry

    lax.fori_loop(0, 8, correct_step, 0, unroll=True)

    for f in range(6):
        k, side = f // 2, f % 2
        edge = 0 if side else 3
        if k == 0:
            part = near[side, 16 * edge:16 * edge + 16]
        elif k == 1:
            part = jnp.concatenate([near[side, 16 * i + 4 * edge:16 * i + 4 * edge + 4] for i in range(4)], axis=0)
        else:
            part = near[side, pl.ds(edge, 16, stride=4)]
        part = pick(part, fidx[f])
        expand2[f, pl.ds(0, 16, stride=2)] = part
        expand2[f, pl.ds(1, 16, stride=2)] = part
        four = expand2[f].reshape(4, 1, 8, LANES)
        far = get_ghost(x3, ghost, f) + jnp.broadcast_to(four, (4, 2, 8, LANES)).reshape(8, 8, LANES)
        own = pick_face(face(xb.at[5], f ^ 1), fidx[f])
        put_ghost(xb.at[5], ghost2, f, jnp.where(fmask[f][None] != 0, far, own))

    sweep(xb.at[5], ghost2, wt, bd, upd, xb.at[6], 0)
    two_sweeps(xb.at[6], ghost, xb.at[7], ghost3, xb.at[8], xb.at[11], 8)
    for c in range(4):
        block = xb[8, 2 * c + 1:2 * c + 3, 1:9].reshape(LANES, LANES).T
        out_ref[:, c * LANES:(c + 1) * LANES] = block

    for offset in (1, -1, 2, -2):
        @pl.when(valid[offset])
        def _():
            for o, made in sent:
                if o == offset:
                    for copy in made:
                        copy.wait_send()


def solution(mesh):
    gx, gy = mesh.shape["gx"], mesh.shape["gy"]
    f32, i32 = jnp.float32, jnp.int32

    def on_device(rhs, guess, coef, links, owner, ccoef, clinks):
        whole = pl.BlockSpec(memory_space=pltpu.VMEM)
        volume, padded = (8, 8, 8, LANES), (10, 10, 8, LANES)
        return pl.pallas_call(
            functools.partial(kernel, gx, gy),
            out_shape=(jax.ShapeDtypeStruct((FINE, 512), f32), jax.ShapeDtypeStruct((COARSE, 512), f32)),
            in_specs=[pl.BlockSpec(memory_space=pltpu.HBM)] * 7,
            out_specs=(whole, whole),
            scratch_shapes=[
                pltpu.VMEM((FINE, 512), f32),
                pltpu.VMEM((FINE, 512), f32),
                pltpu.VMEM((FINE, 512), f32),
                pltpu.VMEM((6, FINE), i32),
                pltpu.VMEM((1, FINE), i32),
                pltpu.VMEM((6, COARSE), i32),
                pltpu.VMEM((12,) + padded, f32),
                pltpu.VMEM((6,) + volume, f32),
                pltpu.VMEM(volume, f32),
                pltpu.VMEM(volume, f32),
                pltpu.VMEM(volume, f32),
                pltpu.VMEM((2, 8, 8, LANES), f32),
                pltpu.VMEM((10, 2, 8, 8, LANES), f32),
                pltpu.VMEM((10, 2, 3, 8, 8, LANES), f32),
                pltpu.VMEM((6, 8, LANES), i32),
                pltpu.VMEM((12, 8, LANES), i32),
                pltpu.VMEM((LANES, 512), f32),
                pltpu.VMEM((4,) + padded, f32),
                pltpu.VMEM((6,) + volume, f32),
                pltpu.VMEM(volume, f32),
                pltpu.VMEM(volume, f32),
                pltpu.VMEM(volume, f32),
                pltpu.VMEM((2, 8, 8, LANES), f32),
                pltpu.VMEM((LANES, 512), f32),
                pltpu.VMEM((8, 8, LANES), i32),
                pltpu.VMEM((4, 8, LANES), i32),
                pltpu.VMEM((6, 8, LANES), i32),
                pltpu.VMEM((2, 64, LANES), f32),
                pltpu.VMEM((2, 64, LANES), f32),
                pltpu.VMEM((12, 8, LANES), i32),
                pltpu.VMEM((5, 2, 8, LANES), i32),
                pltpu.VMEM((4, 64, LANES), f32),
                pltpu.VMEM((2, 32, LANES), f32),
                pltpu.VMEM((2, 32, LANES), f32),
                pltpu.VMEM((LANES, LANES), f32),
                pltpu.VMEM((2, 64, LANES), f32),
                pltpu.VMEM((6, 64, LANES), f32),
                pltpu.VMEM((LANES, LANES), f32),
                pltpu.VMEM((2, 64, LANES), f32),
                pltpu.VMEM((6, 32, LANES), f32),
                pltpu.VMEM((2, 8, 8, LANES), f32),
                pltpu.VMEM((2, 6, FINE), i32),
                pltpu.VMEM((2, 3, 8, LANES), i32),
                pltpu.VMEM((2, 3, 8, LANES), i32),
                pltpu.VMEM((6, 8, 8, LANES), f32),
                pltpu.VMEM((2, 3, 8, 8, LANES), f32),
                pltpu.VMEM((2, 2, 6, 8, LANES), f32),
                pltpu.VMEM((2, 2, 6, 8, LANES), f32),
                pltpu.VMEM((2, 3, 8, 8, LANES), f32),
                pltpu.VMEM((2, 8, 8, LANES), f32),
                pltpu.SemaphoreType.DMA((N_COPIES,)),
                pltpu.SemaphoreType.DMA((N_COPIES,)),
                pltpu.SemaphoreType.DMA((7,)),
            ],
            compiler_params=pltpu.CompilerParams(collective_id=0, has_side_effects=True, vmem_limit_bytes=56 * 1024 * 1024),
        )(rhs, guess, coef, links.T, owner.T, ccoef, clinks.T)

    rows = P(("gx", "gy"), None)
    return jax.shard_map(on_device, mesh=mesh, in_specs=(rows,) * 7, out_specs=(rows, rows), check_vma=False)
```

```python
import functools

import jax
import jax.numpy as jnp
from jax import lax
from jax.experimental import pallas as pl
from jax.experimental.pallas import tpu as pltpu
from jax.sharding import PartitionSpec as P

THETA = 1.25
DELTA = 0.75
SIGMA = THETA / DELTA
RHO0 = 1.0 / SIGMA
RHO1 = 1.0 / (2.0 * SIGMA - RHO0)
RHO2 = 1.0 / (2.0 * SIGMA - RHO1)
SWEEPS = ((0.0, 1.0 / THETA), (RHO1 * RHO0, 2.0 * RHO1 / DELTA), (RHO2 * RHO1, 2.0 * RHO2 / DELTA))

LANES = 128
FINE = 128
COARSE = 32
MESH = pl.DeviceIdType.MESH
N_COPIES = 96


def pick(values, index):
    rows = values.shape[0]
    whole = jnp.broadcast_to(index[None], (rows // 8, 8, LANES)).reshape(rows, LANES)
    return jnp.take_along_axis(values, whole, axis=1, mode="promise_in_bounds")


def pick_face(face, index):
    return pick(face.reshape(64, LANES), index).reshape(8, 8, LANES)


def kernel(
    gx, gy,
    rhs_hbm, guess_hbm, coef_hbm, links_hbm, owner_hbm, ccoef_hbm, clinks_hbm,
    out_ref, cout_ref,
    rhs_ref, guess_ref, coef_ref, links_ref, owner_ref, clinks_ref,
    xb, wt, bd, dg, upd, ghost, packed, recv, fidx, fmask,
    ccrow, cxb, cwt, cidg, cbd, cupd, cghost, idrow, tidx, tsrc, cidx, crec, cpack, cnidx,
    counts, src, pair2, pair2r, tall, back, backr, backp, backpr, expand, near, expand2, ghost2,
    nlinks, nidx, nmask, wface, flux, edges, erecv, beside, ghost3, local, psi, psir, halved,
    ssem, rsem, isem,
):
    devices = gx * gy
    me = lax.axis_index("gx") * gy + lax.axis_index("gy")
    valid = {1: me < devices - 1, -1: me > 0, 2: me < devices - 2, -2: me > 1, 3: me < devices - 3, -3: me > 2}

    def device(offset):
        target = lax.rem(me + offset + devices, devices)
        return (target // gy, lax.rem(target, gy))

    barrier = pltpu.get_barrier_semaphore()
    for offset in valid:
        @pl.when(valid[offset])
        def _():
            pl.semaphore_signal(barrier, inc=1, device_id=device(offset), device_id_type=MESH)

    fetches = []
    for at, (source, target) in enumerate((
            (coef_hbm, coef_ref), (guess_hbm, guess_ref), (owner_hbm, owner_ref), (links_hbm, links_ref),
            (ccoef_hbm, ccrow.at[COARSE:2 * COARSE]), (rhs_hbm, rhs_ref), (clinks_hbm, clinks_ref))):
        fetches.append(pltpu.make_async_copy(source, target, isem.at[at]))
        fetches[-1].start()

    used = [0]
    sent = []

    def send(offset, pairs):
        made = []
        for source, target in pairs:
            at = used[0]
            used[0] += 1
            made.append(pltpu.make_async_remote_copy(
                src_ref=source, dst_ref=target, send_sem=ssem.at[at], recv_sem=rsem.at[at],
                device_id=device(offset), device_id_type=MESH))

        @pl.when(valid[offset])
        def _():
            for copy in made:
                copy.start()

        sent.append((offset, made))
        return (offset, made)

    def arrived(handle, which=None):
        offset, made = handle

        @pl.when(valid[-offset])
        def _():
            for copy in (made if which is None else [made[which]]):
                copy.wait_recv()

    lane = lax.broadcasted_iota(jnp.int32, (8, LANES), 1)
    row = lax.broadcasted_iota(jnp.int32, (8, LANES), 0)
    row3 = lax.broadcasted_iota(jnp.int32, (8, 8, LANES), 1)
    first, last = row3 == 0, row3 == 7

    def load_cells(buffer, rows_ref):
        for c in range(4):
            block = rows_ref[:, c * LANES:(c + 1) * LANES].T
            buffer[2 * c + 1:2 * c + 3, 1:9] = block.reshape(2, 8, 8, LANES)

    def face(x, f):
        at = 1 if f % 2 == 0 else 8
        if f // 2 == 0:
            return x[at, 1:9]
        if f // 2 == 1:
            return x[1:9, at]
        return x[1:9, 1:9, 0 if f % 2 == 0 else 7]

    def put_ghost(x, g, f, value):
        at = 0 if f % 2 == 0 else 9
        if f // 2 == 0:
            x[at, 1:9] = value
        elif f // 2 == 1:
            x[1:9, at] = value
        else:
            g[f % 2] = value

    def get_ghost(x, g, f):
        at = 0 if f % 2 == 0 else 9
        if f // 2 == 0:
            return x[at, 1:9]
        if f // 2 == 1:
            return x[1:9, at]
        return g[f % 2]

    def neighbours(x, g, i):
        centre = x[i + 1, 1:9]
        low = jnp.where(first, g[0, i][:, None, :], pltpu.roll(centre, 1, 1))
        high = jnp.where(last, g[1, i][:, None, :], pltpu.roll(centre, 7, 1))
        return centre, (x[i, 1:9], x[i + 2, 1:9], x[i + 1, 0:8], x[i + 1, 2:10], low, high)

    def scaled_residual(x, g, w, b, i):
        centre, others = neighbours(x, g, i)
        total = b[i] - centre
        for f in range(6):
            total = total + w[f, i] * others[f]
        return centre, total

    def sweep(x, g, w, b, d, new, at, final=True):
        keep, gain = SWEEPS[at]

        def step(i, carry):
            centre, total = scaled_residual(x, g, w, b, i)
            update = gain * total
            if at > 0:
                update = update + keep * d[i]
            if final:
                d[i] = update
            new[i + 1, 1:9] = centre + update
            return carry

        lax.fori_loop(0, 8, step, 0, unroll=True)

    def start_faces(e, x):
        packed[e, 0] = face(x, 4)
        packed[e, 1] = face(x, 5)
        up = send(1, [(x.at[8, 1:9], recv.at[e, 0, 0]), (x.at[1:9, 8], recv.at[e, 0, 1]), (packed.at[e, 1], recv.at[e, 0, 2])])
        down = send(-1, [(x.at[1, 1:9], recv.at[e, 1, 0]), (x.at[1:9, 1], recv.at[e, 1, 1]), (packed.at[e, 0], recv.at[e, 1, 2])])
        return up, down

    def own_ghosts(x, g, keep_own=False, zero_far=False):
        for f in range(6):
            value = pick_face(face(x, f ^ 1), fidx[f])
            if keep_own:
                value = jnp.where(fmask[6 + f][None] != 0, value, face(x, f))
            if zero_far:
                value = jnp.where(fmask[f][None] != 0, 0.0, value)
            put_ghost(x, g, f, value)

    def far_ghosts(faces, x, g, handles=()):
        for handle in handles:
            arrived(handle)
        for k in range(3):
            for side in range(2):
                f = 2 * k + side
                value = pick_face(faces[side, k], fidx[f])
                put_ghost(x, g, f, jnp.where(fmask[f][None] != 0, value, get_ghost(x, g, f)))

    def across(k, m):
        return (m if m < k else m - 1)

    def line(k, m, at):
        return (at,) if across(k, m) == 0 else (slice(None), at)

    def two_sweeps(x, g, middle, g_middle, new, partial, e, between=None):
        keep, gain = SWEEPS[1]
        handles = start_faces(e, x)
        for side in range(2):
            for k in range(3):
                f = 2 * k + side
                value = pick_face(face(x, f) * wface[f], nidx[side, k])
                flux[side, k] = jnp.where(nmask[side, k][None] != 0, value, 0.0)
        at = 0
        for m in range(3):
            for k in range(3):
                if k != m:
                    for side in range(2):
                        edges[e // 7, side, at] = flux[(side, m) + line(m, k, 7 if side else 0)]
                    at += 1
        edge_handles = [send(2, [(edges.at[e // 7, 1], erecv.at[e // 7, 0])]), send(-2, [(edges.at[e // 7, 0], erecv.at[e // 7, 1])])]
        own_ghosts(x, g, zero_far=True)
        sweep(x, g, wt, bd, upd, partial, 1, final=False)
        partial_handles = start_faces(e + 1, partial)
        for side in range(2):
            end = 0 if side else 7
            for k in range(3):
                beside[side, k] = flux[side, k]
                for m in range(3):
                    if m != k:
                        where = (side, k) + line(k, m, end)
                        beside[where] = beside[where] + flux[(side, m) + line(m, k, end)]
        if between is not None:
            between()
        far_ghosts(recv.at[e], x, g, handles)
        sweep(x, g, wt, bd, upd, middle, 1)
        own_ghosts(middle, g_middle)
        for handle in edge_handles + list(partial_handles):
            arrived(handle)
        for side in range(2):
            end = 0 if side else 7
            at = 0
            for m in range(3):
                for k in range(3):
                    if k != m:
                        where = (side, k) + line(k, m, 7 - end)
                        behind = jnp.where(valid[2 if side else -2], erecv[e // 7, side, at], 0.0)
                        beside[where] = beside[where] + behind
                        at += 1
        for side in range(2):
            for k in range(3):
                beside[side, k] = recv[e + 1, side, k] + gain * recv[3, side, k] * beside[side, k]
        far_ghosts(beside, middle, g_middle)
        sweep(middle, g_middle, wt, bd, upd, new, 2)

    coef, x0 = xb.at[0], xb.at[1]
    fetches[0].wait()
    load_cells(coef, coef_ref)
    fetches[1].wait()
    load_cells(x0, guess_ref)
    for fetch in fetches[2:]:
        fetch.wait()

    owner = owner_ref[...]
    to_prev = jnp.sum((owner == me - 1).astype(jnp.float32), axis=1, keepdims=True).astype(jnp.int32)
    to_next = jnp.sum((owner == me + 1).astype(jnp.float32), axis=1, keepdims=True).astype(jnp.int32)
    counts[2, 0] = jnp.broadcast_to(to_prev, (8, LANES))
    counts[2, 1] = jnp.broadcast_to(to_next, (8, LANES))
    ccrow[3 * COARSE:] = jnp.ones((COARSE, 512), jnp.float32)

    pl.semaphore_wait(barrier, jnp.minimum(me, 3) + jnp.minimum(devices - 1 - me, 3))

    coef_handles = start_faces(0, coef)
    x0_handles = start_faces(1, x0)
    count_handles = [send(o, [(counts.at[2], counts.at[2 - o])]) for o in (1, -1, 2, -2)]
    link_handles = [send(1, [(links_ref, nlinks.at[0])]), send(-1, [(links_ref, nlinks.at[1])])]
    ccoef_handles = [send(1, [(ccrow.at[COARSE:2 * COARSE], ccrow.at[0:COARSE])]),
                     send(-1, [(ccrow.at[COARSE:2 * COARSE], ccrow.at[2 * COARSE:3 * COARSE])])]

    links = links_ref[...]
    for f in range(6):
        ids = jnp.broadcast_to(links[f:f + 1], (8, LANES))
        live = ids >= 0
        fidx[f] = jnp.bitwise_and(ids, FINE - 1)
        fmask[f] = jnp.where(live & (jnp.right_shift(ids, 7) != me), 1, 0)
        fmask[6 + f] = jnp.where(live, 1, 0)

    for c in range(4):
        dg[2 * c:2 * c + 2] = rhs_ref[:, c * LANES:(c + 1) * LANES].T.reshape(2, 8, 8, LANES)
    own_ghosts(coef, ghost, keep_own=True)
    far_ghosts(recv.at[0], coef, ghost, coef_handles)

    def weigh(x, g, w, lives, finish):
        mask4 = jnp.where((row == 0) & (lives[4] == 0), 0.0, 1.0)[None]
        mask5 = jnp.where((row == 7) & (lives[5] == 0), 0.0, 1.0)[None]

        def step(i, carry):
            centre, others = neighbours(x, g, i)
            weights = [0.5 * (centre + other) for other in others]
            diag = weights[0]
            for weight in weights[1:]:
                diag = diag + weight
            inverse = 1.0 / diag
            for f in range(6):
                value = weights[f] * inverse
                if f == 4:
                    value = value * mask4
                if f == 5:
                    value = value * mask5
                w[f, i] = value
            finish(i, diag, inverse)
            return carry

        lax.fori_loop(0, 8, step, 0, unroll=True)
        w[0, 0] = jnp.where(lives[0][None] != 0, w[0, 0], 0.0)
        w[1, 7] = jnp.where(lives[1][None] != 0, w[1, 7], 0.0)
        w[2, :, 0] = jnp.where(lives[2][None] != 0, w[2, :, 0], 0.0)
        w[3, :, 7] = jnp.where(lives[3][None] != 0, w[3, :, 7], 0.0)

    def fine_finish(i, diag, inverse):
        bd[i] = dg[i] * inverse
        dg[i] = diag
        xb[9, i + 1, 1:9] = inverse

    weigh(coef, ghost, wt, [fmask[6 + f] for f in range(6)], fine_finish)

    inverse_handles = start_faces(3, xb.at[9])
    own_ghosts(x0, ghost)
    far_ghosts(recv.at[1], x0, ghost, x0_handles)
    sweep(x0, ghost, wt, bd, upd, xb.at[2], 0)
    for handle in link_handles:
        arrived(handle)
    for side in range(2):
        for k in range(3):
            f = 2 * k + side
            cut = (0 if side == 0 else 7,)
            cut = (slice(None),) * k + cut
            wface[f] = wt[(f,) + cut] * dg[cut]
            ids = jnp.broadcast_to(nlinks[side, 2 * k + 1 - side:2 * k + 2 - side], (8, LANES))
            nidx[side, k] = jnp.bitwise_and(ids, FINE - 1)
            linked = (ids >= 0) & (jnp.right_shift(ids, 7) == me) & valid[1 if side else -1]
            nmask[side, k] = jnp.where(linked, 1, 0)

    own_lane = (jnp.right_shift(lane, 5) == 1)
    group = jnp.right_shift(lane, 5)
    slot = jnp.bitwise_and(lane, COARSE - 1)
    coarse_handles = []

    def coarse_setup_a():
        for handle in ccoef_handles + count_handles:
            arrived(handle)
        load_cells(cxb.at[0], ccrow)
        zeros = jnp.zeros((6, COARSE), jnp.int32)
        links_c = jnp.concatenate([zeros, clinks_ref[...], zeros, zeros], axis=1)
        lives = []
        x = cxb.at[0]
        for f in range(6):
            ids = jnp.broadcast_to(links_c[f:f + 1], (8, LANES))
            live = ids >= 0
            step_by = jnp.right_shift(ids, 5) - me
            place = jnp.bitwise_and((step_by + 1) * COARSE + jnp.bitwise_and(ids, COARSE - 1), LANES - 1)
            place = jnp.where(own_lane & live, place, lane)
            cidx[f] = place
            cnidx[f] = jnp.bitwise_and(ids, COARSE - 1) + (f // 2) * COARSE
            cnidx[6 + f] = jnp.where(own_lane & live & (step_by != 0), 1, 0)
            lives.append(jnp.where(live, 1, 0))
            value = jnp.where(live[None], pick_face(face(x, f ^ 1), place), face(x, f))
            put_ghost(x, cghost, f, value)

        def finish(i, diag, inverse):
            cidg[i] = inverse

        weigh(x, cghost, cwt, lives, finish)
        for c in range(4):
            block = cidg[2 * c:2 * c + 2].reshape(LANES, LANES).T
            idrow[COARSE:2 * COARSE, c * LANES:(c + 1) * LANES] = block[COARSE:2 * COARSE]
        coarse_handles.append(send(1, [(idrow.at[COARSE:2 * COARSE], idrow.at[0:COARSE])]))
        coarse_handles.append(send(-1, [(idrow.at[COARSE:2 * COARSE], idrow.at[2 * COARSE:3 * COARSE])]))

    def known(k, which):
        return counts[k, which] if k == 2 else jnp.where(valid[k - 2], counts[k, which], 0)

    def by_group(values):
        return jnp.where(group == 0, values[0], jnp.where(group == 1, values[1], values[2]))

    def coarse_setup_b():
        a = [known(k, 0) for k in range(5)]
        n = [known(k, 1) for k in range(5)]
        stay = [FINE - a[k] - n[k] if k == 2 else jnp.where(valid[k - 2], FINE - a[k] - n[k], 0) for k in range(5)]
        before, here = by_group(n[0:3]), by_group(stay[1:4])
        start, after = by_group(a[1:4]), by_group(a[2:5])
        for o in range(4):
            rank = 8 * slot + 2 * o + jnp.where(row >= 4, 1, 0)
            in_before = rank < before
            in_here = rank < before + here
            in_after = rank < before + here + after
            at = jnp.where(in_before, FINE - before + rank, jnp.where(in_here, start + rank - before, rank - before - here))
            step_by = jnp.where(in_before, group - 2, jnp.where(in_here, group - 1, group))
            source = jnp.where((step_by == 2) | (step_by == -2), 0, step_by + 2)
            tidx[o] = jnp.bitwise_and(at, LANES - 1)
            tsrc[o] = jnp.where(in_after & (group < 3), source, 4)
        rank_own = n[1] + lane - a[2]
        rank_far = jnp.where(lane < 64, n[1] + stay[2] + lane, lane - FINE + n[1])
        for k, rank in enumerate((rank_own, rank_far)):
            rank = jnp.bitwise_and(rank, 255)
            tidx[4 + 2 * k] = COARSE + jnp.right_shift(rank, 3)
            tidx[5 + 2 * k] = jnp.bitwise_and(rank, 7)

    def coarse_setup_c():
        for handle in coarse_handles:
            arrived(handle)
        for c in range(4):
            block = idrow[:, c * LANES:(c + 1) * LANES].T
            cidg[2 * c:2 * c + 2] = block.reshape(2, 8, 8, LANES)

    def setup_first():
        for handle in inverse_handles:
            arrived(handle)
        coarse_setup_a()
        coarse_setup_b()

    two_sweeps(xb.at[2], ghost, xb.at[3], ghost3, xb.at[4], xb.at[10], 6, setup_first)
    x3 = xb.at[4]
    psi[...] = jnp.zeros((2, 64, LANES), jnp.float32)
    for side in range(2):
        edge = 0 if side else 3
        for k in range(3):
            f = 2 * k + side
            pairs = (face(x3, f) * wface[f]).reshape(4, 2, 8, LANES)
            pairs = pairs[:, 0] + pairs[:, 1]
            pairs = 0.5 * (pairs + pltpu.roll(pairs, 7, 1))
            halved[f] = pairs.reshape(32, LANES)
            part = pick(halved[f, pl.ds(0, 16, stride=2)], nidx[side, k])
            mask = jnp.broadcast_to(nmask[side, k][None], (2, 8, LANES)).reshape(16, LANES)
            part = jnp.where(mask != 0, part, 0.0)
            if k == 0:
                psi[side, 16 * edge:16 * edge + 16] = part
            elif k == 1:
                for i in range(4):
                    at = 16 * i + 4 * edge
                    psi[side, at:at + 4] = psi[side, at:at + 4] + part[4 * i:4 * i + 4]
            else:
                psi[side, pl.ds(edge, 16, stride=4)] = psi[side, pl.ds(edge, 16, stride=4)] + part
    low_lane = jnp.broadcast_to((lane < 64)[None], (4, 8, LANES)).reshape(32, LANES)

    def pack(values, keep_low):
        turned = pltpu.roll(values[32:], 64, 1)
        return jnp.where(low_lane, values[:32], turned) if keep_low else jnp.where(low_lane, turned, values[:32])

    for at, (side, distance) in enumerate(((0, 1), (1, -1), (1, 3), (0, -3))):
        pair2[2 + at] = pack(psi[side], distance < 0)
    r_handles = [send(3, [(pair2.at[4], pair2r.at[4])]), send(-3, [(pair2.at[5], pair2r.at[5])]),
                 send(2, [(psi.at[1], psir.at[2])]), send(-2, [(psi.at[0], psir.at[3])]),
                 send(1, [(psi.at[1], psir.at[0]), (pair2.at[2], pair2r.at[2])]),
                 send(-1, [(psi.at[0], psir.at[1]), (pair2.at[3], pair2r.at[3])])]

    own_ghosts(xb.at[4], ghost, zero_far=True)


    def restrict_step(i, carry):
        total = jnp.zeros((4, 8, LANES), jnp.float32)
        for half in range(2):
            _, scaled = scaled_residual(x3, ghost, wt, bd, 2 * i + half)
            quads = (scaled * dg[2 * i + half]).reshape(4, 2, 8, LANES)
            total = total + quads[:, 0] + quads[:, 1]
        total = total + pltpu.roll(total, 7, 1)
        tall[pl.ds(pl.multiple_of(i * 32, 32), 32)] = 0.5 * total.reshape(32, LANES)
        return carry

    lax.fori_loop(0, 4, restrict_step, 0, unroll=True)
    restricted = tall[pl.ds(0, 64, stride=2)]
    local[...] = restricted
    pair2[0] = pack(restricted, False)
    pair2[1] = pack(restricted, True)
    r_handles += [send(2, [(pair2.at[0], pair2r.at[0])]), send(-2, [(pair2.at[1], pair2r.at[1])]),
                  send(1, [(local, src.at[1])]), send(-1, [(local, src.at[3])])]
    x3_handles = start_faces(4, x3)
    coarse_setup_c()
    for handle in r_handles:
        arrived(handle)
    src[1] = src[1] + psi[0] + jnp.where(valid[-2], psir[2], 0.0)
    src[3] = src[3] + psi[1] + jnp.where(valid[2], psir[3], 0.0)
    src[2] = local[...] + jnp.where(valid[-1], psir[0], 0.0) + jnp.where(valid[1], psir[1], 0.0)
    high = pair2r[0] + pair2r[2] + jnp.where(valid[-3], pair2r[4], 0.0)
    low = pair2r[1] + pair2r[3] + jnp.where(valid[3], pair2r[5], 0.0)
    src[0, 0:32] = jnp.where(low_lane, low, high)
    src[0, 32:64] = pltpu.roll(jnp.where(low_lane, high, low), 64, 1)

    for o in range(4):
        ox, oy = o // 2, o % 2
        index, which = tidx[o], tsrc[o]
        for i in range(4):
            for j in range(4):
                q = 4 * (4 * i + j)
                value = jnp.zeros((8, LANES), jnp.float32)
                for k in range(4):
                    four = src[k, q:q + 4]
                    taken = pick(jnp.concatenate([four, four], axis=0), index)
                    value = jnp.where(which == k, taken, value)
                at = (4 * ox + i, 4 * oy + j)
                scaled = value * cidg[at[0], at[1]]
                cbd[at[0], at[1]] = scaled
                update = scaled * (1.0 / THETA)
                cupd[at[0], at[1]] = update
                cxb[1, at[0] + 1, at[1] + 1] = update

    c1, c2, c3 = cxb.at[1], cxb.at[2], cxb.at[3]
    for f in range(6):
        put_ghost(c1, cghost, f, pick_face(face(c1, f ^ 1), cidx[f]))
    sweep(c1, cghost, cwt, cbd, cupd, c2, 1)

    lane64 = jnp.broadcast_to(lane[None], (8, 8, LANES)).reshape(64, LANES)
    for side in range(2):
        faces = [face(c2, 2 * k + side).reshape(64, LANES) for k in range(3)]
        cpack[side] = jnp.where(lane64 < 32, pltpu.roll(faces[0], 96, 1), jnp.where(lane64 < 64, faces[1], pltpu.roll(faces[2], 32, 1)))
    c_handles = [send(1, [(cpack.at[1], crec.at[0])]), send(-1, [(cpack.at[0], crec.at[1])])]
    for f in range(6):
        put_ghost(c2, cghost, f, pick_face(face(c2, f ^ 1), cidx[f]))
    far_ghosts(recv.at[4], x3, ghost, x3_handles)
    for side in range(2):
        arrived(c_handles[side])
    for side in range(2):
        for k in range(3):
            f = 2 * k + side
            value = pick(crec[side], cnidx[f]).reshape(8, 8, LANES)
            put_ghost(c2, cghost, f, jnp.where(cnidx[6 + f][None] != 0, value, get_ghost(c2, cghost, f)))
    sweep(c2, cghost, cwt, cbd, cupd, c3, 2)

    for k in (1, 0):
        place, octant = tidx[4 + 2 * k], tidx[5 + 2 * k]
        straight = (jnp.bitwise_and(octant, 1) == 0) == (row < 4)
        outer = jnp.right_shift(octant, 1)
        for i in range(4):
            quads = []
            for j in range(4):
                value = pick(c3[i + 1, j + 1], place)
                for o in range(1, 4):
                    value = jnp.where(outer == o, pick(c3[4 * (o // 2) + i + 1, 4 * (o % 2) + j + 1], place), value)
                quads.append(jnp.where(straight, value, pltpu.roll(value, 4, 0)))
            for half in range(2):
                at = 16 * i + 8 * half
                back[k, at:at + 8] = jnp.where(row < 4, quads[2 * half], quads[2 * half + 1])
        if k == 1:
            backp[0] = pack(back[1], True)
            backp[1] = pack(back[1], False)
            b_handles = [send(2, [(backp.at[0], backpr.at[2])]), send(-2, [(backp.at[1], backpr.at[3])]),
                         send(1, [(backp.at[0], backpr.at[0])]), send(-1, [(backp.at[1], backpr.at[1])])]
        else:
            b_handles += [send(1, [(back.at[0], backr.at[0])]), send(-1, [(back.at[0], backr.at[1])])]
    for c in range(4):
        block = c3[2 * c + 1:2 * c + 3, 1:9].reshape(LANES, LANES).T
        cout_ref[:, c * LANES:(c + 1) * LANES] = block[COARSE:2 * COARSE]
    for handle in b_handles:
        arrived(handle)

    def by_owner(at, before, here, after):
        low = jnp.where(lane < known(at, 0), 1, 0)
        high = jnp.where(lane >= FINE - known(at, 1), 1, 0)
        low = jnp.broadcast_to(low[None], (8, 8, LANES)).reshape(64, LANES)
        high = jnp.broadcast_to(high[None], (8, 8, LANES)).reshape(64, LANES)
        return jnp.where(low != 0, before, jnp.where(high != 0, after, here))

    first_half, last_half = [
        jnp.concatenate([backpr[at], pltpu.roll(backpr[at], 64, 1)], axis=0) for at in (0, 2)], [
        jnp.concatenate([backpr[at], pltpu.roll(backpr[at], 64, 1)], axis=0) for at in (1, 3)]
    values = by_owner(2, first_half[0], back[0], last_half[0])
    near[0] = by_owner(1, first_half[1], backr[0], back[1])
    near[1] = by_owner(3, back[1], backr[1], last_half[1])
    expand[pl.ds(0, 64, stride=2)] = values
    expand[pl.ds(1, 64, stride=2)] = values

    def correct_step(i, carry):
        four = expand[pl.ds(pl.multiple_of((i // 2) * 32, 32), 32)].reshape(4, 1, 8, LANES)
        xb[5, i + 1, 1:9] = x3[i + 1, 1:9] + jnp.broadcast_to(four, (4, 2, 8, LANES)).reshape(8, 8, LANES)
        return carry

    lax.fori_loop(0, 8, correct_step, 0, unroll=True)

    for f in range(6):
        k, side = f // 2, f % 2
        edge = 0 if side else 3
        if k == 0:
            part = near[side, 16 * edge:16 * edge + 16]
        elif k == 1:
            part = jnp.concatenate([near[side, 16 * i + 4 * edge:16 * i + 4 * edge + 4] for i in range(4)], axis=0)
        else:
            part = near[side, pl.ds(edge, 16, stride=4)]
        part = pick(part, fidx[f])
        expand2[f, pl.ds(0, 16, stride=2)] = part
        expand2[f, pl.ds(1, 16, stride=2)] = part
        four = expand2[f].reshape(4, 1, 8, LANES)
        far = get_ghost(x3, ghost, f) + jnp.broadcast_to(four, (4, 2, 8, LANES)).reshape(8, 8, LANES)
        own = pick_face(face(xb.at[5], f ^ 1), fidx[f])
        put_ghost(xb.at[5], ghost2, f, jnp.where(fmask[f][None] != 0, far, own))

    sweep(xb.at[5], ghost2, wt, bd, upd, xb.at[6], 0)
    two_sweeps(xb.at[6], ghost, xb.at[7], ghost3, xb.at[8], xb.at[11], 8)
    for c in range(4):
        block = xb[8, 2 * c + 1:2 * c + 3, 1:9].reshape(LANES, LANES).T
        out_ref[:, c * LANES:(c + 1) * LANES] = block

    for offset in valid:
        @pl.when(valid[offset])
        def _():
            for o, made in sent:
                if o == offset:
                    for copy in made:
                        copy.wait_send()


def deliver(fine_ref, coarse_ref, fine_out, coarse_out, fine, coarse, in_sem, out_sem):
    parts = [(fine_ref.at[32 * c:32 * c + 32], fine.at[32 * c:32 * c + 32], fine_out.at[32 * c:32 * c + 32]) for c in range(4)]
    parts.append((coarse_ref, coarse, coarse_out))
    fetches = [pltpu.make_async_copy(source, middle, in_sem.at[at]) for at, (source, middle, _) in enumerate(parts)]
    stores = [pltpu.make_async_copy(middle, target, out_sem.at[at]) for at, (_, middle, target) in enumerate(parts)]
    for fetch in fetches:
        fetch.start()
    for fetch, store in zip(fetches, stores):
        fetch.wait()
        store.start()
    for store in stores:
        store.wait()


def solution(mesh):
    gx, gy = mesh.shape["gx"], mesh.shape["gy"]
    f32, i32 = jnp.float32, jnp.int32

    def on_device(rhs, guess, coef, links, owner, ccoef, clinks):
        whole = pl.BlockSpec(memory_space=pltpu.VMEM)
        volume, padded = (8, 8, 8, LANES), (10, 10, 8, LANES)
        results = pl.pallas_call(
            functools.partial(kernel, gx, gy),
            out_shape=(jax.ShapeDtypeStruct((FINE, 512), f32), jax.ShapeDtypeStruct((COARSE, 512), f32)),
            in_specs=[pl.BlockSpec(memory_space=pltpu.HBM)] * 7,
            out_specs=(whole, whole),
            scratch_shapes=[
                pltpu.VMEM((FINE, 512), f32),
                pltpu.VMEM((FINE, 512), f32),
                pltpu.VMEM((FINE, 512), f32),
                pltpu.VMEM((6, FINE), i32),
                pltpu.VMEM((1, FINE), i32),
                pltpu.VMEM((6, COARSE), i32),
                pltpu.VMEM((12,) + padded, f32),
                pltpu.VMEM((6,) + volume, f32),
                pltpu.VMEM(volume, f32),
                pltpu.VMEM(volume, f32),
                pltpu.VMEM(volume, f32),
                pltpu.VMEM((2, 8, 8, LANES), f32),
                pltpu.VMEM((10, 2, 8, 8, LANES), f32),
                pltpu.VMEM((10, 2, 3, 8, 8, LANES), f32),
                pltpu.VMEM((6, 8, LANES), i32),
                pltpu.VMEM((12, 8, LANES), i32),
                pltpu.VMEM((LANES, 512), f32),
                pltpu.VMEM((4,) + padded, f32),
                pltpu.VMEM((6,) + volume, f32),
                pltpu.VMEM(volume, f32),
                pltpu.VMEM(volume, f32),
                pltpu.VMEM(volume, f32),
                pltpu.VMEM((2, 8, 8, LANES), f32),
                pltpu.VMEM((LANES, 512), f32),
                pltpu.VMEM((8, 8, LANES), i32),
                pltpu.VMEM((4, 8, LANES), i32),
                pltpu.VMEM((6, 8, LANES), i32),
                pltpu.VMEM((2, 64, LANES), f32),
                pltpu.VMEM((2, 64, LANES), f32),
                pltpu.VMEM((12, 8, LANES), i32),
                pltpu.VMEM((5, 2, 8, LANES), i32),
                pltpu.VMEM((4, 64, LANES), f32),
                pltpu.VMEM((6, 32, LANES), f32),
                pltpu.VMEM((6, 32, LANES), f32),
                pltpu.VMEM((LANES, LANES), f32),
                pltpu.VMEM((2, 64, LANES), f32),
                pltpu.VMEM((2, 64, LANES), f32),
                pltpu.VMEM((2, 32, LANES), f32),
                pltpu.VMEM((4, 32, LANES), f32),
                pltpu.VMEM((LANES, LANES), f32),
                pltpu.VMEM((2, 64, LANES), f32),
                pltpu.VMEM((6, 32, LANES), f32),
                pltpu.VMEM((2, 8, 8, LANES), f32),
                pltpu.VMEM((2, 6, FINE), i32),
                pltpu.VMEM((2, 3, 8, LANES), i32),
                pltpu.VMEM((2, 3, 8, LANES), i32),
                pltpu.VMEM((6, 8, 8, LANES), f32),
                pltpu.VMEM((2, 3, 8, 8, LANES), f32),
                pltpu.VMEM((2, 2, 6, 8, LANES), f32),
                pltpu.VMEM((2, 2, 6, 8, LANES), f32),
                pltpu.VMEM((2, 3, 8, 8, LANES), f32),
                pltpu.VMEM((2, 8, 8, LANES), f32),
                pltpu.VMEM((64, LANES), f32),
                pltpu.VMEM((2, 64, LANES), f32),
                pltpu.VMEM((4, 64, LANES), f32),
                pltpu.VMEM((6, 32, LANES), f32),
                pltpu.SemaphoreType.DMA((N_COPIES,)),
                pltpu.SemaphoreType.DMA((N_COPIES,)),
                pltpu.SemaphoreType.DMA((7,)),
            ],
            compiler_params=pltpu.CompilerParams(collective_id=0, has_side_effects=True, vmem_limit_bytes=56 * 1024 * 1024),
        )(rhs, guess, coef, links.T, owner.T, ccoef, clinks.T)
        hbm = pl.BlockSpec(memory_space=pltpu.HBM)
        return pl.pallas_call(
            deliver,
            out_shape=(jax.ShapeDtypeStruct((FINE, 512), f32), jax.ShapeDtypeStruct((COARSE, 512), f32)),
            in_specs=[hbm, hbm],
            out_specs=(hbm, hbm),
            scratch_shapes=[pltpu.VMEM((FINE, 512), f32), pltpu.VMEM((COARSE, 512), f32),
                            pltpu.SemaphoreType.DMA((5,)), pltpu.SemaphoreType.DMA((5,))],
        )(*results)

    rows = P(("gx", "gy"), None)
    return jax.shard_map(on_device, mesh=mesh, in_specs=(rows,) * 7, out_specs=(rows, rows), check_vma=False)
```

```python
import functools

import jax
import jax.numpy as jnp
from jax import lax
from jax.experimental import pallas as pl
from jax.experimental.pallas import tpu as pltpu
from jax.sharding import PartitionSpec as P

THETA = 1.25
DELTA = 0.75
SIGMA = THETA / DELTA
RHO0 = 1.0 / SIGMA
RHO1 = 1.0 / (2.0 * SIGMA - RHO0)
RHO2 = 1.0 / (2.0 * SIGMA - RHO1)
SWEEPS = ((0.0, 1.0 / THETA), (RHO1 * RHO0, 2.0 * RHO1 / DELTA), (RHO2 * RHO1, 2.0 * RHO2 / DELTA))

LANES = 128
FINE = 128
COARSE = 32
MESH = pl.DeviceIdType.MESH
N_COPIES = 104


def pick(values, index):
    rows = values.shape[0]
    whole = jnp.broadcast_to(index[None], (rows // 8, 8, LANES)).reshape(rows, LANES)
    return jnp.take_along_axis(values, whole, axis=1, mode="promise_in_bounds")


def pick_face(face, index):
    return pick(face.reshape(64, LANES), index).reshape(8, 8, LANES)


def kernel(
    gx, gy,
    rhs_hbm, guess_hbm, coef_hbm, links_hbm, owner_hbm, ccoef_hbm, clinks_hbm,
    out_ref, cout_ref,
    rhs_ref, guess_ref, coef_ref, links_ref, owner_ref, clinks_ref,
    xb, wt, bd, dg, upd, ghost, packed, recv, fidx, fmask,
    ccrow, cxb, cwt, cidg, cbd, cupd, cghost, idrow, tidx, tsrc, cidx, clb, ccrow2, idrow2, cidg2,
    counts, src, pair2, pair2r, tall, back, backr, backp, backpr, expand, near, expand2, ghost2,
    nlinks, nidx, nmask, wface, flux, edges, erecv, beside, ghost3, local, psi, psir, halved, eb, ebr, eh, ehr,
    ssem, rsem, isem,
):
    devices = gx * gy
    me = lax.axis_index("gx") * gy + lax.axis_index("gy")
    valid = {1: me < devices - 1, -1: me > 0, 2: me < devices - 2, -2: me > 1, 3: me < devices - 3, -3: me > 2,
             4: me < devices - 4, -4: me > 3}

    def device(offset):
        target = lax.rem(me + offset + devices, devices)
        return (target // gy, lax.rem(target, gy))

    barrier = pltpu.get_barrier_semaphore()
    for offset in (1, -1):
        @pl.when(valid[offset])
        def _():
            pl.semaphore_signal(barrier, inc=1, device_id=device(offset), device_id_type=MESH)

    fetches = []
    for at, (source, target) in enumerate((
            (coef_hbm, coef_ref), (guess_hbm, guess_ref), (owner_hbm, owner_ref), (links_hbm, links_ref),
            (ccoef_hbm, ccrow.at[COARSE:2 * COARSE]), (rhs_hbm, rhs_ref), (clinks_hbm, clinks_ref))):
        fetches.append(pltpu.make_async_copy(source, target, isem.at[at]))
        fetches[-1].start()

    used = [0]
    sent = []

    def send(offset, pairs):
        made = []
        for source, target in pairs:
            at = used[0]
            used[0] += 1
            made.append(pltpu.make_async_remote_copy(
                src_ref=source, dst_ref=target, send_sem=ssem.at[at], recv_sem=rsem.at[at],
                device_id=device(offset), device_id_type=MESH))

        @pl.when(valid[offset])
        def _():
            for copy in made:
                copy.start()

        sent.append((offset, made))
        return (offset, made)

    def arrived(handles):
        for offset in valid:
            made = [copy for to, copies in handles if to == offset for copy in copies]
            if made:
                @pl.when(valid[-offset])
                def _():
                    for copy in made:
                        copy.wait_recv()

    lane = lax.broadcasted_iota(jnp.int32, (8, LANES), 1)
    row = lax.broadcasted_iota(jnp.int32, (8, LANES), 0)
    row3 = lax.broadcasted_iota(jnp.int32, (8, 8, LANES), 1)
    first, last = row3 == 0, row3 == 7

    def load_cells(buffer, rows_ref):
        for c in range(4):
            block = rows_ref[:, c * LANES:(c + 1) * LANES].T
            buffer[2 * c + 1:2 * c + 3, 1:9] = block.reshape(2, 8, 8, LANES)

    def face(x, f):
        at = 1 if f % 2 == 0 else 8
        if f // 2 == 0:
            return x[at, 1:9]
        if f // 2 == 1:
            return x[1:9, at]
        return x[1:9, 1:9, 0 if f % 2 == 0 else 7]

    def put_ghost(x, g, f, value):
        at = 0 if f % 2 == 0 else 9
        if f // 2 == 0:
            x[at, 1:9] = value
        elif f // 2 == 1:
            x[1:9, at] = value
        else:
            g[f % 2] = value

    def get_ghost(x, g, f):
        at = 0 if f % 2 == 0 else 9
        if f // 2 == 0:
            return x[at, 1:9]
        if f // 2 == 1:
            return x[1:9, at]
        return g[f % 2]

    def neighbours(x, g, i):
        centre = x[i + 1, 1:9]
        low = jnp.where(first, g[0, i][:, None, :], pltpu.roll(centre, 1, 1))
        high = jnp.where(last, g[1, i][:, None, :], pltpu.roll(centre, 7, 1))
        return centre, (x[i, 1:9], x[i + 2, 1:9], x[i + 1, 0:8], x[i + 1, 2:10], low, high)

    def scaled_residual(x, g, w, b, i):
        centre, others = neighbours(x, g, i)
        total = b[i] - centre
        for f in range(6):
            total = total + w[f, i] * others[f]
        return centre, total

    def sweep(x, g, w, b, d, new, at, final=True):
        keep, gain = SWEEPS[at]

        def step(i, carry):
            centre, total = scaled_residual(x, g, w, b, i)
            update = gain * total
            if at > 0:
                update = update + keep * d[i]
            if final:
                d[i] = update
            new[i + 1, 1:9] = centre + update
            return carry

        lax.fori_loop(0, 8, step, 0, unroll=True)

    def start_faces(e, x):
        packed[e, 0] = face(x, 4)
        packed[e, 1] = face(x, 5)
        up = send(1, [(x.at[8, 1:9], recv.at[e, 0, 0]), (x.at[1:9, 8], recv.at[e, 0, 1]), (packed.at[e, 1], recv.at[e, 0, 2])])
        down = send(-1, [(x.at[1, 1:9], recv.at[e, 1, 0]), (x.at[1:9, 1], recv.at[e, 1, 1]), (packed.at[e, 0], recv.at[e, 1, 2])])
        return up, down

    def own_ghosts(x, g, keep_own=False, zero_far=False):
        for f in range(6):
            value = pick_face(face(x, f ^ 1), fidx[f])
            if keep_own:
                value = jnp.where(fmask[6 + f][None] != 0, value, face(x, f))
            if zero_far:
                value = jnp.where(fmask[f][None] != 0, 0.0, value)
            put_ghost(x, g, f, value)

    def far_ghosts(faces, x, g, handles=()):
        arrived(handles)
        for k in range(3):
            for side in range(2):
                f = 2 * k + side
                value = pick_face(faces[side, k], fidx[f])
                put_ghost(x, g, f, jnp.where(fmask[f][None] != 0, value, get_ghost(x, g, f)))

    def across(k, m):
        return (m if m < k else m - 1)

    def line(k, m, at):
        return (at,) if across(k, m) == 0 else (slice(None), at)

    def two_sweeps(x, g, middle, g_middle, new, partial, e, between=None):
        keep, gain = SWEEPS[1]
        handles = start_faces(e, x)
        for side in range(2):
            for k in range(3):
                f = 2 * k + side
                value = pick_face(face(x, f) * wface[f], nidx[side, k])
                flux[side, k] = jnp.where(nmask[side, k][None] != 0, value, 0.0)
        at = 0
        for m in range(3):
            for k in range(3):
                if k != m:
                    for side in range(2):
                        edges[e // 7, side, at] = flux[(side, m) + line(m, k, 7 if side else 0)]
                    at += 1
        edge_handles = [send(2, [(edges.at[e // 7, 1], erecv.at[e // 7, 0])]), send(-2, [(edges.at[e // 7, 0], erecv.at[e // 7, 1])])]
        own_ghosts(x, g, zero_far=True)
        sweep(x, g, wt, bd, upd, partial, 1, final=False)
        partial_handles = start_faces(e + 1, partial)
        for side in range(2):
            end = 0 if side else 7
            for k in range(3):
                beside[side, k] = flux[side, k]
                for m in range(3):
                    if m != k:
                        where = (side, k) + line(k, m, end)
                        beside[where] = beside[where] + flux[(side, m) + line(m, k, end)]
        if between is not None:
            between()
        far_ghosts(recv.at[e], x, g, handles)
        sweep(x, g, wt, bd, upd, middle, 1)
        own_ghosts(middle, g_middle)
        arrived(edge_handles + list(partial_handles))
        for side in range(2):
            end = 0 if side else 7
            at = 0
            for m in range(3):
                for k in range(3):
                    if k != m:
                        where = (side, k) + line(k, m, 7 - end)
                        behind = jnp.where(valid[2 if side else -2], erecv[e // 7, side, at], 0.0)
                        beside[where] = beside[where] + behind
                        at += 1
        for side in range(2):
            for k in range(3):
                beside[side, k] = recv[e + 1, side, k] + gain * recv[3, side, k] * beside[side, k]
        far_ghosts(beside, middle, g_middle)
        sweep(middle, g_middle, wt, bd, upd, new, 2)

    coef, x0 = xb.at[0], xb.at[1]
    fetches[0].wait()
    load_cells(coef, coef_ref)
    fetches[1].wait()
    load_cells(x0, guess_ref)
    for fetch in fetches[2:]:
        fetch.wait()

    owner = owner_ref[...]
    to_prev = jnp.sum((owner == me - 1).astype(jnp.float32), axis=1, keepdims=True).astype(jnp.int32)
    to_next = jnp.sum((owner == me + 1).astype(jnp.float32), axis=1, keepdims=True).astype(jnp.int32)
    counts[3, 0] = jnp.broadcast_to(to_prev, (8, LANES))
    counts[3, 1] = jnp.broadcast_to(to_next, (8, LANES))

    pl.semaphore_wait(barrier, jnp.minimum(me, 1) + jnp.minimum(devices - 1 - me, 1))

    coef_handles = start_faces(0, coef)
    x0_handles = start_faces(1, x0)
    count_handles = [send(o, [(counts.at[3], counts.at[3 - o])]) for o in (1, -1)]
    link_handles = [send(1, [(links_ref, nlinks.at[0]), (clinks_ref, clb.at[0])]),
                    send(-1, [(links_ref, nlinks.at[1]), (clinks_ref, clb.at[1])])]
    ccoef_handles = [send(1, [(ccrow.at[COARSE:2 * COARSE], ccrow.at[0:COARSE])]),
                     send(-1, [(ccrow.at[COARSE:2 * COARSE], ccrow.at[2 * COARSE:3 * COARSE])])]

    links = links_ref[...]
    for f in range(6):
        ids = jnp.broadcast_to(links[f:f + 1], (8, LANES))
        live = ids >= 0
        fidx[f] = jnp.bitwise_and(ids, FINE - 1)
        fmask[f] = jnp.where(live & (jnp.right_shift(ids, 7) != me), 1, 0)
        fmask[6 + f] = jnp.where(live, 1, 0)

    for c in range(4):
        dg[2 * c:2 * c + 2] = rhs_ref[:, c * LANES:(c + 1) * LANES].T.reshape(2, 8, 8, LANES)
    own_ghosts(coef, ghost, keep_own=True)
    far_ghosts(recv.at[0], coef, ghost, coef_handles)

    def weigh(x, g, w, lives, finish):
        mask4 = jnp.where((row == 0) & (lives[4] == 0), 0.0, 1.0)[None]
        mask5 = jnp.where((row == 7) & (lives[5] == 0), 0.0, 1.0)[None]

        def step(i, carry):
            centre, others = neighbours(x, g, i)
            weights = [0.5 * (centre + other) for other in others]
            diag = weights[0]
            for weight in weights[1:]:
                diag = diag + weight
            inverse = 1.0 / diag
            for f in range(6):
                value = weights[f] * inverse
                if f == 4:
                    value = value * mask4
                if f == 5:
                    value = value * mask5
                w[f, i] = value
            finish(i, diag, inverse)
            return carry

        lax.fori_loop(0, 8, step, 0, unroll=True)
        w[0, 0] = jnp.where(lives[0][None] != 0, w[0, 0], 0.0)
        w[1, 7] = jnp.where(lives[1][None] != 0, w[1, 7], 0.0)
        w[2, :, 0] = jnp.where(lives[2][None] != 0, w[2, :, 0], 0.0)
        w[3, :, 7] = jnp.where(lives[3][None] != 0, w[3, :, 7], 0.0)

    def fine_finish(i, diag, inverse):
        bd[i] = dg[i] * inverse
        dg[i] = diag
        xb[9, i + 1, 1:9] = inverse

    weigh(coef, ghost, wt, [fmask[6 + f] for f in range(6)], fine_finish)

    inverse_handles = start_faces(3, xb.at[9])
    arrived(count_handles)
    count_handles = [send(2, [(counts.at[2:4], counts.at[0:2])]), send(-2, [(counts.at[3:5], counts.at[5:7])])]
    ccoef_handles += [send(2, [(ccrow.at[COARSE:2 * COARSE], ccrow.at[3 * COARSE:])]),
                      send(-2, [(ccrow.at[COARSE:2 * COARSE], ccrow2.at[3 * COARSE:])])]
    own_ghosts(x0, ghost)
    far_ghosts(recv.at[1], x0, ghost, x0_handles)
    sweep(x0, ghost, wt, bd, upd, xb.at[2], 0)
    arrived(link_handles)
    for side in range(2):
        for k in range(3):
            f = 2 * k + side
            cut = (0 if side == 0 else 7,)
            cut = (slice(None),) * k + cut
            wface[f] = wt[(f,) + cut] * dg[cut]
            ids = jnp.broadcast_to(nlinks[side, 2 * k + 1 - side:2 * k + 2 - side], (8, LANES))
            nidx[side, k] = jnp.bitwise_and(ids, FINE - 1)
            linked = (ids >= 0) & (jnp.right_shift(ids, 7) == me) & valid[1 if side else -1]
            nmask[side, k] = jnp.where(linked, 1, 0)

    group = jnp.right_shift(lane, 5)
    slot = jnp.bitwise_and(lane, COARSE - 1)
    coarse_handles = []

    def coarse_ghost(x, x_after, f):
        value = face(x, f ^ 1)
        if f % 2 == 1 and x_after is not None:
            value = jnp.where((group < 3)[None], value, face(x_after, f ^ 1))
        return pick_face(value, cidx[f])

    def coarse_setup_a():
        arrived(ccoef_handles + count_handles)
        load_cells(cxb.at[0], ccrow)
        load_cells(cxb.at[4], ccrow2)
        links_c = jnp.concatenate([jnp.where(valid[-1], clb[0], -1), clinks_ref[...], jnp.where(valid[1], clb[1], -1),
                                   jnp.full((6, COARSE), -1, jnp.int32)], axis=1)
        lives = []
        x = cxb.at[0]
        for f in range(6):
            ids = jnp.broadcast_to(links_c[f:f + 1], (8, LANES))
            live = ids >= 0
            step_by = jnp.right_shift(ids, 5) - me
            place = jnp.bitwise_and((step_by + 1) * COARSE + jnp.bitwise_and(ids, COARSE - 1), LANES - 1)
            cidx[f] = jnp.where(live, place, lane)
            lives.append(jnp.where(live, 1, 0))
            put_ghost(x, cghost, f, jnp.where(live[None], coarse_ghost(x, cxb.at[4], f), face(x, f)))

        def finish(i, diag, inverse):
            cidg[i] = inverse

        weigh(x, cghost, cwt, lives, finish)
        for c in range(4):
            block = cidg[2 * c:2 * c + 2].reshape(LANES, LANES).T
            idrow[COARSE:2 * COARSE, c * LANES:(c + 1) * LANES] = block[COARSE:2 * COARSE]
        coarse_handles.append(send(2, [(idrow.at[COARSE:2 * COARSE], idrow.at[3 * COARSE:])]))
        coarse_handles.append(send(-2, [(idrow.at[COARSE:2 * COARSE], idrow2.at[3 * COARSE:])]))

    def known(k, which):
        return counts[k, which] if k == 3 else jnp.where(valid[k - 3], counts[k, which], 0)

    def by_group(values):
        return jnp.where(group == 0, values[0], jnp.where(group == 1, values[1], jnp.where(group == 2, values[2], values[3])))

    def coarse_setup_b():
        a = [known(k, 0) for k in range(7)]
        n = [known(k, 1) for k in range(7)]
        stay = [FINE - a[k] - n[k] if k == 3 else jnp.where(valid[k - 3], FINE - a[k] - n[k], 0) for k in range(7)]
        for base, last in ((0, 1), (4, 5)):
            before, here = by_group(n[1:4] + [n[last - 1]]), by_group(stay[2:5] + [stay[last]])
            start, after = by_group(a[2:5] + [a[last]]), by_group(a[3:6] + [a[last + 1]])
            place = jnp.where(group < 3, group - 1, last - 3)
            for o in range(4):
                rank = 8 * slot + 2 * o + jnp.where(row >= 4, 1, 0)
                in_before = rank < before
                in_here = rank < before + here
                in_after = rank < before + here + after
                at = jnp.where(in_before, FINE - before + rank, jnp.where(in_here, start + rank - before, rank - before - here))
                step_by = jnp.where(in_before, place - 1, jnp.where(in_here, place, place + 1))
                source = jnp.where((step_by == 3) | (step_by == -3), 5, step_by + 2)
                tidx[2 * base + o] = jnp.bitwise_and(at, LANES - 1)
                tsrc[base + o] = jnp.where(in_after, source, 6)
        rank_own = n[2] + lane - a[3]
        rank_far = jnp.where(lane < 64, n[2] + stay[3] + lane, lane - FINE + n[2])
        for k, rank in enumerate((rank_own, rank_far)):
            rank = jnp.bitwise_and(rank, 255)
            tidx[4 + 2 * k] = COARSE + jnp.right_shift(rank, 3)
            tidx[5 + 2 * k] = jnp.bitwise_and(rank, 7)

    def coarse_setup_c():
        arrived(coarse_handles)
        for c in range(4):
            block = idrow[:, c * LANES:(c + 1) * LANES].T.reshape(2, 8, 8, LANES)
            cidg[2 * c:2 * c + 2] = jnp.where((group < 3)[None, None], cidg[2 * c:2 * c + 2], block)
            cidg2[2 * c:2 * c + 2] = idrow2[:, c * LANES:(c + 1) * LANES].T.reshape(2, 8, 8, LANES)

    def setup_first():
        arrived(inverse_handles)
        coarse_setup_a()
        coarse_setup_b()

    two_sweeps(xb.at[2], ghost, xb.at[3], ghost3, xb.at[4], xb.at[10], 6, setup_first)
    x3 = xb.at[4]
    psi[...] = jnp.zeros((2, 64, LANES), jnp.float32)
    for side in range(2):
        edge = 0 if side else 3
        for k in range(3):
            f = 2 * k + side
            pairs = (face(x3, f) * wface[f]).reshape(4, 2, 8, LANES)
            pairs = pairs[:, 0] + pairs[:, 1]
            pairs = 0.5 * (pairs + pltpu.roll(pairs, 7, 1))
            halved[f] = pairs.reshape(32, LANES)
            part = pick(halved[f, pl.ds(0, 16, stride=2)], nidx[side, k])
            mask = jnp.broadcast_to(nmask[side, k][None], (2, 8, LANES)).reshape(16, LANES)
            part = jnp.where(mask != 0, part, 0.0)
            if k == 0:
                psi[side, 16 * edge:16 * edge + 16] = part
            elif k == 1:
                for i in range(4):
                    at = 16 * i + 4 * edge
                    psi[side, at:at + 4] = psi[side, at:at + 4] + part[4 * i:4 * i + 4]
            else:
                psi[side, pl.ds(edge, 16, stride=4)] = psi[side, pl.ds(edge, 16, stride=4)] + part
    low_lane = jnp.broadcast_to((lane < 64)[None], (4, 8, LANES)).reshape(32, LANES)

    def pack(values, keep_low):
        turned = pltpu.roll(values[32:], 64, 1)
        return jnp.where(low_lane, values[:32], turned) if keep_low else jnp.where(low_lane, turned, values[:32])

    def pack_edges(values, keep_low):
        turned = pltpu.roll(values[8:], 64, 1)
        return jnp.where(lane < 64, values[:8], turned) if keep_low else jnp.where(lane < 64, turned, values[:8])

    def edge_places(upper):
        return (slice(60, 64), pl.ds(51, 4, stride=4), pl.ds(15, 4, stride=16)) if upper else (
            slice(0, 4), pl.ds(0, 4, stride=4), pl.ds(0, 4, stride=16))

    def edge_rows(ref, upper):
        parts = [ref[place] for place in edge_places(upper)]
        return jnp.concatenate(parts + parts[:1], axis=0)

    for at, (side, distance) in enumerate(((0, 1), (1, -1), (1, 3), (0, -3))):
        pair2[2 + at] = pack(psi[side], distance < 0)
    for ahead in (1, 0):
        base = 0 if ahead else 3
        back_edges, ahead_edges = edge_rows(psi.at[1 - ahead], ahead), edge_rows(psi.at[ahead], ahead)
        eb[base], eb[base + 2] = back_edges, ahead_edges
        eh[base], eh[base + 2] = pack_edges(back_edges, not ahead), pack_edges(ahead_edges, not ahead)
    r_handles = [send(4, [(eh.at[2], ehr.at[2])]), send(-4, [(eh.at[5], ehr.at[5])]),
                 send(3, [(pair2.at[4], pair2r.at[4]), (eb.at[2], ebr.at[2])]),
                 send(-3, [(pair2.at[5], pair2r.at[5]), (eb.at[5], ebr.at[5])]),
                 send(2, [(psi.at[1], psir.at[2]), (eh.at[0], ehr.at[0])]),
                 send(-2, [(psi.at[0], psir.at[3]), (eh.at[3], ehr.at[3])]),
                 send(1, [(psi.at[1], psir.at[0]), (pair2.at[2], pair2r.at[2]), (eb.at[0], ebr.at[0])]),
                 send(-1, [(psi.at[0], psir.at[1]), (pair2.at[3], pair2r.at[3]), (eb.at[3], ebr.at[3])])]

    own_ghosts(xb.at[4], ghost, zero_far=True)


    def restrict_step(i, carry):
        total = jnp.zeros((4, 8, LANES), jnp.float32)
        for half in range(2):
            _, scaled = scaled_residual(x3, ghost, wt, bd, 2 * i + half)
            quads = (scaled * dg[2 * i + half]).reshape(4, 2, 8, LANES)
            total = total + quads[:, 0] + quads[:, 1]
        total = total + pltpu.roll(total, 7, 1)
        tall[pl.ds(pl.multiple_of(i * 32, 32), 32)] = 0.5 * total.reshape(32, LANES)
        return carry

    lax.fori_loop(0, 4, restrict_step, 0, unroll=True)
    restricted = tall[pl.ds(0, 64, stride=2)]
    local[...] = restricted
    pair2[0] = pack(restricted, False)
    pair2[1] = pack(restricted, True)
    for ahead in (1, 0):
        base = 0 if ahead else 3
        own_edges = edge_rows(local, ahead)
        eb[base + 1] = own_edges
        eh[base + 1] = pack_edges(own_edges, not ahead)
    r_handles += [send(3, [(eh.at[1], ehr.at[1])]), send(-3, [(eh.at[4], ehr.at[4])]),
                  send(2, [(pair2.at[0], pair2r.at[0]), (eb.at[1], ebr.at[1])]),
                  send(-2, [(pair2.at[1], pair2r.at[1]), (eb.at[4], ebr.at[4])]),
                  send(1, [(local, src.at[1])]), send(-1, [(local, src.at[3])])]
    x3_handles = start_faces(4, x3)
    coarse_setup_c()
    arrived(r_handles)
    src[1] = src[1] + psi[0] + jnp.where(valid[-2], psir[2], 0.0)
    src[3] = src[3] + psi[1] + jnp.where(valid[2], psir[3], 0.0)
    src[2] = local[...] + jnp.where(valid[-1], psir[0], 0.0) + jnp.where(valid[1], psir[1], 0.0)
    high = pair2r[0] + pair2r[2] + jnp.where(valid[-3], pair2r[4], 0.0)
    low = pair2r[1] + pair2r[3] + jnp.where(valid[3], pair2r[5], 0.0)
    src[0] = jnp.concatenate([high, pltpu.roll(high, 64, 1)], axis=0)
    src[4] = jnp.concatenate([low, pltpu.roll(low, 64, 1)], axis=0)
    for ahead in (1, 0):
        base, sign = (0, -1) if ahead else (3, 1)
        edge_two = ebr[base] + ebr[base + 1] + jnp.where(valid[3 * sign], ebr[base + 2], 0.0)
        edge_three = ehr[base] + ehr[base + 1] + jnp.where(valid[4 * sign], ehr[base + 2], 0.0)
        edge_three = jnp.concatenate([edge_three, pltpu.roll(edge_three, 64, 1)], axis=0)
        for at, place in enumerate(edge_places(ahead)):
            src[0 if ahead else 4, place] = edge_two[4 * at:4 * at + 4]
            src[5, place] = edge_three[4 * at:4 * at + 4]

    for o in range(4):
        ox, oy = o // 2, o % 2
        index, which = tidx[o], tsrc[o]
        for i in range(4):
            for j in range(4):
                q = 4 * (4 * i + j)
                value = jnp.zeros((8, LANES), jnp.float32)
                for k in range(6):
                    four = src[k, q:q + 4]
                    taken = pick(jnp.concatenate([four, four], axis=0), index)
                    value = jnp.where(which == k, taken, value)
                at = (4 * ox + i, 4 * oy + j)
                scaled = value * cidg[at[0], at[1]]
                cbd[at[0], at[1]] = scaled
                update = scaled * (1.0 / THETA)
                cupd[at[0], at[1]] = update
                cxb[1, at[0] + 1, at[1] + 1] = update
                if at[0] == 0 or at[1] == 0:
                    for k in (3, 4, 5):
                        four = src[k, q:q + 4]
                        taken = pick(jnp.concatenate([four, four], axis=0), tidx[8 + o])
                        value = taken if k == 3 else jnp.where(tsrc[4 + o] == k, taken, value)
                    value = jnp.where(tsrc[4 + o] < 6, value, 0.0)
                    cxb[5, at[0] + 1, at[1] + 1] = value * cidg2[at[0], at[1]] * (1.0 / THETA)

    c1, c2, c3 = cxb.at[1], cxb.at[2], cxb.at[3]
    for f in range(6):
        put_ghost(c1, cghost, f, coarse_ghost(c1, cxb.at[5], f))
    sweep(c1, cghost, cwt, cbd, cupd, c2, 1)
    for f in range(6):
        put_ghost(c2, cghost, f, coarse_ghost(c2, None, f))
    sweep(c2, cghost, cwt, cbd, cupd, c3, 2)

    for k in (1, 0):
        place, octant = tidx[4 + 2 * k], tidx[5 + 2 * k]
        straight = (jnp.bitwise_and(octant, 1) == 0) == (row < 4)
        outer = jnp.right_shift(octant, 1)
        for i in range(4):
            quads = []
            for j in range(4):
                value = pick(c3[i + 1, j + 1], place)
                for o in range(1, 4):
                    value = jnp.where(outer == o, pick(c3[4 * (o // 2) + i + 1, 4 * (o % 2) + j + 1], place), value)
                quads.append(jnp.where(straight, value, pltpu.roll(value, 4, 0)))
            for half in range(2):
                at = 16 * i + 8 * half
                back[k, at:at + 8] = jnp.where(row < 4, quads[2 * half], quads[2 * half + 1])
        if k == 1:
            backp[0] = pack(back[1], True)
            backp[1] = pack(back[1], False)
            b_handles = [send(2, [(backp.at[0], backpr.at[2])]), send(-2, [(backp.at[1], backpr.at[3])]),
                         send(1, [(backp.at[0], backpr.at[0])]), send(-1, [(backp.at[1], backpr.at[1])])]
        else:
            b_handles += [send(1, [(back.at[0], backr.at[0])]), send(-1, [(back.at[0], backr.at[1])])]
    for c in range(4):
        block = c3[2 * c + 1:2 * c + 3, 1:9].reshape(LANES, LANES).T
        cout_ref[:, c * LANES:(c + 1) * LANES] = block[COARSE:2 * COARSE]
    far_ghosts(recv.at[4], x3, ghost, x3_handles)
    arrived(b_handles)

    def by_owner(at, before, here, after):
        low = jnp.where(lane < known(at, 0), 1, 0)
        high = jnp.where(lane >= FINE - known(at, 1), 1, 0)
        low = jnp.broadcast_to(low[None], (8, 8, LANES)).reshape(64, LANES)
        high = jnp.broadcast_to(high[None], (8, 8, LANES)).reshape(64, LANES)
        return jnp.where(low != 0, before, jnp.where(high != 0, after, here))

    first_half, last_half = [
        jnp.concatenate([backpr[at], pltpu.roll(backpr[at], 64, 1)], axis=0) for at in (0, 2)], [
        jnp.concatenate([backpr[at], pltpu.roll(backpr[at], 64, 1)], axis=0) for at in (1, 3)]
    values = by_owner(3, first_half[0], back[0], last_half[0])
    near[0] = by_owner(2, first_half[1], backr[0], back[1])
    near[1] = by_owner(4, back[1], backr[1], last_half[1])
    expand[pl.ds(0, 64, stride=2)] = values
    expand[pl.ds(1, 64, stride=2)] = values

    def correct_step(i, carry):
        four = expand[pl.ds(pl.multiple_of((i // 2) * 32, 32), 32)].reshape(4, 1, 8, LANES)
        xb[5, i + 1, 1:9] = x3[i + 1, 1:9] + jnp.broadcast_to(four, (4, 2, 8, LANES)).reshape(8, 8, LANES)
        return carry

    lax.fori_loop(0, 8, correct_step, 0, unroll=True)

    for f in range(6):
        k, side = f // 2, f % 2
        edge = 0 if side else 3
        if k == 0:
            part = near[side, 16 * edge:16 * edge + 16]
        elif k == 1:
            part = jnp.concatenate([near[side, 16 * i + 4 * edge:16 * i + 4 * edge + 4] for i in range(4)], axis=0)
        else:
            part = near[side, pl.ds(edge, 16, stride=4)]
        part = pick(part, fidx[f])
        expand2[f, pl.ds(0, 16, stride=2)] = part
        expand2[f, pl.ds(1, 16, stride=2)] = part
        four = expand2[f].reshape(4, 1, 8, LANES)
        far = get_ghost(x3, ghost, f) + jnp.broadcast_to(four, (4, 2, 8, LANES)).reshape(8, 8, LANES)
        own = pick_face(face(xb.at[5], f ^ 1), fidx[f])
        put_ghost(xb.at[5], ghost2, f, jnp.where(fmask[f][None] != 0, far, own))

    sweep(xb.at[5], ghost2, wt, bd, upd, xb.at[6], 0)
    two_sweeps(xb.at[6], ghost, xb.at[7], ghost3, xb.at[8], xb.at[11], 8)
    for c in range(4):
        block = xb[8, 2 * c + 1:2 * c + 3, 1:9].reshape(LANES, LANES).T
        out_ref[:, c * LANES:(c + 1) * LANES] = block

    for offset in valid:
        @pl.when(valid[offset])
        def _():
            for o, made in sent:
                if o == offset:
                    for copy in made:
                        copy.wait_send()


def deliver(fine_ref, coarse_ref, fine_out, coarse_out, fine, coarse, in_sem, out_sem):
    parts = [(fine_ref.at[32 * c:32 * c + 32], fine.at[32 * c:32 * c + 32], fine_out.at[32 * c:32 * c + 32]) for c in range(4)]
    parts.append((coarse_ref, coarse, coarse_out))
    fetches = [pltpu.make_async_copy(source, middle, in_sem.at[at]) for at, (source, middle, _) in enumerate(parts)]
    stores = [pltpu.make_async_copy(middle, target, out_sem.at[at]) for at, (_, middle, target) in enumerate(parts)]
    for fetch in fetches:
        fetch.start()
    for fetch, store in zip(fetches, stores):
        fetch.wait()
        store.start()
    for store in stores:
        store.wait()


def solution(mesh):
    gx, gy = mesh.shape["gx"], mesh.shape["gy"]
    f32, i32 = jnp.float32, jnp.int32

    def on_device(rhs, guess, coef, links, owner, ccoef, clinks):
        whole = pl.BlockSpec(memory_space=pltpu.VMEM)
        volume, padded = (8, 8, 8, LANES), (10, 10, 8, LANES)
        results = pl.pallas_call(
            functools.partial(kernel, gx, gy),
            out_shape=(jax.ShapeDtypeStruct((FINE, 512), f32), jax.ShapeDtypeStruct((COARSE, 512), f32)),
            in_specs=[pl.BlockSpec(memory_space=pltpu.HBM)] * 7,
            out_specs=(whole, whole),
            scratch_shapes=[
                pltpu.VMEM((FINE, 512), f32),
                pltpu.VMEM((FINE, 512), f32),
                pltpu.VMEM((FINE, 512), f32),
                pltpu.VMEM((6, FINE), i32),
                pltpu.VMEM((1, FINE), i32),
                pltpu.VMEM((6, COARSE), i32),
                pltpu.VMEM((12,) + padded, f32),
                pltpu.VMEM((6,) + volume, f32),
                pltpu.VMEM(volume, f32),
                pltpu.VMEM(volume, f32),
                pltpu.VMEM(volume, f32),
                pltpu.VMEM((2, 8, 8, LANES), f32),
                pltpu.VMEM((10, 2, 8, 8, LANES), f32),
                pltpu.VMEM((10, 2, 3, 8, 8, LANES), f32),
                pltpu.VMEM((6, 8, LANES), i32),
                pltpu.VMEM((12, 8, LANES), i32),
                pltpu.VMEM((LANES, 512), f32),
                pltpu.VMEM((6,) + padded, f32),
                pltpu.VMEM((6,) + volume, f32),
                pltpu.VMEM(volume, f32),
                pltpu.VMEM(volume, f32),
                pltpu.VMEM(volume, f32),
                pltpu.VMEM((2, 8, 8, LANES), f32),
                pltpu.VMEM((LANES, 512), f32),
                pltpu.VMEM((12, 8, LANES), i32),
                pltpu.VMEM((8, 8, LANES), i32),
                pltpu.VMEM((6, 8, LANES), i32),
                pltpu.VMEM((2, 6, COARSE), i32),
                pltpu.VMEM((LANES, 512), f32),
                pltpu.VMEM((LANES, 512), f32),
                pltpu.VMEM(volume, f32),
                pltpu.VMEM((7, 2, 8, LANES), i32),
                pltpu.VMEM((6, 64, LANES), f32),
                pltpu.VMEM((6, 32, LANES), f32),
                pltpu.VMEM((6, 32, LANES), f32),
                pltpu.VMEM((LANES, LANES), f32),
                pltpu.VMEM((2, 64, LANES), f32),
                pltpu.VMEM((2, 64, LANES), f32),
                pltpu.VMEM((2, 32, LANES), f32),
                pltpu.VMEM((4, 32, LANES), f32),
                pltpu.VMEM((LANES, LANES), f32),
                pltpu.VMEM((2, 64, LANES), f32),
                pltpu.VMEM((6, 32, LANES), f32),
                pltpu.VMEM((2, 8, 8, LANES), f32),
                pltpu.VMEM((2, 6, FINE), i32),
                pltpu.VMEM((2, 3, 8, LANES), i32),
                pltpu.VMEM((2, 3, 8, LANES), i32),
                pltpu.VMEM((6, 8, 8, LANES), f32),
                pltpu.VMEM((2, 3, 8, 8, LANES), f32),
                pltpu.VMEM((2, 2, 6, 8, LANES), f32),
                pltpu.VMEM((2, 2, 6, 8, LANES), f32),
                pltpu.VMEM((2, 3, 8, 8, LANES), f32),
                pltpu.VMEM((2, 8, 8, LANES), f32),
                pltpu.VMEM((64, LANES), f32),
                pltpu.VMEM((2, 64, LANES), f32),
                pltpu.VMEM((4, 64, LANES), f32),
                pltpu.VMEM((6, 32, LANES), f32),
                pltpu.VMEM((6, 16, LANES), f32),
                pltpu.VMEM((6, 16, LANES), f32),
                pltpu.VMEM((6, 8, LANES), f32),
                pltpu.VMEM((6, 8, LANES), f32),
                pltpu.SemaphoreType.DMA((N_COPIES,)),
                pltpu.SemaphoreType.DMA((N_COPIES,)),
                pltpu.SemaphoreType.DMA((7,)),
            ],
            compiler_params=pltpu.CompilerParams(collective_id=0, has_side_effects=True, vmem_limit_bytes=56 * 1024 * 1024),
        )(rhs, guess, coef, links.T, owner.T, ccoef, clinks.T)
        hbm = pl.BlockSpec(memory_space=pltpu.HBM)
        return pl.pallas_call(
            deliver,
            out_shape=(jax.ShapeDtypeStruct((FINE, 512), f32), jax.ShapeDtypeStruct((COARSE, 512), f32)),
            in_specs=[hbm, hbm],
            out_specs=(hbm, hbm),
            scratch_shapes=[pltpu.VMEM((FINE, 512), f32), pltpu.VMEM((COARSE, 512), f32),
                            pltpu.SemaphoreType.DMA((5,)), pltpu.SemaphoreType.DMA((5,))],
        )(*results)

    rows = P(("gx", "gy"), None)
    return jax.shard_map(on_device, mesh=mesh, in_specs=(rows,) * 7, out_specs=(rows, rows), check_vma=False)
```

```python
import functools

import jax
import jax.numpy as jnp
from jax import lax
from jax.experimental import pallas as pl
from jax.experimental.pallas import tpu as pltpu
from jax.sharding import PartitionSpec as P

THETA = 1.25
DELTA = 0.75
SIGMA = THETA / DELTA
RHO0 = 1.0 / SIGMA
RHO1 = 1.0 / (2.0 * SIGMA - RHO0)
RHO2 = 1.0 / (2.0 * SIGMA - RHO1)
SWEEPS = ((0.0, 1.0 / THETA), (RHO1 * RHO0, 2.0 * RHO1 / DELTA), (RHO2 * RHO1, 2.0 * RHO2 / DELTA))

LANES = 128
FINE = 128
COARSE = 32
MESH = pl.DeviceIdType.MESH
N_COPIES = 104


def pick(values, index):
    rows = values.shape[0]
    whole = jnp.broadcast_to(index[None], (rows // 8, 8, LANES)).reshape(rows, LANES)
    return jnp.take_along_axis(values, whole, axis=1, mode="promise_in_bounds")


def pick_face(face, index):
    return pick(face.reshape(64, LANES), index).reshape(8, 8, LANES)


def kernel(
    gx, gy,
    rhs_hbm, guess_hbm, coef_hbm, links_hbm, owner_hbm, ccoef_hbm, clinks_hbm,
    out_hbm, cout_hbm,
    out_ref, cout_ref,
    rhs_ref, guess_ref, coef_ref, links_ref, owner_ref, clinks_ref,
    xb, wt, bd, dg, upd, ghost, packed, recv, fidx, fmask,
    ccrow, cxb, cwt, cidg, cbd, cupd, cghost, idrow, tidx, tsrc, cidx, clb, ccrow2, idrow2, cidg2,
    counts, src, pair2, pair2r, tall, back, backr, backp, backpr, expand, near, expand2, ghost2,
    nlinks, nidx, nmask, wface, flux, edges, erecv, beside, ghost3, local, psi, psir, halved, eb, ebr, eh, ehr,
    ssem, rsem, isem, osem,
):
    devices = gx * gy
    me = lax.axis_index("gx") * gy + lax.axis_index("gy")
    valid = {1: me < devices - 1, -1: me > 0, 2: me < devices - 2, -2: me > 1, 3: me < devices - 3, -3: me > 2,
             4: me < devices - 4, -4: me > 3}

    def device(offset):
        target = lax.rem(me + offset + devices, devices)
        return (target // gy, lax.rem(target, gy))

    barrier = pltpu.get_barrier_semaphore()
    for offset in (1, -1, 2, -2):
        @pl.when(valid[offset])
        def _():
            pl.semaphore_signal(barrier, inc=1, device_id=device(offset), device_id_type=MESH)

    fetches = []
    for at, (source, target) in enumerate((
            (coef_hbm, coef_ref), (guess_hbm, guess_ref), (owner_hbm, owner_ref), (links_hbm, links_ref),
            (ccoef_hbm, ccrow.at[COARSE:2 * COARSE]), (rhs_hbm, rhs_ref), (clinks_hbm, clinks_ref))):
        fetches.append(pltpu.make_async_copy(source, target, isem.at[at]))
        fetches[-1].start()

    used = [0]
    sent = []

    def send(offset, pairs):
        made = []
        for source, target in pairs:
            at = used[0]
            used[0] += 1
            made.append(pltpu.make_async_remote_copy(
                src_ref=source, dst_ref=target, send_sem=ssem.at[at], recv_sem=rsem.at[at],
                device_id=device(offset), device_id_type=MESH))

        @pl.when(valid[offset])
        def _():
            for copy in made:
                copy.start()

        sent.append((offset, made))
        return (offset, made)

    def arrived(handles):
        for offset in valid:
            made = [copy for to, copies in handles if to == offset for copy in copies]
            if made:
                @pl.when(valid[-offset])
                def _():
                    for copy in made:
                        copy.wait_recv()

    lane = lax.broadcasted_iota(jnp.int32, (8, LANES), 1)
    row = lax.broadcasted_iota(jnp.int32, (8, LANES), 0)
    row3 = lax.broadcasted_iota(jnp.int32, (8, 8, LANES), 1)
    first, last = row3 == 0, row3 == 7

    def load_cells(buffer, rows_ref):
        for c in range(4):
            block = rows_ref[:, c * LANES:(c + 1) * LANES].T
            buffer[2 * c + 1:2 * c + 3, 1:9] = block.reshape(2, 8, 8, LANES)

    def face(x, f):
        at = 1 if f % 2 == 0 else 8
        if f // 2 == 0:
            return x[at, 1:9]
        if f // 2 == 1:
            return x[1:9, at]
        return x[1:9, 1:9, 0 if f % 2 == 0 else 7]

    def put_ghost(x, g, f, value):
        at = 0 if f % 2 == 0 else 9
        if f // 2 == 0:
            x[at, 1:9] = value
        elif f // 2 == 1:
            x[1:9, at] = value
        else:
            g[f % 2] = value

    def get_ghost(x, g, f):
        at = 0 if f % 2 == 0 else 9
        if f // 2 == 0:
            return x[at, 1:9]
        if f // 2 == 1:
            return x[1:9, at]
        return g[f % 2]

    def neighbours(x, g, i):
        centre = x[i + 1, 1:9]
        low = jnp.where(first, g[0, i][:, None, :], pltpu.roll(centre, 1, 1))
        high = jnp.where(last, g[1, i][:, None, :], pltpu.roll(centre, 7, 1))
        return centre, (x[i, 1:9], x[i + 2, 1:9], x[i + 1, 0:8], x[i + 1, 2:10], low, high)

    def scaled_residual(x, g, w, b, i):
        centre, others = neighbours(x, g, i)
        total = b[i] - centre
        for f in range(6):
            total = total + w[f, i] * others[f]
        return centre, total

    def sweep(x, g, w, b, d, new, at, final=True):
        keep, gain = SWEEPS[at]

        def step(i, carry):
            centre, total = scaled_residual(x, g, w, b, i)
            update = gain * total
            if at > 0:
                update = update + keep * d[i]
            if final:
                d[i] = update
            new[i + 1, 1:9] = centre + update
            return carry

        lax.fori_loop(0, 8, step, 0, unroll=True)

    def start_faces(e, x):
        packed[e, 0] = face(x, 4)
        packed[e, 1] = face(x, 5)
        up = send(1, [(x.at[8, 1:9], recv.at[e, 0, 0]), (x.at[1:9, 8], recv.at[e, 0, 1]), (packed.at[e, 1], recv.at[e, 0, 2])])
        down = send(-1, [(x.at[1, 1:9], recv.at[e, 1, 0]), (x.at[1:9, 1], recv.at[e, 1, 1]), (packed.at[e, 0], recv.at[e, 1, 2])])
        return up, down

    def own_ghosts(x, g, keep_own=False, zero_far=False):
        for f in range(6):
            value = pick_face(face(x, f ^ 1), fidx[f])
            if keep_own:
                value = jnp.where(fmask[6 + f][None] != 0, value, face(x, f))
            if zero_far:
                value = jnp.where(fmask[f][None] != 0, 0.0, value)
            put_ghost(x, g, f, value)

    def far_ghosts(faces, x, g, handles=()):
        arrived(handles)
        for k in range(3):
            for side in range(2):
                f = 2 * k + side
                value = pick_face(faces[side, k], fidx[f])
                put_ghost(x, g, f, jnp.where(fmask[f][None] != 0, value, get_ghost(x, g, f)))

    def across(k, m):
        return (m if m < k else m - 1)

    def line(k, m, at):
        return (at,) if across(k, m) == 0 else (slice(None), at)

    def two_sweeps(x, handles, g, middle, g_middle, new, partial, e, between=None):
        keep, gain = SWEEPS[1]
        for side in range(2):
            for k in range(3):
                f = 2 * k + side
                value = pick_face(face(x, f) * wface[f], nidx[side, k])
                flux[side, k] = jnp.where(nmask[side, k][None] != 0, value, 0.0)
        at = 0
        for m in range(3):
            for k in range(3):
                if k != m:
                    for side in range(2):
                        edges[e // 7, side, at] = flux[(side, m) + line(m, k, 7 if side else 0)]
                    at += 1
        edge_handles = [send(2, [(edges.at[e // 7, 1], erecv.at[e // 7, 0])]), send(-2, [(edges.at[e // 7, 0], erecv.at[e // 7, 1])])]
        own_ghosts(x, g, zero_far=True)
        sweep(x, g, wt, bd, upd, partial, 1, final=False)
        partial_handles = start_faces(e + 1, partial)
        for side in range(2):
            end = 0 if side else 7
            for k in range(3):
                beside[side, k] = flux[side, k]
                for m in range(3):
                    if m != k:
                        where = (side, k) + line(k, m, end)
                        beside[where] = beside[where] + flux[(side, m) + line(m, k, end)]
        if between is not None:
            between()
        far_ghosts(recv.at[e], x, g, handles)
        sweep(x, g, wt, bd, upd, middle, 1)
        own_ghosts(middle, g_middle)
        arrived(edge_handles + list(partial_handles))
        for side in range(2):
            end = 0 if side else 7
            at = 0
            for m in range(3):
                for k in range(3):
                    if k != m:
                        where = (side, k) + line(k, m, 7 - end)
                        behind = jnp.where(valid[2 if side else -2], erecv[e // 7, side, at], 0.0)
                        beside[where] = beside[where] + behind
                        at += 1
        for side in range(2):
            for k in range(3):
                beside[side, k] = recv[e + 1, side, k] + gain * recv[3, side, k] * beside[side, k]
        far_ghosts(beside, middle, g_middle)
        sweep(middle, g_middle, wt, bd, upd, new, 2)

    coef, x0 = xb.at[0], xb.at[1]
    fetches[0].wait()
    load_cells(coef, coef_ref)
    fetches[1].wait()
    load_cells(x0, guess_ref)
    for fetch in fetches[2:]:
        fetch.wait()

    owner = owner_ref[...]
    to_prev = jnp.sum((owner == me - 1).astype(jnp.float32), axis=1, keepdims=True).astype(jnp.int32)
    to_next = jnp.sum((owner == me + 1).astype(jnp.float32), axis=1, keepdims=True).astype(jnp.int32)
    counts[3, 0] = jnp.broadcast_to(to_prev, (8, LANES))
    counts[3, 1] = jnp.broadcast_to(to_next, (8, LANES))

    pl.semaphore_wait(barrier, jnp.minimum(me, 2) + jnp.minimum(devices - 1 - me, 2))

    coef_handles = start_faces(0, coef)
    x0_handles = start_faces(1, x0)
    count_handles = [send(o, [(counts.at[3], counts.at[3 - o])]) for o in (1, -1)]
    link_handles = [send(1, [(links_ref, nlinks.at[0]), (clinks_ref, clb.at[0])]),
                    send(-1, [(links_ref, nlinks.at[1]), (clinks_ref, clb.at[1])])]
    ccoef_handles = [send(1, [(ccrow.at[COARSE:2 * COARSE], ccrow.at[0:COARSE])]),
                     send(-1, [(ccrow.at[COARSE:2 * COARSE], ccrow.at[2 * COARSE:3 * COARSE])])]

    ccoef_handles += [send(2, [(ccrow.at[COARSE:2 * COARSE], ccrow.at[3 * COARSE:])]),
                      send(-2, [(ccrow.at[COARSE:2 * COARSE], ccrow2.at[3 * COARSE:])])]

    links = links_ref[...]
    for f in range(6):
        ids = jnp.broadcast_to(links[f:f + 1], (8, LANES))
        live = ids >= 0
        fidx[f] = jnp.bitwise_and(ids, FINE - 1)
        fmask[f] = jnp.where(live & (jnp.right_shift(ids, 7) != me), 1, 0)
        fmask[6 + f] = jnp.where(live, 1, 0)

    for c in range(4):
        dg[2 * c:2 * c + 2] = rhs_ref[:, c * LANES:(c + 1) * LANES].T.reshape(2, 8, 8, LANES)
    own_ghosts(x0, ghost3)
    own_ghosts(coef, ghost, keep_own=True)
    far_ghosts(recv.at[0], coef, ghost, coef_handles)

    def weigh(x, g, w, lives, finish):
        mask4 = jnp.where((row == 0) & (lives[4] == 0), 0.0, 1.0)[None]
        mask5 = jnp.where((row == 7) & (lives[5] == 0), 0.0, 1.0)[None]

        def step(i, carry):
            centre, others = neighbours(x, g, i)
            weights = [0.5 * (centre + other) for other in others]
            diag = weights[0]
            for weight in weights[1:]:
                diag = diag + weight
            inverse = 1.0 / diag
            for f in range(6):
                value = weights[f] * inverse
                if f == 4:
                    value = value * mask4
                if f == 5:
                    value = value * mask5
                w[f, i] = value
            finish(i, diag, inverse)
            return carry

        lax.fori_loop(0, 8, step, 0, unroll=True)
        w[0, 0] = jnp.where(lives[0][None] != 0, w[0, 0], 0.0)
        w[1, 7] = jnp.where(lives[1][None] != 0, w[1, 7], 0.0)
        w[2, :, 0] = jnp.where(lives[2][None] != 0, w[2, :, 0], 0.0)
        w[3, :, 7] = jnp.where(lives[3][None] != 0, w[3, :, 7], 0.0)

    def fine_finish(i, diag, inverse):
        bd[i] = dg[i] * inverse
        dg[i] = diag
        xb[9, i + 1, 1:9] = inverse

    weigh(coef, ghost, wt, [fmask[6 + f] for f in range(6)], fine_finish)

    inverse_handles = start_faces(3, xb.at[9])
    arrived(count_handles)
    count_handles = [send(2, [(counts.at[2:4], counts.at[0:2])]), send(-2, [(counts.at[3:5], counts.at[5:7])])]
    far_ghosts(recv.at[1], x0, ghost3, x0_handles)
    sweep(x0, ghost3, wt, bd, upd, xb.at[2], 0)
    x1_handles = start_faces(6, xb.at[2])
    arrived(link_handles)
    for side in range(2):
        for k in range(3):
            f = 2 * k + side
            cut = (0 if side == 0 else 7,)
            cut = (slice(None),) * k + cut
            wface[f] = wt[(f,) + cut] * dg[cut]
            ids = jnp.broadcast_to(nlinks[side, 2 * k + 1 - side:2 * k + 2 - side], (8, LANES))
            nidx[side, k] = jnp.bitwise_and(ids, FINE - 1)
            linked = (ids >= 0) & (jnp.right_shift(ids, 7) == me) & valid[1 if side else -1]
            nmask[side, k] = jnp.where(linked, 1, 0)

    group = jnp.right_shift(lane, 5)
    slot = jnp.bitwise_and(lane, COARSE - 1)
    coarse_handles = []

    def coarse_ghost(x, x_after, f):
        value = face(x, f ^ 1)
        if f % 2 == 1 and x_after is not None:
            value = jnp.where((group < 3)[None], value, face(x_after, f ^ 1))
        return pick_face(value, cidx[f])

    def coarse_setup_a():
        arrived(ccoef_handles + count_handles)
        load_cells(cxb.at[0], ccrow)
        load_cells(cxb.at[4], ccrow2)
        links_c = jnp.concatenate([jnp.where(valid[-1], clb[0], -1), clinks_ref[...], jnp.where(valid[1], clb[1], -1),
                                   jnp.full((6, COARSE), -1, jnp.int32)], axis=1)
        lives = []
        x = cxb.at[0]
        for f in range(6):
            ids = jnp.broadcast_to(links_c[f:f + 1], (8, LANES))
            live = ids >= 0
            step_by = jnp.right_shift(ids, 5) - me
            place = jnp.bitwise_and((step_by + 1) * COARSE + jnp.bitwise_and(ids, COARSE - 1), LANES - 1)
            cidx[f] = jnp.where(live, place, lane)
            lives.append(jnp.where(live, 1, 0))
            put_ghost(x, cghost, f, jnp.where(live[None], coarse_ghost(x, cxb.at[4], f), face(x, f)))

        def finish(i, diag, inverse):
            cidg[i] = inverse

        weigh(x, cghost, cwt, lives, finish)
        for c in range(4):
            block = cidg[2 * c:2 * c + 2].reshape(LANES, LANES).T
            idrow[COARSE:2 * COARSE, c * LANES:(c + 1) * LANES] = block[COARSE:2 * COARSE]
        coarse_handles.append(send(2, [(idrow.at[COARSE:2 * COARSE], idrow.at[3 * COARSE:])]))
        coarse_handles.append(send(-2, [(idrow.at[COARSE:2 * COARSE], idrow2.at[3 * COARSE:])]))

    def known(k, which):
        return counts[k, which] if k == 3 else jnp.where(valid[k - 3], counts[k, which], 0)

    def by_group(values):
        return jnp.where(group == 0, values[0], jnp.where(group == 1, values[1], jnp.where(group == 2, values[2], values[3])))

    def coarse_setup_b():
        a = [known(k, 0) for k in range(7)]
        n = [known(k, 1) for k in range(7)]
        stay = [FINE - a[k] - n[k] if k == 3 else jnp.where(valid[k - 3], FINE - a[k] - n[k], 0) for k in range(7)]
        for base, last in ((0, 1), (4, 5)):
            before, here = by_group(n[1:4] + [n[last - 1]]), by_group(stay[2:5] + [stay[last]])
            start, after = by_group(a[2:5] + [a[last]]), by_group(a[3:6] + [a[last + 1]])
            place = jnp.where(group < 3, group - 1, last - 3)
            for o in range(4):
                rank = 8 * slot + 2 * o + jnp.where(row >= 4, 1, 0)
                in_before = rank < before
                in_here = rank < before + here
                in_after = rank < before + here + after
                at = jnp.where(in_before, FINE - before + rank, jnp.where(in_here, start + rank - before, rank - before - here))
                step_by = jnp.where(in_before, place - 1, jnp.where(in_here, place, place + 1))
                source = jnp.where((step_by == 3) | (step_by == -3), 5, step_by + 2)
                tidx[2 * base + o] = jnp.bitwise_and(at, LANES - 1)
                tsrc[base + o] = jnp.where(in_after, source, 6)
        rank_own = n[2] + lane - a[3]
        rank_far = jnp.where(lane < 64, n[2] + stay[3] + lane, lane - FINE + n[2])
        for k, rank in enumerate((rank_own, rank_far)):
            rank = jnp.bitwise_and(rank, 255)
            tidx[4 + 2 * k] = COARSE + jnp.right_shift(rank, 3)
            tidx[5 + 2 * k] = jnp.bitwise_and(rank, 7)

    def coarse_setup_c():
        arrived(coarse_handles)
        for c in range(4):
            block = idrow[:, c * LANES:(c + 1) * LANES].T.reshape(2, 8, 8, LANES)
            cidg[2 * c:2 * c + 2] = jnp.where((group < 3)[None, None], cidg[2 * c:2 * c + 2], block)
            cidg2[2 * c:2 * c + 2] = idrow2[:, c * LANES:(c + 1) * LANES].T.reshape(2, 8, 8, LANES)

    def setup_first():
        arrived(inverse_handles)
        coarse_setup_a()
        coarse_setup_b()

    two_sweeps(xb.at[2], x1_handles, ghost, xb.at[3], ghost3, xb.at[4], xb.at[10], 6, setup_first)
    x3 = xb.at[4]
    psi[...] = jnp.zeros((2, 64, LANES), jnp.float32)
    for side in range(2):
        edge = 0 if side else 3
        for k in range(3):
            f = 2 * k + side
            pairs = (face(x3, f) * wface[f]).reshape(4, 2, 8, LANES)
            pairs = pairs[:, 0] + pairs[:, 1]
            pairs = 0.5 * (pairs + pltpu.roll(pairs, 7, 1))
            halved[f] = pairs.reshape(32, LANES)
            part = pick(halved[f, pl.ds(0, 16, stride=2)], nidx[side, k])
            mask = jnp.broadcast_to(nmask[side, k][None], (2, 8, LANES)).reshape(16, LANES)
            part = jnp.where(mask != 0, part, 0.0)
            if k == 0:
                psi[side, 16 * edge:16 * edge + 16] = part
            elif k == 1:
                for i in range(4):
                    at = 16 * i + 4 * edge
                    psi[side, at:at + 4] = psi[side, at:at + 4] + part[4 * i:4 * i + 4]
            else:
                psi[side, pl.ds(edge, 16, stride=4)] = psi[side, pl.ds(edge, 16, stride=4)] + part
    low_lane = jnp.broadcast_to((lane < 64)[None], (4, 8, LANES)).reshape(32, LANES)

    def pack(values, keep_low):
        turned = pltpu.roll(values[32:], 64, 1)
        return jnp.where(low_lane, values[:32], turned) if keep_low else jnp.where(low_lane, turned, values[:32])

    def pack_edges(values, keep_low):
        turned = pltpu.roll(values[8:], 64, 1)
        return jnp.where(lane < 64, values[:8], turned) if keep_low else jnp.where(lane < 64, turned, values[:8])

    def edge_places(upper):
        return (slice(60, 64), pl.ds(51, 4, stride=4), pl.ds(15, 4, stride=16)) if upper else (
            slice(0, 4), pl.ds(0, 4, stride=4), pl.ds(0, 4, stride=16))

    def edge_rows(ref, upper):
        parts = [ref[place] for place in edge_places(upper)]
        return jnp.concatenate(parts + parts[:1], axis=0)

    for at, (side, distance) in enumerate(((0, 1), (1, -1), (1, 3), (0, -3))):
        pair2[2 + at] = pack(psi[side], distance < 0)
    for ahead in (1, 0):
        base = 0 if ahead else 3
        back_edges, ahead_edges = edge_rows(psi.at[1 - ahead], ahead), edge_rows(psi.at[ahead], ahead)
        eb[base], eb[base + 2] = back_edges, ahead_edges
        eh[base], eh[base + 2] = pack_edges(back_edges, not ahead), pack_edges(ahead_edges, not ahead)
    r_handles = [send(2, [(psi.at[1], psir.at[2])]), send(-2, [(psi.at[0], psir.at[3])]),
                 send(4, [(eh.at[2], ehr.at[2])]), send(-4, [(eh.at[5], ehr.at[5])]),
                 send(3, [(pair2.at[4], pair2r.at[4]), (eb.at[2], ebr.at[2])]),
                 send(-3, [(pair2.at[5], pair2r.at[5]), (eb.at[5], ebr.at[5])]),
                 send(2, [(eh.at[0], ehr.at[0])]), send(-2, [(eh.at[3], ehr.at[3])])]

    own_ghosts(xb.at[4], ghost, zero_far=True)


    def restrict_step(i, carry):
        total = jnp.zeros((4, 8, LANES), jnp.float32)
        for half in range(2):
            _, scaled = scaled_residual(x3, ghost, wt, bd, 2 * i + half)
            quads = (scaled * dg[2 * i + half]).reshape(4, 2, 8, LANES)
            total = total + quads[:, 0] + quads[:, 1]
        total = total + pltpu.roll(total, 7, 1)
        tall[pl.ds(pl.multiple_of(i * 32, 32), 32)] = 0.5 * total.reshape(32, LANES)
        return carry

    lax.fori_loop(0, 4, restrict_step, 0, unroll=True)
    restricted = tall[pl.ds(0, 64, stride=2)]
    local[...] = restricted
    pair2[0] = pack(restricted, False)
    pair2[1] = pack(restricted, True)
    for ahead in (1, 0):
        base = 0 if ahead else 3
        own_edges = edge_rows(local, ahead)
        eb[base + 1] = own_edges
        eh[base + 1] = pack_edges(own_edges, not ahead)
    r_handles += [send(3, [(eh.at[1], ehr.at[1])]), send(-3, [(eh.at[4], ehr.at[4])]),
                  send(2, [(pair2.at[0], pair2r.at[0]), (eb.at[1], ebr.at[1])]),
                  send(-2, [(pair2.at[1], pair2r.at[1]), (eb.at[4], ebr.at[4])]),
                  send(1, [(local, src.at[1])]), send(-1, [(local, src.at[3])])]
    r_handles += [send(1, [(psi.at[1], psir.at[0]), (pair2.at[2], pair2r.at[2]), (eb.at[0], ebr.at[0])]),
                  send(-1, [(psi.at[0], psir.at[1]), (pair2.at[3], pair2r.at[3]), (eb.at[3], ebr.at[3])])]
    x3_handles = start_faces(4, x3)
    coarse_setup_c()
    arrived(r_handles)
    src[1] = src[1] + psi[0] + jnp.where(valid[-2], psir[2], 0.0)
    src[3] = src[3] + psi[1] + jnp.where(valid[2], psir[3], 0.0)
    src[2] = local[...] + jnp.where(valid[-1], psir[0], 0.0) + jnp.where(valid[1], psir[1], 0.0)
    high = pair2r[0] + pair2r[2] + jnp.where(valid[-3], pair2r[4], 0.0)
    low = pair2r[1] + pair2r[3] + jnp.where(valid[3], pair2r[5], 0.0)
    src[0] = jnp.concatenate([high, pltpu.roll(high, 64, 1)], axis=0)
    src[4] = jnp.concatenate([low, pltpu.roll(low, 64, 1)], axis=0)
    for ahead in (1, 0):
        base, sign = (0, -1) if ahead else (3, 1)
        edge_two = ebr[base] + ebr[base + 1] + jnp.where(valid[3 * sign], ebr[base + 2], 0.0)
        edge_three = ehr[base] + ehr[base + 1] + jnp.where(valid[4 * sign], ehr[base + 2], 0.0)
        edge_three = jnp.concatenate([edge_three, pltpu.roll(edge_three, 64, 1)], axis=0)
        for at, place in enumerate(edge_places(ahead)):
            src[0 if ahead else 4, place] = edge_two[4 * at:4 * at + 4]
            src[5, place] = edge_three[4 * at:4 * at + 4]

    def doubled(k, q):
        four = src[k, q:q + 4]
        return jnp.concatenate([four, four], axis=0)

    for i in range(4):
        for j in range(4):
            q = 4 * (4 * i + j)
            sources = [doubled(k, q) for k in range(6)]
            for o in range(4):
                x, y = 4 * (o // 2) + i, 4 * (o % 2) + j
                value = jnp.zeros((8, LANES), jnp.float32)
                for k in range(6):
                    value = jnp.where(tsrc[o] == k, pick(sources[k], tidx[o]), value)
                scaled = value * cidg[x, y]
                cbd[x, y] = scaled
                update = scaled * (1.0 / THETA)
                cupd[x, y] = update
                cxb[1, x + 1, y + 1] = update
                if x == 0 or y == 0:
                    value = jnp.zeros((8, LANES), jnp.float32)
                    for k in (3, 4, 5):
                        value = jnp.where(tsrc[4 + o] == k, pick(sources[k], tidx[8 + o]), value)
                    cxb[5, x + 1, y + 1] = value * cidg2[x, y] * (1.0 / THETA)

    c1, c2, c3 = cxb.at[1], cxb.at[2], cxb.at[3]
    for f in range(6):
        put_ghost(c1, cghost, f, coarse_ghost(c1, cxb.at[5], f))
    sweep(c1, cghost, cwt, cbd, cupd, c2, 1)
    for f in range(6):
        put_ghost(c2, cghost, f, coarse_ghost(c2, None, f))
    sweep(c2, cghost, cwt, cbd, cupd, c3, 2)

    for k in (1, 0):
        place, octant = tidx[4 + 2 * k], tidx[5 + 2 * k]
        straight = (jnp.bitwise_and(octant, 1) == 0) == (row < 4)
        outer = jnp.right_shift(octant, 1)
        for i in range(4):
            quads = []
            for j in range(4):
                value = pick(c3[i + 1, j + 1], place)
                for o in range(1, 4):
                    value = jnp.where(outer == o, pick(c3[4 * (o // 2) + i + 1, 4 * (o % 2) + j + 1], place), value)
                quads.append(jnp.where(straight, value, pltpu.roll(value, 4, 0)))
            for half in range(2):
                at = 16 * i + 8 * half
                back[k, at:at + 8] = jnp.where(row < 4, quads[2 * half], quads[2 * half + 1])
        if k == 1:
            backp[0] = pack(back[1], True)
            backp[1] = pack(back[1], False)
            b_handles = [send(2, [(backp.at[0], backpr.at[2])]), send(-2, [(backp.at[1], backpr.at[3])]),
                         send(1, [(backp.at[0], backpr.at[0])]), send(-1, [(backp.at[1], backpr.at[1])])]
        else:
            b_handles += [send(1, [(back.at[0], backr.at[0])]), send(-1, [(back.at[0], backr.at[1])])]
    for c in range(4):
        block = c3[2 * c + 1:2 * c + 3, 1:9].reshape(LANES, LANES).T
        cout_ref[:, c * LANES:(c + 1) * LANES] = block[COARSE:2 * COARSE]
    results = [pltpu.make_async_copy(cout_ref, cout_hbm, osem.at[4])]
    results[0].start()
    far_ghosts(recv.at[4], x3, ghost, x3_handles)
    arrived(b_handles)

    def by_owner(at, before, here, after):
        low = jnp.where(lane < known(at, 0), 1, 0)
        high = jnp.where(lane >= FINE - known(at, 1), 1, 0)
        low = jnp.broadcast_to(low[None], (8, 8, LANES)).reshape(64, LANES)
        high = jnp.broadcast_to(high[None], (8, 8, LANES)).reshape(64, LANES)
        return jnp.where(low != 0, before, jnp.where(high != 0, after, here))

    first_half, last_half = [
        jnp.concatenate([backpr[at], pltpu.roll(backpr[at], 64, 1)], axis=0) for at in (0, 2)], [
        jnp.concatenate([backpr[at], pltpu.roll(backpr[at], 64, 1)], axis=0) for at in (1, 3)]
    values = by_owner(3, first_half[0], back[0], last_half[0])
    near[0] = by_owner(2, first_half[1], backr[0], back[1])
    near[1] = by_owner(4, back[1], backr[1], last_half[1])
    expand[pl.ds(0, 64, stride=2)] = values
    expand[pl.ds(1, 64, stride=2)] = values

    def correct_step(i, carry):
        four = expand[pl.ds(pl.multiple_of((i // 2) * 32, 32), 32)].reshape(4, 1, 8, LANES)
        xb[5, i + 1, 1:9] = x3[i + 1, 1:9] + jnp.broadcast_to(four, (4, 2, 8, LANES)).reshape(8, 8, LANES)
        return carry

    lax.fori_loop(0, 8, correct_step, 0, unroll=True)

    for f in range(6):
        k, side = f // 2, f % 2
        edge = 0 if side else 3
        if k == 0:
            part = near[side, 16 * edge:16 * edge + 16]
        elif k == 1:
            part = jnp.concatenate([near[side, 16 * i + 4 * edge:16 * i + 4 * edge + 4] for i in range(4)], axis=0)
        else:
            part = near[side, pl.ds(edge, 16, stride=4)]
        part = pick(part, fidx[f])
        expand2[f, pl.ds(0, 16, stride=2)] = part
        expand2[f, pl.ds(1, 16, stride=2)] = part
        four = expand2[f].reshape(4, 1, 8, LANES)
        far = get_ghost(x3, ghost, f) + jnp.broadcast_to(four, (4, 2, 8, LANES)).reshape(8, 8, LANES)
        own = pick_face(face(xb.at[5], f ^ 1), fidx[f])
        put_ghost(xb.at[5], ghost2, f, jnp.where(fmask[f][None] != 0, far, own))

    sweep(xb.at[5], ghost2, wt, bd, upd, xb.at[6], 0)
    two_sweeps(xb.at[6], start_faces(8, xb.at[6]), ghost, xb.at[7], ghost3, xb.at[8], xb.at[11], 8)
    for c in range(4):
        columns = slice(c * LANES, (c + 1) * LANES)
        out_ref[:, columns] = xb[8, 2 * c + 1:2 * c + 3, 1:9].reshape(LANES, LANES).T
        results.append(pltpu.make_async_copy(out_ref.at[:, columns], out_hbm.at[:, columns], osem.at[c]))
        results[-1].start()

    for offset in valid:
        @pl.when(valid[offset])
        def _():
            for o, made in sent:
                if o == offset:
                    for copy in made:
                        copy.wait_send()
    for result in results:
        result.wait()


def deliver(fine_ref, coarse_ref, fine_out, coarse_out, fine, coarse, in_sem, out_sem):
    parts = [(fine_ref.at[32 * c:32 * c + 32], fine.at[32 * c:32 * c + 32], fine_out.at[32 * c:32 * c + 32]) for c in range(4)]
    parts.append((coarse_ref, coarse, coarse_out))
    fetches = [pltpu.make_async_copy(source, middle, in_sem.at[at]) for at, (source, middle, _) in enumerate(parts)]
    stores = [pltpu.make_async_copy(middle, target, out_sem.at[at]) for at, (_, middle, target) in enumerate(parts)]
    for fetch in fetches:
        fetch.start()
    for fetch, store in zip(fetches, stores):
        fetch.wait()
        store.start()
    for store in stores:
        store.wait()


def solution(mesh):
    gx, gy = mesh.shape["gx"], mesh.shape["gy"]
    f32, i32 = jnp.float32, jnp.int32

    def on_device(rhs, guess, coef, links, owner, ccoef, clinks):
        volume, padded = (8, 8, 8, LANES), (10, 10, 8, LANES)
        results = pl.pallas_call(
            functools.partial(kernel, gx, gy),
            out_shape=(jax.ShapeDtypeStruct((FINE, 512), f32), jax.ShapeDtypeStruct((COARSE, 512), f32)),
            in_specs=[pl.BlockSpec(memory_space=pltpu.HBM)] * 7,
            out_specs=(pl.BlockSpec(memory_space=pltpu.HBM),) * 2,
            scratch_shapes=[
                pltpu.VMEM((FINE, 512), f32),
                pltpu.VMEM((COARSE, 512), f32),
                pltpu.VMEM((FINE, 512), f32),
                pltpu.VMEM((FINE, 512), f32),
                pltpu.VMEM((FINE, 512), f32),
                pltpu.VMEM((6, FINE), i32),
                pltpu.VMEM((1, FINE), i32),
                pltpu.VMEM((6, COARSE), i32),
                pltpu.VMEM((12,) + padded, f32),
                pltpu.VMEM((6,) + volume, f32),
                pltpu.VMEM(volume, f32),
                pltpu.VMEM(volume, f32),
                pltpu.VMEM(volume, f32),
                pltpu.VMEM((2, 8, 8, LANES), f32),
                pltpu.VMEM((10, 2, 8, 8, LANES), f32),
                pltpu.VMEM((10, 2, 3, 8, 8, LANES), f32),
                pltpu.VMEM((6, 8, LANES), i32),
                pltpu.VMEM((12, 8, LANES), i32),
                pltpu.VMEM((LANES, 512), f32),
                pltpu.VMEM((6,) + padded, f32),
                pltpu.VMEM((6,) + volume, f32),
                pltpu.VMEM(volume, f32),
                pltpu.VMEM(volume, f32),
                pltpu.VMEM(volume, f32),
                pltpu.VMEM((2, 8, 8, LANES), f32),
                pltpu.VMEM((LANES, 512), f32),
                pltpu.VMEM((12, 8, LANES), i32),
                pltpu.VMEM((8, 8, LANES), i32),
                pltpu.VMEM((6, 8, LANES), i32),
                pltpu.VMEM((2, 6, COARSE), i32),
                pltpu.VMEM((LANES, 512), f32),
                pltpu.VMEM((LANES, 512), f32),
                pltpu.VMEM(volume, f32),
                pltpu.VMEM((7, 2, 8, LANES), i32),
                pltpu.VMEM((6, 64, LANES), f32),
                pltpu.VMEM((6, 32, LANES), f32),
                pltpu.VMEM((6, 32, LANES), f32),
                pltpu.VMEM((LANES, LANES), f32),
                pltpu.VMEM((2, 64, LANES), f32),
                pltpu.VMEM((2, 64, LANES), f32),
                pltpu.VMEM((2, 32, LANES), f32),
                pltpu.VMEM((4, 32, LANES), f32),
                pltpu.VMEM((LANES, LANES), f32),
                pltpu.VMEM((2, 64, LANES), f32),
                pltpu.VMEM((6, 32, LANES), f32),
                pltpu.VMEM((2, 8, 8, LANES), f32),
                pltpu.VMEM((2, 6, FINE), i32),
                pltpu.VMEM((2, 3, 8, LANES), i32),
                pltpu.VMEM((2, 3, 8, LANES), i32),
                pltpu.VMEM((6, 8, 8, LANES), f32),
                pltpu.VMEM((2, 3, 8, 8, LANES), f32),
                pltpu.VMEM((2, 2, 6, 8, LANES), f32),
                pltpu.VMEM((2, 2, 6, 8, LANES), f32),
                pltpu.VMEM((2, 3, 8, 8, LANES), f32),
                pltpu.VMEM((2, 8, 8, LANES), f32),
                pltpu.VMEM((64, LANES), f32),
                pltpu.VMEM((2, 64, LANES), f32),
                pltpu.VMEM((4, 64, LANES), f32),
                pltpu.VMEM((6, 32, LANES), f32),
                pltpu.VMEM((6, 16, LANES), f32),
                pltpu.VMEM((6, 16, LANES), f32),
                pltpu.VMEM((6, 8, LANES), f32),
                pltpu.VMEM((6, 8, LANES), f32),
                pltpu.SemaphoreType.DMA((N_COPIES,)),
                pltpu.SemaphoreType.DMA((N_COPIES,)),
                pltpu.SemaphoreType.DMA((7,)),
                pltpu.SemaphoreType.DMA((5,)),
            ],
            compiler_params=pltpu.CompilerParams(collective_id=0, has_side_effects=True, vmem_limit_bytes=56 * 1024 * 1024),
        )(rhs, guess, coef, links.T, owner.T, ccoef, clinks.T)
        hbm = pl.BlockSpec(memory_space=pltpu.HBM)
        return pl.pallas_call(
            deliver,
            out_shape=(jax.ShapeDtypeStruct((FINE, 512), f32), jax.ShapeDtypeStruct((COARSE, 512), f32)),
            in_specs=[hbm, hbm],
            out_specs=(hbm, hbm),
            scratch_shapes=[pltpu.VMEM((FINE, 512), f32), pltpu.VMEM((COARSE, 512), f32),
                            pltpu.SemaphoreType.DMA((5,)), pltpu.SemaphoreType.DMA((5,))],
        )(*results)

    rows = P(("gx", "gy"), None)
    return jax.shard_map(on_device, mesh=mesh, in_specs=(rows,) * 7, out_specs=(rows, rows), check_vma=False)
```

```python
import functools

import jax
import jax.numpy as jnp
from jax import lax
from jax.experimental import pallas as pl
from jax.experimental.pallas import tpu as pltpu
from jax.sharding import PartitionSpec as P

THETA = 1.25
DELTA = 0.75
SIGMA = THETA / DELTA
RHO0 = 1.0 / SIGMA
RHO1 = 1.0 / (2.0 * SIGMA - RHO0)
RHO2 = 1.0 / (2.0 * SIGMA - RHO1)
SWEEPS = ((0.0, 1.0 / THETA), (RHO1 * RHO0, 2.0 * RHO1 / DELTA), (RHO2 * RHO1, 2.0 * RHO2 / DELTA))

LANES = 128
FINE = 128
COARSE = 32
MESH = pl.DeviceIdType.MESH
N_COPIES = 104


def pick(values, index):
    rows = values.shape[0]
    whole = jnp.broadcast_to(index[None], (rows // 8, 8, LANES)).reshape(rows, LANES)
    return jnp.take_along_axis(values, whole, axis=1, mode="promise_in_bounds")


def pick_face(face, index):
    return pick(face.reshape(64, LANES), index).reshape(8, 8, LANES)


def kernel(
    gx, gy,
    rhs_hbm, guess_hbm, coef_hbm, links_hbm, owner_hbm, ccoef_hbm, clinks_hbm,
    out_hbm, cout_hbm,
    out_ref, cout_ref,
    rhs_ref, guess_ref, coef_ref, links_ref, owner_ref, clinks_ref,
    xb, wt, bd, dg, upd, ghost, packed, recv, fidx, fmask,
    ccrow, cxb, cwt, cidg, cbd, cupd, cghost, idrow, tidx, tsrc, cidx, clb, ccrow2, idrow2, cidg2,
    counts, src, pair2, pair2r, tall, back, backr, backp, backpr, expand, near, expand2, ghost2,
    nlinks, nidx, nmask, wface, flux, edges, erecv, beside, ghost3, local, psi, psir, halved, eb, ebr, eh, ehr,
    ssem, rsem, isem, osem,
):
    devices = gx * gy
    me = lax.axis_index("gx") * gy + lax.axis_index("gy")
    valid = {1: me < devices - 1, -1: me > 0, 2: me < devices - 2, -2: me > 1, 3: me < devices - 3, -3: me > 2,
             4: me < devices - 4, -4: me > 3}

    def device(offset):
        target = lax.rem(me + offset + devices, devices)
        return (target // gy, lax.rem(target, gy))

    barrier = pltpu.get_barrier_semaphore()
    for offset in (1, -1, 2, -2):
        @pl.when(valid[offset])
        def _():
            pl.semaphore_signal(barrier, inc=1, device_id=device(offset), device_id_type=MESH)

    fetches = []
    for at, (source, target) in enumerate((
            (coef_hbm, coef_ref), (guess_hbm, guess_ref), (owner_hbm, owner_ref), (links_hbm, links_ref),
            (ccoef_hbm, ccrow.at[COARSE:2 * COARSE]), (rhs_hbm, rhs_ref), (clinks_hbm, clinks_ref))):
        fetches.append(pltpu.make_async_copy(source, target, isem.at[at]))
        fetches[-1].start()

    used = [0]
    sent = []

    def send(offset, pairs):
        made = []
        for source, target in pairs:
            at = used[0]
            used[0] += 1
            made.append(pltpu.make_async_remote_copy(
                src_ref=source, dst_ref=target, send_sem=ssem.at[at], recv_sem=rsem.at[at],
                device_id=device(offset), device_id_type=MESH))

        @pl.when(valid[offset])
        def _():
            for copy in made:
                copy.start()

        sent.append((offset, made))
        return (offset, made)

    def arrived(handles):
        for offset in valid:
            made = [copy for to, copies in handles if to == offset for copy in copies]
            if made:
                @pl.when(valid[-offset])
                def _():
                    for copy in made:
                        copy.wait_recv()

    lane = lax.broadcasted_iota(jnp.int32, (8, LANES), 1)
    row = lax.broadcasted_iota(jnp.int32, (8, LANES), 0)
    row3 = lax.broadcasted_iota(jnp.int32, (8, 8, LANES), 1)
    first, last = row3 == 0, row3 == 7

    def load_cells(buffer, rows_ref):
        for c in range(4):
            block = rows_ref[:, c * LANES:(c + 1) * LANES].T
            buffer[2 * c + 1:2 * c + 3, 1:9] = block.reshape(2, 8, 8, LANES)

    def face(x, f):
        at = 1 if f % 2 == 0 else 8
        if f // 2 == 0:
            return x[at, 1:9]
        if f // 2 == 1:
            return x[1:9, at]
        return x[1:9, 1:9, 0 if f % 2 == 0 else 7]

    def put_ghost(x, g, f, value):
        at = 0 if f % 2 == 0 else 9
        if f // 2 == 0:
            x[at, 1:9] = value
        elif f // 2 == 1:
            x[1:9, at] = value
        else:
            g[f % 2] = value

    def get_ghost(x, g, f):
        at = 0 if f % 2 == 0 else 9
        if f // 2 == 0:
            return x[at, 1:9]
        if f // 2 == 1:
            return x[1:9, at]
        return g[f % 2]

    def neighbours(x, g, i):
        centre = x[i + 1, 1:9]
        low = jnp.where(first, g[0, i][:, None, :], pltpu.roll(centre, 1, 1))
        high = jnp.where(last, g[1, i][:, None, :], pltpu.roll(centre, 7, 1))
        return centre, (x[i, 1:9], x[i + 2, 1:9], x[i + 1, 0:8], x[i + 1, 2:10], low, high)

    def scaled_residual(x, g, w, b, i):
        centre, others = neighbours(x, g, i)
        total = b[i] - centre
        for f in range(6):
            total = total + w[f, i] * others[f]
        return centre, total

    def sweep(x, g, w, b, d, new, at, final=True):
        keep, gain = SWEEPS[at]

        def step(i, carry):
            centre, total = scaled_residual(x, g, w, b, i)
            update = gain * total
            if at > 0:
                update = update + keep * d[i]
            if final:
                d[i] = update
            new[i + 1, 1:9] = centre + update
            return carry

        lax.fori_loop(0, 8, step, 0, unroll=True)

    def start_faces(e, x):
        packed[e, 0] = face(x, 4)
        packed[e, 1] = face(x, 5)
        up = send(1, [(x.at[8, 1:9], recv.at[e, 0, 0]), (x.at[1:9, 8], recv.at[e, 0, 1]), (packed.at[e, 1], recv.at[e, 0, 2])])
        down = send(-1, [(x.at[1, 1:9], recv.at[e, 1, 0]), (x.at[1:9, 1], recv.at[e, 1, 1]), (packed.at[e, 0], recv.at[e, 1, 2])])
        return up, down

    def own_ghosts(x, g, keep_own=False, zero_far=False):
        for f in range(6):
            value = pick_face(face(x, f ^ 1), fidx[f])
            if keep_own:
                value = jnp.where(fmask[6 + f][None] != 0, value, face(x, f))
            if zero_far:
                value = jnp.where(fmask[f][None] != 0, 0.0, value)
            put_ghost(x, g, f, value)

    def far_ghosts(faces, x, g, handles=()):
        arrived(handles)
        for k in range(3):
            for side in range(2):
                f = 2 * k + side
                value = pick_face(faces[side, k], fidx[f])
                put_ghost(x, g, f, jnp.where(fmask[f][None] != 0, value, get_ghost(x, g, f)))

    def across(k, m):
        return (m if m < k else m - 1)

    def line(k, m, at):
        return (at,) if across(k, m) == 0 else (slice(None), at)

    def two_sweeps(x, handles, g, middle, g_middle, new, partial, e, between=None):
        keep, gain = SWEEPS[1]
        for side in range(2):
            for k in range(3):
                f = 2 * k + side
                value = pick_face(face(x, f) * wface[f], nidx[side, k])
                flux[side, k] = jnp.where(nmask[side, k][None] != 0, value, 0.0)
        at = 0
        for m in range(3):
            for k in range(3):
                if k != m:
                    for side in range(2):
                        edges[e // 7, side, at] = flux[(side, m) + line(m, k, 7 if side else 0)]
                    at += 1
        edge_handles = [send(2, [(edges.at[e // 7, 1], erecv.at[e // 7, 0])]), send(-2, [(edges.at[e // 7, 0], erecv.at[e // 7, 1])])]
        own_ghosts(x, g, zero_far=True)
        sweep(x, g, wt, bd, upd, partial, 1, final=False)
        partial_handles = start_faces(e + 1, partial)
        for side in range(2):
            end = 0 if side else 7
            for k in range(3):
                beside[side, k] = flux[side, k]
                for m in range(3):
                    if m != k:
                        where = (side, k) + line(k, m, end)
                        beside[where] = beside[where] + flux[(side, m) + line(m, k, end)]
        if between is not None:
            between()
        far_ghosts(recv.at[e], x, g, handles)
        sweep(x, g, wt, bd, upd, middle, 1)
        own_ghosts(middle, g_middle)
        arrived(edge_handles + list(partial_handles))
        for side in range(2):
            end = 0 if side else 7
            at = 0
            for m in range(3):
                for k in range(3):
                    if k != m:
                        where = (side, k) + line(k, m, 7 - end)
                        behind = jnp.where(valid[2 if side else -2], erecv[e // 7, side, at], 0.0)
                        beside[where] = beside[where] + behind
                        at += 1
        for side in range(2):
            for k in range(3):
                beside[side, k] = recv[e + 1, side, k] + gain * recv[3, side, k] * beside[side, k]
        far_ghosts(beside, middle, g_middle)
        sweep(middle, g_middle, wt, bd, upd, new, 2)

    coef, x0 = xb.at[0], xb.at[1]
    fetches[0].wait()
    load_cells(coef, coef_ref)
    fetches[1].wait()
    load_cells(x0, guess_ref)
    for fetch in fetches[2:]:
        fetch.wait()

    owner = owner_ref[...]
    to_prev = jnp.sum((owner == me - 1).astype(jnp.float32), axis=1, keepdims=True).astype(jnp.int32)
    to_next = jnp.sum((owner == me + 1).astype(jnp.float32), axis=1, keepdims=True).astype(jnp.int32)
    counts[3, 0] = jnp.broadcast_to(to_prev, (8, LANES))
    counts[3, 1] = jnp.broadcast_to(to_next, (8, LANES))

    pl.semaphore_wait(barrier, jnp.minimum(me, 2) + jnp.minimum(devices - 1 - me, 2))

    coef_handles = start_faces(0, coef)
    x0_handles = start_faces(1, x0)
    count_handles = [send(o, [(counts.at[3], counts.at[3 - o])]) for o in (1, -1)]
    link_handles = [send(1, [(links_ref, nlinks.at[0]), (clinks_ref, clb.at[0])]),
                    send(-1, [(links_ref, nlinks.at[1]), (clinks_ref, clb.at[1])])]
    ccoef_handles = [send(1, [(ccrow.at[COARSE:2 * COARSE], ccrow.at[0:COARSE])]),
                     send(-1, [(ccrow.at[COARSE:2 * COARSE], ccrow.at[2 * COARSE:3 * COARSE])])]

    ccoef_handles += [send(2, [(ccrow.at[COARSE:2 * COARSE], ccrow.at[3 * COARSE:])]),
                      send(-2, [(ccrow.at[COARSE:2 * COARSE], ccrow2.at[3 * COARSE:])])]

    links = links_ref[...]
    for f in range(6):
        ids = jnp.broadcast_to(links[f:f + 1], (8, LANES))
        live = ids >= 0
        fidx[f] = jnp.bitwise_and(ids, FINE - 1)
        fmask[f] = jnp.where(live & (jnp.right_shift(ids, 7) != me), 1, 0)
        fmask[6 + f] = jnp.where(live, 1, 0)

    for c in range(4):
        dg[2 * c:2 * c + 2] = rhs_ref[:, c * LANES:(c + 1) * LANES].T.reshape(2, 8, 8, LANES)
    own_ghosts(x0, ghost3)
    own_ghosts(coef, ghost, keep_own=True)
    far_ghosts(recv.at[0], coef, ghost, coef_handles)

    def weigh(x, g, w, lives, finish):
        mask4 = jnp.where((row == 0) & (lives[4] == 0), 0.0, 1.0)[None]
        mask5 = jnp.where((row == 7) & (lives[5] == 0), 0.0, 1.0)[None]

        def step(i, carry):
            centre, others = neighbours(x, g, i)
            weights = [0.5 * (centre + other) for other in others]
            diag = weights[0]
            for weight in weights[1:]:
                diag = diag + weight
            inverse = 1.0 / diag
            for f in range(6):
                value = weights[f] * inverse
                if f == 4:
                    value = value * mask4
                if f == 5:
                    value = value * mask5
                w[f, i] = value
            finish(i, diag, inverse)
            return carry

        lax.fori_loop(0, 8, step, 0, unroll=True)
        w[0, 0] = jnp.where(lives[0][None] != 0, w[0, 0], 0.0)
        w[1, 7] = jnp.where(lives[1][None] != 0, w[1, 7], 0.0)
        w[2, :, 0] = jnp.where(lives[2][None] != 0, w[2, :, 0], 0.0)
        w[3, :, 7] = jnp.where(lives[3][None] != 0, w[3, :, 7], 0.0)

    def fine_finish(i, diag, inverse):
        bd[i] = dg[i] * inverse
        dg[i] = diag
        xb[9, i + 1, 1:9] = inverse

    weigh(coef, ghost, wt, [fmask[6 + f] for f in range(6)], fine_finish)

    inverse_handles = start_faces(3, xb.at[9])
    arrived(count_handles)
    count_handles = [send(2, [(counts.at[2:4], counts.at[0:2])]), send(-2, [(counts.at[3:5], counts.at[5:7])])]
    far_ghosts(recv.at[1], x0, ghost3, x0_handles)
    sweep(x0, ghost3, wt, bd, upd, xb.at[2], 0)
    x1_handles = start_faces(6, xb.at[2])
    arrived(link_handles)
    for side in range(2):
        for k in range(3):
            f = 2 * k + side
            cut = (0 if side == 0 else 7,)
            cut = (slice(None),) * k + cut
            wface[f] = wt[(f,) + cut] * dg[cut]
            ids = jnp.broadcast_to(nlinks[side, 2 * k + 1 - side:2 * k + 2 - side], (8, LANES))
            nidx[side, k] = jnp.bitwise_and(ids, FINE - 1)
            linked = (ids >= 0) & (jnp.right_shift(ids, 7) == me) & valid[1 if side else -1]
            nmask[side, k] = jnp.where(linked, 1, 0)

    group = jnp.right_shift(lane, 5)
    slot = jnp.bitwise_and(lane, COARSE - 1)
    coarse_handles = []

    def coarse_ghost(x, x_after, f):
        value = face(x, f ^ 1)
        if f % 2 == 1 and x_after is not None:
            value = jnp.where((group < 3)[None], value, face(x_after, f ^ 1))
        return pick_face(value, cidx[f])

    def coarse_setup_a():
        arrived(ccoef_handles + count_handles)
        load_cells(cxb.at[0], ccrow)
        load_cells(cxb.at[4], ccrow2)
        links_c = jnp.concatenate([jnp.where(valid[-1], clb[0], -1), clinks_ref[...], jnp.where(valid[1], clb[1], -1),
                                   jnp.full((6, COARSE), -1, jnp.int32)], axis=1)
        lives = []
        x = cxb.at[0]
        for f in range(6):
            ids = jnp.broadcast_to(links_c[f:f + 1], (8, LANES))
            live = ids >= 0
            step_by = jnp.right_shift(ids, 5) - me
            place = jnp.bitwise_and((step_by + 1) * COARSE + jnp.bitwise_and(ids, COARSE - 1), LANES - 1)
            cidx[f] = jnp.where(live, place, lane)
            lives.append(jnp.where(live, 1, 0))
            put_ghost(x, cghost, f, jnp.where(live[None], coarse_ghost(x, cxb.at[4], f), face(x, f)))

        def finish(i, diag, inverse):
            cidg[i] = inverse

        weigh(x, cghost, cwt, lives, finish)
        for c in range(4):
            block = cidg[2 * c:2 * c + 2].reshape(LANES, LANES).T
            idrow[COARSE:2 * COARSE, c * LANES:(c + 1) * LANES] = block[COARSE:2 * COARSE]
        coarse_handles.append(send(2, [(idrow.at[COARSE:2 * COARSE], idrow.at[3 * COARSE:])]))
        coarse_handles.append(send(-2, [(idrow.at[COARSE:2 * COARSE], idrow2.at[3 * COARSE:])]))

    def known(k, which):
        return counts[k, which] if k == 3 else jnp.where(valid[k - 3], counts[k, which], 0)

    def by_group(values):
        return jnp.where(group == 0, values[0], jnp.where(group == 1, values[1], jnp.where(group == 2, values[2], values[3])))

    def coarse_setup_b():
        a = [known(k, 0) for k in range(7)]
        n = [known(k, 1) for k in range(7)]
        stay = [FINE - a[k] - n[k] if k == 3 else jnp.where(valid[k - 3], FINE - a[k] - n[k], 0) for k in range(7)]
        for base, last in ((0, 1), (4, 5)):
            before, here = by_group(n[1:4] + [n[last - 1]]), by_group(stay[2:5] + [stay[last]])
            start, after = by_group(a[2:5] + [a[last]]), by_group(a[3:6] + [a[last + 1]])
            place = jnp.where(group < 3, group - 1, last - 3)
            for o in range(4):
                rank = 8 * slot + 2 * o + jnp.where(row >= 4, 1, 0)
                in_before = rank < before
                in_here = rank < before + here
                in_after = rank < before + here + after
                at = jnp.where(in_before, FINE - before + rank, jnp.where(in_here, start + rank - before, rank - before - here))
                step_by = jnp.where(in_before, place - 1, jnp.where(in_here, place, place + 1))
                source = jnp.where((step_by == 3) | (step_by == -3), 5, step_by + 2)
                tidx[2 * base + o] = jnp.bitwise_and(at, LANES - 1)
                tsrc[base + o] = jnp.where(in_after, source, 6)
        rank_own = n[2] + lane - a[3]
        rank_far = jnp.where(lane < 64, n[2] + stay[3] + lane, lane - FINE + n[2])
        for k, rank in enumerate((rank_own, rank_far)):
            rank = jnp.bitwise_and(rank, 255)
            tidx[4 + 2 * k] = COARSE + jnp.right_shift(rank, 3)
            tidx[5 + 2 * k] = jnp.bitwise_and(rank, 7)

    def coarse_setup_c():
        arrived(coarse_handles)
        for c in range(4):
            block = idrow[:, c * LANES:(c + 1) * LANES].T.reshape(2, 8, 8, LANES)
            cidg[2 * c:2 * c + 2] = jnp.where((group < 3)[None, None], cidg[2 * c:2 * c + 2], block)
            cidg2[2 * c:2 * c + 2] = idrow2[:, c * LANES:(c + 1) * LANES].T.reshape(2, 8, 8, LANES)

    def setup_first():
        arrived(inverse_handles)
        coarse_setup_a()
        coarse_setup_b()

    two_sweeps(xb.at[2], x1_handles, ghost, xb.at[3], ghost3, xb.at[4], xb.at[10], 6, setup_first)
    x3 = xb.at[4]
    psi[:, 0:64] = jnp.zeros((2, 64, LANES), jnp.float32)
    for side in range(2):
        edge = 0 if side else 3
        for k in range(3):
            f = 2 * k + side
            pairs = (face(x3, f) * wface[f]).reshape(4, 2, 8, LANES)
            pairs = pairs[:, 0] + pairs[:, 1]
            pairs = 0.5 * (pairs + pltpu.roll(pairs, 7, 1))
            halved[f] = pairs.reshape(32, LANES)
            part = pick(halved[f, pl.ds(0, 16, stride=2)], nidx[side, k])
            mask = jnp.broadcast_to(nmask[side, k][None], (2, 8, LANES)).reshape(16, LANES)
            part = jnp.where(mask != 0, part, 0.0)
            if k == 0:
                psi[side, 16 * edge:16 * edge + 16] = part
            elif k == 1:
                for i in range(4):
                    at = 16 * i + 4 * edge
                    psi[side, at:at + 4] = psi[side, at:at + 4] + part[4 * i:4 * i + 4]
            else:
                psi[side, pl.ds(edge, 16, stride=4)] = psi[side, pl.ds(edge, 16, stride=4)] + part
    low_lane = jnp.broadcast_to((lane < 64)[None], (4, 8, LANES)).reshape(32, LANES)

    def pack(values, keep_low):
        turned = pltpu.roll(values[32:], 64, 1)
        return jnp.where(low_lane, values[:32], turned) if keep_low else jnp.where(low_lane, turned, values[:32])

    def pack_edges(values, keep_low):
        turned = pltpu.roll(values[8:], 64, 1)
        return jnp.where(lane < 64, values[:8], turned) if keep_low else jnp.where(lane < 64, turned, values[:8])

    def edge_places(upper):
        return (slice(60, 64), pl.ds(51, 4, stride=4), pl.ds(15, 4, stride=16)) if upper else (
            slice(0, 4), pl.ds(0, 4, stride=4), pl.ds(0, 4, stride=16))

    def edge_rows(ref, upper):
        parts = [ref[place] for place in edge_places(upper)]
        return jnp.concatenate(parts + parts[:1], axis=0)

    for at, (side, distance) in enumerate(((0, 1), (1, -1), (1, 3), (0, -3))):
        pair2[2 + at] = pack(psi[side, 0:64], distance < 0)
    for ahead in (1, 0):
        base = 0 if ahead else 3
        back_edges, ahead_edges = edge_rows(psi.at[1 - ahead], ahead), edge_rows(psi.at[ahead], ahead)
        eb[base], eb[base + 2] = back_edges, ahead_edges
        eh[base], eh[base + 2] = pack_edges(back_edges, not ahead), pack_edges(ahead_edges, not ahead)
    r_handles = [send(2, [(psi.at[1, 0:64], psir.at[2])]), send(-2, [(psi.at[0, 0:64], psir.at[3])]),
                 send(4, [(eh.at[2], ehr.at[2])]), send(-4, [(eh.at[5], ehr.at[5])]),
                 send(3, [(pair2.at[4], pair2r.at[4]), (eb.at[2], ebr.at[2])]),
                 send(-3, [(pair2.at[5], pair2r.at[5]), (eb.at[5], ebr.at[5])]),
                 send(2, [(eh.at[0], ehr.at[0])]), send(-2, [(eh.at[3], ehr.at[3])])]

    own_ghosts(xb.at[4], ghost, zero_far=True)


    def restrict_step(i, carry):
        total = jnp.zeros((4, 8, LANES), jnp.float32)
        for half in range(2):
            _, scaled = scaled_residual(x3, ghost, wt, bd, 2 * i + half)
            quads = (scaled * dg[2 * i + half]).reshape(4, 2, 8, LANES)
            total = total + quads[:, 0] + quads[:, 1]
        total = total + pltpu.roll(total, 7, 1)
        tall[pl.ds(pl.multiple_of(i * 32, 32), 32)] = 0.5 * total.reshape(32, LANES)
        return carry

    lax.fori_loop(0, 4, restrict_step, 0, unroll=True)
    restricted = tall[pl.ds(0, 64, stride=2)]
    local[0:64] = restricted
    pair2[0] = pack(restricted, False)
    pair2[1] = pack(restricted, True)
    for ahead in (1, 0):
        base = 0 if ahead else 3
        own_edges = edge_rows(local, ahead)
        eb[base + 1] = own_edges
        eh[base + 1] = pack_edges(own_edges, not ahead)
    r_handles += [send(3, [(eh.at[1], ehr.at[1])]), send(-3, [(eh.at[4], ehr.at[4])]),
                  send(2, [(pair2.at[0], pair2r.at[0]), (eb.at[1], ebr.at[1])]),
                  send(-2, [(pair2.at[1], pair2r.at[1]), (eb.at[4], ebr.at[4])]),
                  send(1, [(local.at[0:64], src.at[1, 0:64])]), send(-1, [(local.at[0:64], src.at[3, 0:64])])]
    r_handles += [send(1, [(psi.at[1, 0:64], psir.at[0]), (pair2.at[2], pair2r.at[2]), (eb.at[0], ebr.at[0])]),
                  send(-1, [(psi.at[0, 0:64], psir.at[1]), (pair2.at[3], pair2r.at[3]), (eb.at[3], ebr.at[3])])]
    x3_handles = start_faces(4, x3)
    coarse_setup_c()
    arrived(r_handles)
    src[1, 0:64] = src[1, 0:64] + psi[0, 0:64] + jnp.where(valid[-2], psir[2], 0.0)
    src[3, 0:64] = src[3, 0:64] + psi[1, 0:64] + jnp.where(valid[2], psir[3], 0.0)
    src[2, 0:64] = local[0:64] + jnp.where(valid[-1], psir[0], 0.0) + jnp.where(valid[1], psir[1], 0.0)
    high = pair2r[0] + pair2r[2] + jnp.where(valid[-3], pair2r[4], 0.0)
    low = pair2r[1] + pair2r[3] + jnp.where(valid[3], pair2r[5], 0.0)
    src[0, 0:64] = jnp.concatenate([high, pltpu.roll(high, 64, 1)], axis=0)
    src[4, 0:64] = jnp.concatenate([low, pltpu.roll(low, 64, 1)], axis=0)
    for ahead in (1, 0):
        base, sign = (0, -1) if ahead else (3, 1)
        edge_two = ebr[base] + ebr[base + 1] + jnp.where(valid[3 * sign], ebr[base + 2], 0.0)
        edge_three = ehr[base] + ehr[base + 1] + jnp.where(valid[4 * sign], ehr[base + 2], 0.0)
        edge_three = jnp.concatenate([edge_three, pltpu.roll(edge_three, 64, 1)], axis=0)
        for at, place in enumerate(edge_places(ahead)):
            src[0 if ahead else 4, place] = edge_two[4 * at:4 * at + 4]
            src[5, place] = edge_three[4 * at:4 * at + 4]

    def doubled(k, q):
        four = src[k, q:q + 4]
        return jnp.concatenate([four, four], axis=0)

    for i in range(4):
        for j in range(4):
            q = 4 * (4 * i + j)
            sources = [doubled(k, q) for k in range(6)]
            for o in range(4):
                x, y = 4 * (o // 2) + i, 4 * (o % 2) + j
                value = jnp.zeros((8, LANES), jnp.float32)
                for k in range(6):
                    value = jnp.where(tsrc[o] == k, pick(sources[k], tidx[o]), value)
                scaled = value * cidg[x, y]
                cbd[x, y] = scaled
                update = scaled * (1.0 / THETA)
                cupd[x, y] = update
                cxb[1, x + 1, y + 1] = update
                if x == 0 or y == 0:
                    value = jnp.zeros((8, LANES), jnp.float32)
                    for k in (3, 4, 5):
                        value = jnp.where(tsrc[4 + o] == k, pick(sources[k], tidx[8 + o]), value)
                    cxb[5, x + 1, y + 1] = value * cidg2[x, y] * (1.0 / THETA)

    c1, c2, c3 = cxb.at[1], cxb.at[2], cxb.at[3]
    for f in range(6):
        put_ghost(c1, cghost, f, coarse_ghost(c1, cxb.at[5], f))
    sweep(c1, cghost, cwt, cbd, cupd, c2, 1)
    for f in range(6):
        put_ghost(c2, cghost, f, coarse_ghost(c2, None, f))
    sweep(c2, cghost, cwt, cbd, cupd, c3, 2)

    for k in (1, 0):
        place, octant = tidx[4 + 2 * k], tidx[5 + 2 * k]
        straight = (jnp.bitwise_and(octant, 1) == 0) == (row < 4)
        outer = jnp.right_shift(octant, 1)
        for i in range(4):
            quads = []
            for j in range(4):
                value = pick(c3[i + 1, j + 1], place)
                for o in range(1, 4):
                    value = jnp.where(outer == o, pick(c3[4 * (o // 2) + i + 1, 4 * (o % 2) + j + 1], place), value)
                quads.append(jnp.where(straight, value, pltpu.roll(value, 4, 0)))
            for half in range(2):
                at = 16 * i + 8 * half
                back[k, at:at + 8] = jnp.where(row < 4, quads[2 * half], quads[2 * half + 1])
        if k == 1:
            backp[0] = pack(back[1], True)
            backp[1] = pack(back[1], False)
            b_handles = [send(2, [(backp.at[0], backpr.at[2])]), send(-2, [(backp.at[1], backpr.at[3])]),
                         send(1, [(backp.at[0], backpr.at[0])]), send(-1, [(backp.at[1], backpr.at[1])])]
        else:
            b_handles += [send(1, [(back.at[0], backr.at[0])]), send(-1, [(back.at[0], backr.at[1])])]
    for c in range(4):
        block = c3[2 * c + 1:2 * c + 3, 1:9].reshape(LANES, LANES).T
        cout_ref[:, c * LANES:(c + 1) * LANES] = block[COARSE:2 * COARSE]
    results = [pltpu.make_async_copy(cout_ref, cout_hbm, osem.at[4])]
    results[0].start()
    far_ghosts(recv.at[4], x3, ghost, x3_handles)
    arrived(b_handles)

    def by_owner(at, before, here, after):
        low = jnp.where(lane < known(at, 0), 1, 0)
        high = jnp.where(lane >= FINE - known(at, 1), 1, 0)
        low = jnp.broadcast_to(low[None], (8, 8, LANES)).reshape(64, LANES)
        high = jnp.broadcast_to(high[None], (8, 8, LANES)).reshape(64, LANES)
        return jnp.where(low != 0, before, jnp.where(high != 0, after, here))

    first_half, last_half = [
        jnp.concatenate([backpr[at], pltpu.roll(backpr[at], 64, 1)], axis=0) for at in (0, 2)], [
        jnp.concatenate([backpr[at], pltpu.roll(backpr[at], 64, 1)], axis=0) for at in (1, 3)]
    values = by_owner(3, first_half[0], back[0], last_half[0])
    near[0, 0:64] = by_owner(2, first_half[1], backr[0], back[1])
    near[1, 0:64] = by_owner(4, back[1], backr[1], last_half[1])
    expand[pl.ds(0, 64, stride=2)] = values
    expand[pl.ds(1, 64, stride=2)] = values

    def correct_step(i, carry):
        four = expand[pl.ds(pl.multiple_of((i // 2) * 32, 32), 32)].reshape(4, 1, 8, LANES)
        xb[5, i + 1, 1:9] = x3[i + 1, 1:9] + jnp.broadcast_to(four, (4, 2, 8, LANES)).reshape(8, 8, LANES)
        return carry

    lax.fori_loop(0, 8, correct_step, 0, unroll=True)

    for f in range(6):
        k, side = f // 2, f % 2
        edge = 0 if side else 3
        if k == 0:
            part = near[side, 16 * edge:16 * edge + 16]
        elif k == 1:
            part = jnp.concatenate([near[side, 16 * i + 4 * edge:16 * i + 4 * edge + 4] for i in range(4)], axis=0)
        else:
            part = near[side, pl.ds(edge, 16, stride=4)]
        part = pick(part, fidx[f])
        expand2[f, pl.ds(0, 16, stride=2)] = part
        expand2[f, pl.ds(1, 16, stride=2)] = part
        four = expand2[f].reshape(4, 1, 8, LANES)
        far = get_ghost(x3, ghost, f) + jnp.broadcast_to(four, (4, 2, 8, LANES)).reshape(8, 8, LANES)
        own = pick_face(face(xb.at[5], f ^ 1), fidx[f])
        put_ghost(xb.at[5], ghost2, f, jnp.where(fmask[f][None] != 0, far, own))

    sweep(xb.at[5], ghost2, wt, bd, upd, xb.at[6], 0)
    two_sweeps(xb.at[6], start_faces(8, xb.at[6]), ghost, xb.at[7], ghost3, xb.at[8], xb.at[11], 8)
    for c in range(4):
        columns = slice(c * LANES, (c + 1) * LANES)
        out_ref[:, columns] = xb[8, 2 * c + 1:2 * c + 3, 1:9].reshape(LANES, LANES).T
        results.append(pltpu.make_async_copy(out_ref.at[:, columns], out_hbm.at[:, columns], osem.at[c]))
        results[-1].start()

    for offset in valid:
        @pl.when(valid[offset])
        def _():
            for o, made in sent:
                if o == offset:
                    for copy in made:
                        copy.wait_send()
    for result in results:
        result.wait()


def deliver(fine_ref, coarse_ref, fine_out, coarse_out, fine, coarse, in_sem, out_sem):
    parts = [(fine_ref.at[32 * c:32 * c + 32], fine.at[32 * c:32 * c + 32], fine_out.at[32 * c:32 * c + 32]) for c in range(4)]
    parts.append((coarse_ref, coarse, coarse_out))
    fetches = [pltpu.make_async_copy(source, middle, in_sem.at[at]) for at, (source, middle, _) in enumerate(parts)]
    stores = [pltpu.make_async_copy(middle, target, out_sem.at[at]) for at, (_, middle, target) in enumerate(parts)]
    for fetch in fetches:
        fetch.start()
    for fetch, store in zip(fetches, stores):
        fetch.wait()
        store.start()
    for store in stores:
        store.wait()


def solution(mesh):
    gx, gy = mesh.shape["gx"], mesh.shape["gy"]
    f32, i32 = jnp.float32, jnp.int32

    def on_device(rhs, guess, coef, links, owner, ccoef, clinks):
        volume, padded = (8, 8, 8, LANES), (10, 10, 8, LANES)
        results = pl.pallas_call(
            functools.partial(kernel, gx, gy),
            out_shape=(jax.ShapeDtypeStruct((FINE, 512), f32), jax.ShapeDtypeStruct((COARSE, 512), f32)),
            in_specs=[pl.BlockSpec(memory_space=pltpu.HBM)] * 7,
            out_specs=(pl.BlockSpec(memory_space=pltpu.HBM),) * 2,
            scratch_shapes=[
                pltpu.VMEM((FINE, 512), f32),
                pltpu.VMEM((COARSE, 512), f32),
                pltpu.VMEM((FINE, 512), f32),
                pltpu.VMEM((FINE, 512), f32),
                pltpu.VMEM((FINE, 512), f32),
                pltpu.VMEM((6, FINE), i32),
                pltpu.VMEM((1, FINE), i32),
                pltpu.VMEM((6, COARSE), i32),
                pltpu.VMEM((12,) + padded, f32),
                pltpu.VMEM((6,) + volume, f32),
                pltpu.VMEM(volume, f32),
                pltpu.VMEM(volume, f32),
                pltpu.VMEM(volume, f32),
                pltpu.VMEM((2, 8, 8, LANES), f32),
                pltpu.VMEM((10, 2, 8, 8, LANES), f32),
                pltpu.VMEM((10, 2, 3, 8, 8, LANES), f32),
                pltpu.VMEM((6, 8, LANES), i32),
                pltpu.VMEM((12, 8, LANES), i32),
                pltpu.VMEM((LANES, 512), f32),
                pltpu.VMEM((6,) + padded, f32),
                pltpu.VMEM((6,) + volume, f32),
                pltpu.VMEM(volume, f32),
                pltpu.VMEM(volume, f32),
                pltpu.VMEM(volume, f32),
                pltpu.VMEM((2, 8, 8, LANES), f32),
                pltpu.VMEM((LANES, 512), f32),
                pltpu.VMEM((12, 8, LANES), i32),
                pltpu.VMEM((8, 8, LANES), i32),
                pltpu.VMEM((6, 8, LANES), i32),
                pltpu.VMEM((2, 6, COARSE), i32),
                pltpu.VMEM((LANES, 512), f32),
                pltpu.VMEM((LANES, 512), f32),
                pltpu.VMEM(volume, f32),
                pltpu.VMEM((7, 2, 8, LANES), i32),
                pltpu.VMEM((6, 128, LANES), f32),
                pltpu.VMEM((6, 32, LANES), f32),
                pltpu.VMEM((6, 32, LANES), f32),
                pltpu.VMEM((LANES, LANES), f32),
                pltpu.VMEM((2, 64, LANES), f32),
                pltpu.VMEM((2, 64, LANES), f32),
                pltpu.VMEM((2, 32, LANES), f32),
                pltpu.VMEM((4, 32, LANES), f32),
                pltpu.VMEM((LANES, LANES), f32),
                pltpu.VMEM((2, 128, LANES), f32),
                pltpu.VMEM((6, 32, LANES), f32),
                pltpu.VMEM((2, 8, 8, LANES), f32),
                pltpu.VMEM((2, 6, FINE), i32),
                pltpu.VMEM((2, 3, 8, LANES), i32),
                pltpu.VMEM((2, 3, 8, LANES), i32),
                pltpu.VMEM((6, 8, 8, LANES), f32),
                pltpu.VMEM((2, 3, 8, 8, LANES), f32),
                pltpu.VMEM((2, 2, 6, 8, LANES), f32),
                pltpu.VMEM((2, 2, 6, 8, LANES), f32),
                pltpu.VMEM((2, 3, 8, 8, LANES), f32),
                pltpu.VMEM((2, 8, 8, LANES), f32),
                pltpu.VMEM((128, LANES), f32),
                pltpu.VMEM((2, 128, LANES), f32),
                pltpu.VMEM((4, 64, LANES), f32),
                pltpu.VMEM((6, 32, LANES), f32),
                pltpu.VMEM((6, 16, LANES), f32),
                pltpu.VMEM((6, 16, LANES), f32),
                pltpu.VMEM((6, 8, LANES), f32),
                pltpu.VMEM((6, 8, LANES), f32),
                pltpu.SemaphoreType.DMA((N_COPIES,)),
                pltpu.SemaphoreType.DMA((N_COPIES,)),
                pltpu.SemaphoreType.DMA((7,)),
                pltpu.SemaphoreType.DMA((5,)),
            ],
            compiler_params=pltpu.CompilerParams(collective_id=0, has_side_effects=True, vmem_limit_bytes=56 * 1024 * 1024),
        )(rhs, guess, coef, links.T, owner.T, ccoef, clinks.T)
        hbm = pl.BlockSpec(memory_space=pltpu.HBM)
        return pl.pallas_call(
            deliver,
            out_shape=(jax.ShapeDtypeStruct((FINE, 512), f32), jax.ShapeDtypeStruct((COARSE, 512), f32)),
            in_specs=[hbm, hbm],
            out_specs=(hbm, hbm),
            scratch_shapes=[pltpu.VMEM((FINE, 512), f32), pltpu.VMEM((COARSE, 512), f32),
                            pltpu.SemaphoreType.DMA((5,)), pltpu.SemaphoreType.DMA((5,))],
        )(*results)

    rows = P(("gx", "gy"), None)
    return jax.shard_map(on_device, mesh=mesh, in_specs=(rows,) * 7, out_specs=(rows, rows), check_vma=False)
```

```python
import functools

import jax
import jax.numpy as jnp
from jax import lax
from jax.experimental import pallas as pl
from jax.experimental.pallas import tpu as pltpu
from jax.sharding import PartitionSpec as P

THETA = 1.25
DELTA = 0.75
SIGMA = THETA / DELTA
RHO0 = 1.0 / SIGMA
RHO1 = 1.0 / (2.0 * SIGMA - RHO0)
RHO2 = 1.0 / (2.0 * SIGMA - RHO1)
SWEEPS = ((0.0, 1.0 / THETA), (RHO1 * RHO0, 2.0 * RHO1 / DELTA), (RHO2 * RHO1, 2.0 * RHO2 / DELTA))

LANES = 128
FINE = 128
COARSE = 32
MESH = pl.DeviceIdType.MESH
N_COPIES = 104


def pick(values, index):
    rows = values.shape[0]
    whole = jnp.broadcast_to(index[None], (rows // 8, 8, LANES)).reshape(rows, LANES)
    return jnp.take_along_axis(values, whole, axis=1, mode="promise_in_bounds")


def pick_face(face, index):
    return pick(face.reshape(64, LANES), index).reshape(8, 8, LANES)


def kernel(
    gx, gy,
    rhs_hbm, guess_hbm, coef_hbm, links_hbm, owner_hbm, ccoef_hbm, clinks_hbm,
    out_hbm, cout_hbm,
    out_ref, cout_ref,
    rhs_ref, guess_ref, coef_ref, links_ref, owner_ref, clinks_ref,
    xb, wt, bd, dg, upd, ghost, packed, recv, fidx, fmask,
    ccrow, cxb, cwt, cidg, cbd, cupd, cghost, idrow, tidx, tsrc, cidx, clb, ccrow2, idrow2, cidg2,
    counts, src, pair2, pair2r, tall, back, backr, backp, backpr, expand, near, expand2, ghost2,
    nlinks, nidx, nmask, wface, flux, edges, erecv, beside, ghost3, local, psi, psir, halved, eb, ebr, eh, ehr,
    ssem, rsem, isem, osem,
):
    devices = gx * gy
    me = lax.axis_index("gx") * gy + lax.axis_index("gy")
    valid = {1: me < devices - 1, -1: me > 0, 2: me < devices - 2, -2: me > 1, 3: me < devices - 3, -3: me > 2,
             4: me < devices - 4, -4: me > 3}

    def device(offset):
        target = lax.rem(me + offset + devices, devices)
        return (target // gy, lax.rem(target, gy))

    barrier = pltpu.get_barrier_semaphore()
    for offset in (1, -1, 2, -2):
        @pl.when(valid[offset])
        def _():
            pl.semaphore_signal(barrier, inc=1, device_id=device(offset), device_id_type=MESH)

    fetches = []
    for at, (source, target) in enumerate((
            (coef_hbm, coef_ref), (guess_hbm, guess_ref), (owner_hbm, owner_ref), (links_hbm, links_ref),
            (ccoef_hbm, ccrow.at[COARSE:2 * COARSE]), (rhs_hbm, rhs_ref), (clinks_hbm, clinks_ref))):
        fetches.append(pltpu.make_async_copy(source, target, isem.at[at]))
        fetches[-1].start()

    used = [0]
    sent = []

    def send(offset, pairs):
        made = []
        for source, target in pairs:
            at = used[0]
            used[0] += 1
            made.append(pltpu.make_async_remote_copy(
                src_ref=source, dst_ref=target, send_sem=ssem.at[at], recv_sem=rsem.at[at],
                device_id=device(offset), device_id_type=MESH))

        @pl.when(valid[offset])
        def _():
            for copy in made:
                copy.start()

        sent.append((offset, made))
        return (offset, made)

    def arrived(handles):
        for offset in valid:
            made = [copy for to, copies in handles if to == offset for copy in copies]
            if made:
                @pl.when(valid[-offset])
                def _():
                    for copy in made:
                        copy.wait_recv()

    lane = lax.broadcasted_iota(jnp.int32, (8, LANES), 1)
    row = lax.broadcasted_iota(jnp.int32, (8, LANES), 0)
    row3 = lax.broadcasted_iota(jnp.int32, (8, 8, LANES), 1)
    first, last = row3 == 0, row3 == 7

    def load_cells(buffer, rows_ref):
        for c in range(4):
            block = rows_ref[:, c * LANES:(c + 1) * LANES].T
            buffer[2 * c + 1:2 * c + 3, 1:9] = block.reshape(2, 8, 8, LANES)

    def face(x, f):
        at = 1 if f % 2 == 0 else 8
        if f // 2 == 0:
            return x[at, 1:9]
        if f // 2 == 1:
            return x[1:9, at]
        return x[1:9, 1:9, 0 if f % 2 == 0 else 7]

    def put_ghost(x, g, f, value):
        at = 0 if f % 2 == 0 else 9
        if f // 2 == 0:
            x[at, 1:9] = value
        elif f // 2 == 1:
            x[1:9, at] = value
        else:
            g[f % 2] = value

    def get_ghost(x, g, f):
        at = 0 if f % 2 == 0 else 9
        if f // 2 == 0:
            return x[at, 1:9]
        if f // 2 == 1:
            return x[1:9, at]
        return g[f % 2]

    def neighbours(x, g, i):
        centre = x[i + 1, 1:9]
        low = jnp.where(first, g[0, i][:, None, :], pltpu.roll(centre, 1, 1))
        high = jnp.where(last, g[1, i][:, None, :], pltpu.roll(centre, 7, 1))
        return centre, (x[i, 1:9], x[i + 2, 1:9], x[i + 1, 0:8], x[i + 1, 2:10], low, high)

    def scaled_residual(x, g, w, b, i):
        centre, others = neighbours(x, g, i)
        total = b[i] - centre
        for f in range(6):
            total = total + w[f, i] * others[f]
        return centre, total

    def sweep(x, g, w, b, d, new, at, final=True):
        keep, gain = SWEEPS[at]

        def step(i, carry):
            centre, total = scaled_residual(x, g, w, b, i)
            update = gain * total
            if at > 0:
                update = update + keep * d[i]
            if final:
                d[i] = update
            new[i + 1, 1:9] = centre + update
            return carry

        lax.fori_loop(0, 8, step, 0, unroll=True)

    def start_faces(e, x):
        packed[e, 0] = face(x, 4)
        packed[e, 1] = face(x, 5)
        up = send(1, [(x.at[8, 1:9], recv.at[e, 0, 0]), (x.at[1:9, 8], recv.at[e, 0, 1]), (packed.at[e, 1], recv.at[e, 0, 2])])
        down = send(-1, [(x.at[1, 1:9], recv.at[e, 1, 0]), (x.at[1:9, 1], recv.at[e, 1, 1]), (packed.at[e, 0], recv.at[e, 1, 2])])
        return up, down

    def own_ghosts(x, g, keep_own=False, zero_far=False):
        for f in range(6):
            value = pick_face(face(x, f ^ 1), fidx[f])
            if keep_own:
                value = jnp.where(fmask[6 + f][None] != 0, value, face(x, f))
            if zero_far:
                value = jnp.where(fmask[f][None] != 0, 0.0, value)
            put_ghost(x, g, f, value)

    def far_ghosts(faces, x, g, handles=()):
        arrived(handles)
        for k in range(3):
            for side in range(2):
                f = 2 * k + side
                value = pick_face(faces[side, k], fidx[f])
                put_ghost(x, g, f, jnp.where(fmask[f][None] != 0, value, get_ghost(x, g, f)))

    def across(k, m):
        return (m if m < k else m - 1)

    def line(k, m, at):
        return (at,) if across(k, m) == 0 else (slice(None), at)

    def two_sweeps(x, handles, g, middle, g_middle, new, partial, e, between=None):
        keep, gain = SWEEPS[1]
        for side in range(2):
            for k in range(3):
                f = 2 * k + side
                value = pick_face(face(x, f) * wface[f], nidx[side, k])
                flux[side, k] = jnp.where(nmask[side, k][None] != 0, value, 0.0)
        at = 0
        for m in range(3):
            for k in range(3):
                if k != m:
                    for side in range(2):
                        edges[e // 7, side, at] = flux[(side, m) + line(m, k, 7 if side else 0)]
                    at += 1
        edge_handles = [send(2, [(edges.at[e // 7, 1], erecv.at[e // 7, 0])]), send(-2, [(edges.at[e // 7, 0], erecv.at[e // 7, 1])])]
        own_ghosts(x, g, zero_far=True)
        sweep(x, g, wt, bd, upd, partial, 1, final=False)
        partial_handles = start_faces(e + 1, partial)
        for side in range(2):
            end = 0 if side else 7
            for k in range(3):
                beside[side, k] = flux[side, k]
                for m in range(3):
                    if m != k:
                        where = (side, k) + line(k, m, end)
                        beside[where] = beside[where] + flux[(side, m) + line(m, k, end)]
        if between is not None:
            between()
        far_ghosts(recv.at[e], x, g, handles)
        sweep(x, g, wt, bd, upd, middle, 1)
        own_ghosts(middle, g_middle)
        arrived(edge_handles + list(partial_handles))
        for side in range(2):
            end = 0 if side else 7
            at = 0
            for m in range(3):
                for k in range(3):
                    if k != m:
                        where = (side, k) + line(k, m, 7 - end)
                        behind = jnp.where(valid[2 if side else -2], erecv[e // 7, side, at], 0.0)
                        beside[where] = beside[where] + behind
                        at += 1
        for side in range(2):
            for k in range(3):
                beside[side, k] = recv[e + 1, side, k] + gain * recv[3, side, k] * beside[side, k]
        far_ghosts(beside, middle, g_middle)
        sweep(middle, g_middle, wt, bd, upd, new, 2)

    coef, x0 = xb.at[0], xb.at[1]
    fetches[0].wait()
    load_cells(coef, coef_ref)
    fetches[1].wait()
    load_cells(x0, guess_ref)
    for fetch in fetches[2:]:
        fetch.wait()

    owner = owner_ref[...]
    to_prev = jnp.sum((owner == me - 1).astype(jnp.float32), axis=1, keepdims=True).astype(jnp.int32)
    to_next = jnp.sum((owner == me + 1).astype(jnp.float32), axis=1, keepdims=True).astype(jnp.int32)
    counts[3, 0] = jnp.broadcast_to(to_prev, (8, LANES))
    counts[3, 1] = jnp.broadcast_to(to_next, (8, LANES))

    pl.semaphore_wait(barrier, jnp.minimum(me, 2) + jnp.minimum(devices - 1 - me, 2))

    coef_handles = start_faces(0, coef)
    x0_handles = start_faces(1, x0)
    count_handles = [send(o, [(counts.at[3], counts.at[3 - o])]) for o in (1, -1)]
    link_handles = [send(1, [(links_ref, nlinks.at[0]), (clinks_ref, clb.at[0])]),
                    send(-1, [(links_ref, nlinks.at[1]), (clinks_ref, clb.at[1])])]
    ccoef_handles = [send(1, [(ccrow.at[COARSE:2 * COARSE], ccrow.at[0:COARSE])]),
                     send(-1, [(ccrow.at[COARSE:2 * COARSE], ccrow.at[2 * COARSE:3 * COARSE])])]

    ccoef_handles += [send(2, [(ccrow.at[COARSE:2 * COARSE], ccrow.at[3 * COARSE:])]),
                      send(-2, [(ccrow.at[COARSE:2 * COARSE], ccrow2.at[3 * COARSE:])])]

    links = links_ref[...]
    for f in range(6):
        ids = jnp.broadcast_to(links[f:f + 1], (8, LANES))
        live = ids >= 0
        fidx[f] = jnp.bitwise_and(ids, FINE - 1)
        fmask[f] = jnp.where(live & (jnp.right_shift(ids, 7) != me), 1, 0)
        fmask[6 + f] = jnp.where(live, 1, 0)

    for c in range(4):
        dg[2 * c:2 * c + 2] = rhs_ref[:, c * LANES:(c + 1) * LANES].T.reshape(2, 8, 8, LANES)
    own_ghosts(x0, ghost3)
    own_ghosts(coef, ghost, keep_own=True)
    far_ghosts(recv.at[0], coef, ghost, coef_handles)

    def weigh(x, g, w, lives, finish):
        mask4 = jnp.where((row == 0) & (lives[4] == 0), 0.0, 1.0)[None]
        mask5 = jnp.where((row == 7) & (lives[5] == 0), 0.0, 1.0)[None]

        def step(i, carry):
            centre, others = neighbours(x, g, i)
            weights = [0.5 * (centre + other) for other in others]
            diag = weights[0]
            for weight in weights[1:]:
                diag = diag + weight
            inverse = 1.0 / diag
            for f in range(6):
                value = weights[f] * inverse
                if f == 4:
                    value = value * mask4
                if f == 5:
                    value = value * mask5
                w[f, i] = value
            finish(i, diag, inverse)
            return carry

        lax.fori_loop(0, 8, step, 0, unroll=True)
        w[0, 0] = jnp.where(lives[0][None] != 0, w[0, 0], 0.0)
        w[1, 7] = jnp.where(lives[1][None] != 0, w[1, 7], 0.0)
        w[2, :, 0] = jnp.where(lives[2][None] != 0, w[2, :, 0], 0.0)
        w[3, :, 7] = jnp.where(lives[3][None] != 0, w[3, :, 7], 0.0)

    def fine_finish(i, diag, inverse):
        bd[i] = dg[i] * inverse
        dg[i] = diag
        xb[9, i + 1, 1:9] = inverse

    weigh(coef, ghost, wt, [fmask[6 + f] for f in range(6)], fine_finish)

    inverse_handles = start_faces(3, xb.at[9])
    arrived(count_handles)
    count_handles = [send(2, [(counts.at[2:4], counts.at[0:2])]), send(-2, [(counts.at[3:5], counts.at[5:7])])]
    far_ghosts(recv.at[1], x0, ghost3, x0_handles)
    sweep(x0, ghost3, wt, bd, upd, xb.at[2], 0)
    x1_handles = start_faces(6, xb.at[2])
    arrived(link_handles)
    for side in range(2):
        for k in range(3):
            f = 2 * k + side
            cut = (0 if side == 0 else 7,)
            cut = (slice(None),) * k + cut
            wface[f] = wt[(f,) + cut] * dg[cut]
            ids = jnp.broadcast_to(nlinks[side, 2 * k + 1 - side:2 * k + 2 - side], (8, LANES))
            nidx[side, k] = jnp.bitwise_and(ids, FINE - 1)
            linked = (ids >= 0) & (jnp.right_shift(ids, 7) == me) & valid[1 if side else -1]
            nmask[side, k] = jnp.where(linked, 1, 0)

    group = jnp.right_shift(lane, 5)
    slot = jnp.bitwise_and(lane, COARSE - 1)
    coarse_handles = []

    def coarse_ghost(x, x_after, f):
        value = face(x, f ^ 1)
        if f % 2 == 1 and x_after is not None:
            value = jnp.where((group < 3)[None], value, face(x_after, f ^ 1))
        return pick_face(value, cidx[f])

    def coarse_setup_a():
        arrived(ccoef_handles + count_handles)
        load_cells(cxb.at[0], ccrow)
        load_cells(cxb.at[4], ccrow2)
        links_c = jnp.concatenate([jnp.where(valid[-1], clb[0], -1), clinks_ref[...], jnp.where(valid[1], clb[1], -1),
                                   jnp.full((6, COARSE), -1, jnp.int32)], axis=1)
        lives = []
        x = cxb.at[0]
        for f in range(6):
            ids = jnp.broadcast_to(links_c[f:f + 1], (8, LANES))
            live = ids >= 0
            step_by = jnp.right_shift(ids, 5) - me
            place = jnp.bitwise_and((step_by + 1) * COARSE + jnp.bitwise_and(ids, COARSE - 1), LANES - 1)
            cidx[f] = jnp.where(live, place, lane)
            lives.append(jnp.where(live, 1, 0))
            put_ghost(x, cghost, f, jnp.where(live[None], coarse_ghost(x, cxb.at[4], f), face(x, f)))

        def finish(i, diag, inverse):
            cidg[i] = inverse

        weigh(x, cghost, cwt, lives, finish)
        for c in range(4):
            block = cidg[2 * c:2 * c + 2].reshape(LANES, LANES).T
            idrow[COARSE:2 * COARSE, c * LANES:(c + 1) * LANES] = block[COARSE:2 * COARSE]
        coarse_handles.append(send(2, [(idrow.at[COARSE:2 * COARSE], idrow.at[3 * COARSE:])]))
        coarse_handles.append(send(-2, [(idrow.at[COARSE:2 * COARSE], idrow2.at[3 * COARSE:])]))

    def known(k, which):
        return counts[k, which] if k == 3 else jnp.where(valid[k - 3], counts[k, which], 0)

    def by_group(values):
        return jnp.where(group == 0, values[0], jnp.where(group == 1, values[1], jnp.where(group == 2, values[2], values[3])))

    def coarse_setup_b():
        a = [known(k, 0) for k in range(7)]
        n = [known(k, 1) for k in range(7)]
        stay = [FINE - a[k] - n[k] if k == 3 else jnp.where(valid[k - 3], FINE - a[k] - n[k], 0) for k in range(7)]
        for base, last in ((0, 1), (4, 5)):
            before, here = by_group(n[1:4] + [n[last - 1]]), by_group(stay[2:5] + [stay[last]])
            start, after = by_group(a[2:5] + [a[last]]), by_group(a[3:6] + [a[last + 1]])
            place = jnp.where(group < 3, group - 1, last - 3)
            for o in range(4):
                rank = 8 * slot + 2 * o + jnp.where(row >= 4, 1, 0)
                in_before = rank < before
                in_here = rank < before + here
                in_after = rank < before + here + after
                at = jnp.where(in_before, FINE - before + rank, jnp.where(in_here, start + rank - before, rank - before - here))
                step_by = jnp.where(in_before, place - 1, jnp.where(in_here, place, place + 1))
                source = jnp.where((step_by == 3) | (step_by == -3), 5, step_by + 2)
                tidx[2 * base + o] = jnp.bitwise_and(at, LANES - 1)
                tsrc[base + o] = jnp.where(in_after, source, 6)
        rank_own = n[2] + lane - a[3]
        rank_far = jnp.where(lane < 64, n[2] + stay[3] + lane, lane - FINE + n[2])
        for k, rank in enumerate((rank_own, rank_far)):
            rank = jnp.bitwise_and(rank, 255)
            tidx[4 + 2 * k] = COARSE + jnp.right_shift(rank, 3)
            tidx[5 + 2 * k] = jnp.bitwise_and(rank, 7)

    def coarse_setup_c():
        arrived(coarse_handles)
        for c in range(4):
            block = idrow[:, c * LANES:(c + 1) * LANES].T.reshape(2, 8, 8, LANES)
            cidg[2 * c:2 * c + 2] = jnp.where((group < 3)[None, None], cidg[2 * c:2 * c + 2], block)
            cidg2[2 * c:2 * c + 2] = idrow2[:, c * LANES:(c + 1) * LANES].T.reshape(2, 8, 8, LANES)

    def setup_first():
        arrived(inverse_handles)
        coarse_setup_a()
        coarse_setup_b()

    two_sweeps(xb.at[2], x1_handles, ghost, xb.at[3], ghost3, xb.at[4], xb.at[10], 6, setup_first)
    x3 = xb.at[4]
    psi[:, 0:64] = jnp.zeros((2, 64, LANES), jnp.float32)
    for side in range(2):
        edge = 0 if side else 3
        for k in range(3):
            f = 2 * k + side
            pairs = (face(x3, f) * wface[f]).reshape(4, 2, 8, LANES)
            pairs = pairs[:, 0] + pairs[:, 1]
            pairs = 0.5 * (pairs + pltpu.roll(pairs, 7, 1))
            halved[f] = pairs.reshape(32, LANES)
            part = pick(halved[f, pl.ds(0, 16, stride=2)], nidx[side, k])
            mask = jnp.broadcast_to(nmask[side, k][None], (2, 8, LANES)).reshape(16, LANES)
            part = jnp.where(mask != 0, part, 0.0)
            if k == 0:
                psi[side, 16 * edge:16 * edge + 16] = part
            elif k == 1:
                for i in range(4):
                    at = 16 * i + 4 * edge
                    psi[side, at:at + 4] = psi[side, at:at + 4] + part[4 * i:4 * i + 4]
            else:
                psi[side, pl.ds(edge, 16, stride=4)] = psi[side, pl.ds(edge, 16, stride=4)] + part
    low_lane = jnp.broadcast_to((lane < 64)[None], (4, 8, LANES)).reshape(32, LANES)

    def pack(values, keep_low):
        turned = pltpu.roll(values[32:], 64, 1)
        return jnp.where(low_lane, values[:32], turned) if keep_low else jnp.where(low_lane, turned, values[:32])

    def pack_edges(values, keep_low):
        turned = pltpu.roll(values[8:], 64, 1)
        return jnp.where(lane < 64, values[:8], turned) if keep_low else jnp.where(lane < 64, turned, values[:8])

    def edge_places(upper):
        return (slice(60, 64), pl.ds(51, 4, stride=4), pl.ds(15, 4, stride=16)) if upper else (
            slice(0, 4), pl.ds(0, 4, stride=4), pl.ds(0, 4, stride=16))

    def edge_rows(ref, upper):
        parts = [ref[place] for place in edge_places(upper)]
        return jnp.concatenate(parts + parts[:1], axis=0)

    for at, (side, distance) in enumerate(((0, 1), (1, -1), (1, 3), (0, -3))):
        pair2[2 + at] = pack(psi[side, 0:64], distance < 0)
    for ahead in (1, 0):
        base = 0 if ahead else 3
        back_edges, ahead_edges = edge_rows(psi.at[1 - ahead], ahead), edge_rows(psi.at[ahead], ahead)
        eb[base], eb[base + 2] = back_edges, ahead_edges
        eh[base], eh[base + 2] = pack_edges(back_edges, not ahead), pack_edges(ahead_edges, not ahead)
    r_handles = [send(2, [(psi.at[1, 0:64], psir.at[2])]), send(-2, [(psi.at[0, 0:64], psir.at[3])]),
                 send(4, [(eh.at[2], ehr.at[2])]), send(-4, [(eh.at[5], ehr.at[5])]),
                 send(3, [(pair2.at[4], pair2r.at[4]), (eb.at[2], ebr.at[2])]),
                 send(-3, [(pair2.at[5], pair2r.at[5]), (eb.at[5], ebr.at[5])]),
                 send(2, [(eh.at[0], ehr.at[0])]), send(-2, [(eh.at[3], ehr.at[3])])]

    own_ghosts(xb.at[4], ghost, zero_far=True)


    def restrict_step(i, carry):
        total = jnp.zeros((4, 8, LANES), jnp.float32)
        for half in range(2):
            _, scaled = scaled_residual(x3, ghost, wt, bd, 2 * i + half)
            quads = (scaled * dg[2 * i + half]).reshape(4, 2, 8, LANES)
            total = total + quads[:, 0] + quads[:, 1]
        total = total + pltpu.roll(total, 7, 1)
        tall[pl.ds(pl.multiple_of(i * 32, 32), 32)] = 0.5 * total.reshape(32, LANES)
        return carry

    lax.fori_loop(0, 4, restrict_step, 0, unroll=True)
    restricted = tall[pl.ds(0, 64, stride=2)]
    local[0:64] = restricted
    pair2[0] = pack(restricted, False)
    pair2[1] = pack(restricted, True)
    for ahead in (1, 0):
        base = 0 if ahead else 3
        own_edges = edge_rows(local, ahead)
        eb[base + 1] = own_edges
        eh[base + 1] = pack_edges(own_edges, not ahead)
    r_handles += [send(3, [(eh.at[1], ehr.at[1])]), send(-3, [(eh.at[4], ehr.at[4])]),
                  send(2, [(pair2.at[0], pair2r.at[0]), (eb.at[1], ebr.at[1])]),
                  send(-2, [(pair2.at[1], pair2r.at[1]), (eb.at[4], ebr.at[4])]),
                  send(1, [(local.at[0:64], src.at[1, 0:64])]), send(-1, [(local.at[0:64], src.at[3, 0:64])])]
    r_handles += [send(1, [(psi.at[1, 0:64], psir.at[0]), (pair2.at[2], pair2r.at[2]), (eb.at[0], ebr.at[0])]),
                  send(-1, [(psi.at[0, 0:64], psir.at[1]), (pair2.at[3], pair2r.at[3]), (eb.at[3], ebr.at[3])])]
    x3_handles = start_faces(4, x3)
    coarse_setup_c()
    arrived(r_handles)
    src[1, 0:64] = src[1, 0:64] + psi[0, 0:64] + jnp.where(valid[-2], psir[2], 0.0)
    src[3, 0:64] = src[3, 0:64] + psi[1, 0:64] + jnp.where(valid[2], psir[3], 0.0)
    src[2, 0:64] = local[0:64] + jnp.where(valid[-1], psir[0], 0.0) + jnp.where(valid[1], psir[1], 0.0)
    high = pair2r[0] + pair2r[2] + jnp.where(valid[-3], pair2r[4], 0.0)
    low = pair2r[1] + pair2r[3] + jnp.where(valid[3], pair2r[5], 0.0)
    src[0, 0:64] = jnp.concatenate([high, pltpu.roll(high, 64, 1)], axis=0)
    src[4, 0:64] = jnp.concatenate([low, pltpu.roll(low, 64, 1)], axis=0)
    for ahead in (1, 0):
        base, sign = (0, -1) if ahead else (3, 1)
        edge_two = ebr[base] + ebr[base + 1] + jnp.where(valid[3 * sign], ebr[base + 2], 0.0)
        edge_three = ehr[base] + ehr[base + 1] + jnp.where(valid[4 * sign], ehr[base + 2], 0.0)
        edge_three = jnp.concatenate([edge_three, pltpu.roll(edge_three, 64, 1)], axis=0)
        for at, place in enumerate(edge_places(ahead)):
            src[0 if ahead else 4, place] = edge_two[4 * at:4 * at + 4]
            src[5, place] = edge_three[4 * at:4 * at + 4]

    def doubled(k, q):
        four = src[k, q:q + 4]
        return jnp.concatenate([four, four], axis=0)

    for i in range(4):
        for j in range(4):
            q = 4 * (4 * i + j)
            sources = [doubled(k, q) for k in range(6)]
            outer = jnp.where(lane < 64, sources[4], sources[5])
            for o in range(4):
                x, y = 4 * (o // 2) + i, 4 * (o % 2) + j
                value = jnp.zeros((8, LANES), jnp.float32)
                for k in range(4):
                    value = jnp.where(tsrc[o] == k, pick(sources[k], tidx[o]), value)
                value = jnp.where((tsrc[o] == 4) | (tsrc[o] == 5), pick(outer, tidx[o]), value)
                scaled = value * cidg[x, y]
                cbd[x, y] = scaled
                update = scaled * (1.0 / THETA)
                cupd[x, y] = update
                cxb[1, x + 1, y + 1] = update
                if x == 0 or y == 0:
                    value = jnp.zeros((8, LANES), jnp.float32)
                    for k in (3, 4, 5):
                        value = jnp.where(tsrc[4 + o] == k, pick(sources[k], tidx[8 + o]), value)
                    cxb[5, x + 1, y + 1] = value * cidg2[x, y] * (1.0 / THETA)

    c1, c2, c3 = cxb.at[1], cxb.at[2], cxb.at[3]
    for f in range(6):
        put_ghost(c1, cghost, f, coarse_ghost(c1, cxb.at[5], f))
    sweep(c1, cghost, cwt, cbd, cupd, c2, 1)
    for f in range(6):
        put_ghost(c2, cghost, f, coarse_ghost(c2, None, f))
    sweep(c2, cghost, cwt, cbd, cupd, c3, 2)

    for k in (1, 0):
        place, octant = tidx[4 + 2 * k], tidx[5 + 2 * k]
        straight = (jnp.bitwise_and(octant, 1) == 0) == (row < 4)
        outer = jnp.right_shift(octant, 1)
        for i in range(4):
            quads = []
            for j in range(4):
                value = pick(c3[i + 1, j + 1], place)
                for o in range(1, 4):
                    value = jnp.where(outer == o, pick(c3[4 * (o // 2) + i + 1, 4 * (o % 2) + j + 1], place), value)
                quads.append(jnp.where(straight, value, pltpu.roll(value, 4, 0)))
            for half in range(2):
                at = 16 * i + 8 * half
                back[k, at:at + 8] = jnp.where(row < 4, quads[2 * half], quads[2 * half + 1])
        if k == 1:
            backp[0] = pack(back[1], True)
            backp[1] = pack(back[1], False)
            b_handles = [send(2, [(backp.at[0], backpr.at[2])]), send(-2, [(backp.at[1], backpr.at[3])]),
                         send(1, [(backp.at[0], backpr.at[0])]), send(-1, [(backp.at[1], backpr.at[1])])]
        else:
            b_handles += [send(1, [(back.at[0], backr.at[0])]), send(-1, [(back.at[0], backr.at[1])])]
    for c in range(4):
        block = c3[2 * c + 1:2 * c + 3, 1:9].reshape(LANES, LANES).T
        cout_ref[:, c * LANES:(c + 1) * LANES] = block[COARSE:2 * COARSE]
    results = [pltpu.make_async_copy(cout_ref, cout_hbm, osem.at[4])]
    results[0].start()
    far_ghosts(recv.at[4], x3, ghost, x3_handles)
    arrived(b_handles)

    def by_owner(at, before, here, after):
        low = jnp.where(lane < known(at, 0), 1, 0)
        high = jnp.where(lane >= FINE - known(at, 1), 1, 0)
        low = jnp.broadcast_to(low[None], (8, 8, LANES)).reshape(64, LANES)
        high = jnp.broadcast_to(high[None], (8, 8, LANES)).reshape(64, LANES)
        return jnp.where(low != 0, before, jnp.where(high != 0, after, here))

    first_half, last_half = [
        jnp.concatenate([backpr[at], pltpu.roll(backpr[at], 64, 1)], axis=0) for at in (0, 2)], [
        jnp.concatenate([backpr[at], pltpu.roll(backpr[at], 64, 1)], axis=0) for at in (1, 3)]
    values = by_owner(3, first_half[0], back[0], last_half[0])
    near[0, 0:64] = by_owner(2, first_half[1], backr[0], back[1])
    near[1, 0:64] = by_owner(4, back[1], backr[1], last_half[1])
    expand[pl.ds(0, 64, stride=2)] = values
    expand[pl.ds(1, 64, stride=2)] = values

    def correct_step(i, carry):
        four = expand[pl.ds(pl.multiple_of((i // 2) * 32, 32), 32)].reshape(4, 1, 8, LANES)
        xb[5, i + 1, 1:9] = x3[i + 1, 1:9] + jnp.broadcast_to(four, (4, 2, 8, LANES)).reshape(8, 8, LANES)
        return carry

    lax.fori_loop(0, 8, correct_step, 0, unroll=True)

    for f in range(6):
        k, side = f // 2, f % 2
        edge = 0 if side else 3
        if k == 0:
            part = near[side, 16 * edge:16 * edge + 16]
        elif k == 1:
            part = jnp.concatenate([near[side, 16 * i + 4 * edge:16 * i + 4 * edge + 4] for i in range(4)], axis=0)
        else:
            part = near[side, pl.ds(edge, 16, stride=4)]
        part = pick(part, fidx[f])
        expand2[f, pl.ds(0, 16, stride=2)] = part
        expand2[f, pl.ds(1, 16, stride=2)] = part
        four = expand2[f].reshape(4, 1, 8, LANES)
        far = get_ghost(x3, ghost, f) + jnp.broadcast_to(four, (4, 2, 8, LANES)).reshape(8, 8, LANES)
        own = pick_face(face(xb.at[5], f ^ 1), fidx[f])
        put_ghost(xb.at[5], ghost2, f, jnp.where(fmask[f][None] != 0, far, own))

    sweep(xb.at[5], ghost2, wt, bd, upd, xb.at[6], 0)
    two_sweeps(xb.at[6], start_faces(8, xb.at[6]), ghost, xb.at[7], ghost3, xb.at[8], xb.at[11], 8)
    for c in range(4):
        columns = slice(c * LANES, (c + 1) * LANES)
        out_ref[:, columns] = xb[8, 2 * c + 1:2 * c + 3, 1:9].reshape(LANES, LANES).T
        results.append(pltpu.make_async_copy(out_ref.at[:, columns], out_hbm.at[:, columns], osem.at[c]))
        results[-1].start()

    for offset in valid:
        @pl.when(valid[offset])
        def _():
            for o, made in sent:
                if o == offset:
                    for copy in made:
                        copy.wait_send()
    for result in results:
        result.wait()


def deliver(fine_ref, coarse_ref, fine_out, coarse_out, fine, coarse, in_sem, out_sem):
    parts = [(fine_ref.at[32 * c:32 * c + 32], fine.at[32 * c:32 * c + 32], fine_out.at[32 * c:32 * c + 32]) for c in range(4)]
    parts.append((coarse_ref, coarse, coarse_out))
    fetches = [pltpu.make_async_copy(source, middle, in_sem.at[at]) for at, (source, middle, _) in enumerate(parts)]
    stores = [pltpu.make_async_copy(middle, target, out_sem.at[at]) for at, (_, middle, target) in enumerate(parts)]
    for fetch in fetches:
        fetch.start()
    for fetch, store in zip(fetches, stores):
        fetch.wait()
        store.start()
    for store in stores:
        store.wait()


def solution(mesh):
    gx, gy = mesh.shape["gx"], mesh.shape["gy"]
    f32, i32 = jnp.float32, jnp.int32

    def on_device(rhs, guess, coef, links, owner, ccoef, clinks):
        volume, padded = (8, 8, 8, LANES), (10, 10, 8, LANES)
        results = pl.pallas_call(
            functools.partial(kernel, gx, gy),
            out_shape=(jax.ShapeDtypeStruct((FINE, 512), f32), jax.ShapeDtypeStruct((COARSE, 512), f32)),
            in_specs=[pl.BlockSpec(memory_space=pltpu.HBM)] * 7,
            out_specs=(pl.BlockSpec(memory_space=pltpu.HBM),) * 2,
            scratch_shapes=[
                pltpu.VMEM((FINE, 512), f32),
                pltpu.VMEM((COARSE, 512), f32),
                pltpu.VMEM((FINE, 512), f32),
                pltpu.VMEM((FINE, 512), f32),
                pltpu.VMEM((FINE, 512), f32),
                pltpu.VMEM((6, FINE), i32),
                pltpu.VMEM((1, FINE), i32),
                pltpu.VMEM((6, COARSE), i32),
                pltpu.VMEM((12,) + padded, f32),
                pltpu.VMEM((6,) + volume, f32),
                pltpu.VMEM(volume, f32),
                pltpu.VMEM(volume, f32),
                pltpu.VMEM(volume, f32),
                pltpu.VMEM((2, 8, 8, LANES), f32),
                pltpu.VMEM((10, 2, 8, 8, LANES), f32),
                pltpu.VMEM((10, 2, 3, 8, 8, LANES), f32),
                pltpu.VMEM((6, 8, LANES), i32),
                pltpu.VMEM((12, 8, LANES), i32),
                pltpu.VMEM((LANES, 512), f32),
                pltpu.VMEM((6,) + padded, f32),
                pltpu.VMEM((6,) + volume, f32),
                pltpu.VMEM(volume, f32),
                pltpu.VMEM(volume, f32),
                pltpu.VMEM(volume, f32),
                pltpu.VMEM((2, 8, 8, LANES), f32),
                pltpu.VMEM((LANES, 512), f32),
                pltpu.VMEM((12, 8, LANES), i32),
                pltpu.VMEM((8, 8, LANES), i32),
                pltpu.VMEM((6, 8, LANES), i32),
                pltpu.VMEM((2, 6, COARSE), i32),
                pltpu.VMEM((LANES, 512), f32),
                pltpu.VMEM((LANES, 512), f32),
                pltpu.VMEM(volume, f32),
                pltpu.VMEM((7, 2, 8, LANES), i32),
                pltpu.VMEM((6, 128, LANES), f32),
                pltpu.VMEM((6, 32, LANES), f32),
                pltpu.VMEM((6, 32, LANES), f32),
                pltpu.VMEM((LANES, LANES), f32),
                pltpu.VMEM((2, 64, LANES), f32),
                pltpu.VMEM((2, 64, LANES), f32),
                pltpu.VMEM((2, 32, LANES), f32),
                pltpu.VMEM((4, 32, LANES), f32),
                pltpu.VMEM((LANES, LANES), f32),
                pltpu.VMEM((2, 128, LANES), f32),
                pltpu.VMEM((6, 32, LANES), f32),
                pltpu.VMEM((2, 8, 8, LANES), f32),
                pltpu.VMEM((2, 6, FINE), i32),
                pltpu.VMEM((2, 3, 8, LANES), i32),
                pltpu.VMEM((2, 3, 8, LANES), i32),
                pltpu.VMEM((6, 8, 8, LANES), f32),
                pltpu.VMEM((2, 3, 8, 8, LANES), f32),
                pltpu.VMEM((2, 2, 6, 8, LANES), f32),
                pltpu.VMEM((2, 2, 6, 8, LANES), f32),
                pltpu.VMEM((2, 3, 8, 8, LANES), f32),
                pltpu.VMEM((2, 8, 8, LANES), f32),
                pltpu.VMEM((128, LANES), f32),
                pltpu.VMEM((2, 128, LANES), f32),
                pltpu.VMEM((4, 64, LANES), f32),
                pltpu.VMEM((6, 32, LANES), f32),
                pltpu.VMEM((6, 16, LANES), f32),
                pltpu.VMEM((6, 16, LANES), f32),
                pltpu.VMEM((6, 8, LANES), f32),
                pltpu.VMEM((6, 8, LANES), f32),
                pltpu.SemaphoreType.DMA((N_COPIES,)),
                pltpu.SemaphoreType.DMA((N_COPIES,)),
                pltpu.SemaphoreType.DMA((7,)),
                pltpu.SemaphoreType.DMA((5,)),
            ],
            compiler_params=pltpu.CompilerParams(collective_id=0, has_side_effects=True, vmem_limit_bytes=56 * 1024 * 1024),
        )(rhs, guess, coef, links.T, owner.T, ccoef, clinks.T)
        hbm = pl.BlockSpec(memory_space=pltpu.HBM)
        return pl.pallas_call(
            deliver,
            out_shape=(jax.ShapeDtypeStruct((FINE, 512), f32), jax.ShapeDtypeStruct((COARSE, 512), f32)),
            in_specs=[hbm, hbm],
            out_specs=(hbm, hbm),
            scratch_shapes=[pltpu.VMEM((FINE, 512), f32), pltpu.VMEM((COARSE, 512), f32),
                            pltpu.SemaphoreType.DMA((5,)), pltpu.SemaphoreType.DMA((5,))],
        )(*results)

    rows = P(("gx", "gy"), None)
    return jax.shard_map(on_device, mesh=mesh, in_specs=(rows,) * 7, out_specs=(rows, rows), check_vma=False)
```
